256 devices in a mesh: gx: 8 (over y, core), gy: 32 (over x, z).
Axes of the slice: x: 4, y: 4, z: 8, core: 2. Of those that a mesh axis runs over, the one named last changes fastest.
Arguments:
- free_velocity: float32 [8, 32, 6, 2048], P('gx', 'gy'), may hold values from -6 to 6
- body_radius: float32 [8, 32, 2048], P('gx', 'gy'), may hold values from 0.8 to 1.25
- face_lists: int32 [8, 32, 4, 256], P('gx', 'gy'), may hold values from 0 to 2047
- corner_lists: int32 [8, 32, 4, 32], P('gx', 'gy'), may hold values from 0 to 2047
- owner_body: int32 [8, 32, 4096], P('gx', 'gy'), may hold values from 0 to 2047
- other_body: int32 [8, 32, 4096], P('gx', 'gy'), may hold values from 0 to 3199
- contact_angles: float32 [8, 32, 2, 4096], P('gx', 'gy'), may hold values from -3.140625 to 3.140625
- contact_arms: float32 [8, 32, 2, 4096], P('gx', 'gy'), may hold values from 0.8 to 1.25
- friction: float32 [8, 32, 4096], P('gx', 'gy'), may hold values from 0.2 to 0.6
- approach: float32 [8, 32, 4096], P('gx', 'gy'), may hold values from -3 to 3
- start_impulse: float32 [8, 32, 3, 4096], P('gx', 'gy'), may hold values from -3 to 3
Outputs:
- velocity: float32 [8, 32, 6, 2048], P('gx', 'gy')
- impulse: float32 [8, 32, 3, 4096], P('gx', 'gy')
The draws below stay inside these ranges and needn't reach their ends.
Inputs may be any that keep to these rules, and one draw needn't show every extreme that they name: `other_body`: columns below 2048 of the extended table are owned spheres; the rest are the copy blocks in the order of the statement. `face_lists`: indices of owned spheres; a sphere may stand in several lists. `corner_lists`: indices of owned spheres. `owner_body`: indices of owned spheres.
All inputs are finite; a program needn't handle non-finite values.
Results may differ from the reference program's by a relative error of at most 0.0003.
Values sent between devices are 32-bit elements; how exact they have to be, the bound alone decides.
No kernel may reach another device: no remote copies, remote signals or barrier semaphores. Data moves between devices by JAX's collectives and lax.ppermute only.
A program may use at most 64 MiB of HBM per device.

```python
import math
import jax
import jax.numpy as jnp
from jax import lax

BODY_DEV = 2048
FACE_LEN = 256
CORNER_LEN = 32
CONTACTS = 4096
EXTENT = 3200
SWEEPS = 4
N_GX = 8
N_GY = 32


def set_ends(entries, own_key, smallest, high):
    longest = entries.shape.index(max(entries.shape))
    spots = []
    for shift in (0, 1):
        where = [jax.random.randint(jax.random.fold_in(own_key, axis), (), 0, length) for axis, length in enumerate(entries.shape)]
        where[longest] = (where[longest] + shift) % entries.shape[longest]
        spots.append(tuple(where))
    return entries.at[spots[0]].set(smallest).at[spots[1]].set(high)


def block_levels(rng, extent, shards, low, largest):
    def one(axis_at, blocks):
        steps = jax.random.uniform(jax.random.fold_in(jax.random.fold_in(rng, 6), axis_at), (blocks,), jnp.float32, low / len(shards), largest / len(shards))
        return jnp.repeat(jnp.exp(steps), extent[axis_at] // blocks).reshape((-1,) + (1,) * (len(extent) - axis_at - 1))

    level = one(*shards[0])
    for cut in shards[1:]:
        level = level * one(*cut)
    return level


def centred(stream_key, dims, width, limit, shards=(), kind=jnp.bfloat16):
    drawn = jax.random.normal(stream_key, dims, jnp.float32) * width
    if len(shards) > 0:
        drawn = block_levels(stream_key, dims, shards, -0.22, 0.18) * drawn
    return jnp.clip(drawn, min=-limit, max=limit).astype(kind)


def setup_inputs(seed: int = 0) -> dict:
    streams_of = jax.random.split(jax.random.key(seed), 12)
    return {
        "free_velocity": centred(streams_of[0], (N_GX, N_GY, 6, BODY_DEV), 1.0, 6.0, ((0, 8), (1, 32)), jnp.float32),
        "body_radius": jnp.clip(jnp.exp(math.log(1.25) - 0.4462871 * jax.random.uniform(streams_of[1], (N_GX, N_GY, BODY_DEV), jnp.float32) ** block_levels(streams_of[1], (N_GX, N_GY, BODY_DEV), ((0, 8), (1, 32)), -0.2, 0.2)), 0.8, 1.25),
        "face_lists": set_ends(jax.random.randint(streams_of[2], (N_GX, N_GY, 4, FACE_LEN), 0, BODY_DEV), jax.random.fold_in(streams_of[2], 1), 0, BODY_DEV - 1).astype(jnp.int32),
        "corner_lists": set_ends(jax.random.randint(streams_of[3], (N_GX, N_GY, 4, CORNER_LEN), 0, BODY_DEV), jax.random.fold_in(streams_of[3], 1), 0, BODY_DEV - 1).astype(jnp.int32),
        "owner_body": set_ends(jax.random.randint(streams_of[4], (N_GX, N_GY, CONTACTS), 0, BODY_DEV), jax.random.fold_in(streams_of[4], 1), 0, BODY_DEV - 1).astype(jnp.int32),
        "other_body": set_ends(jax.random.randint(streams_of[5], (N_GX, N_GY, CONTACTS), 0, EXTENT), jax.random.fold_in(streams_of[5], 1), 0, EXTENT - 1).astype(jnp.int32),
        "contact_angles": jnp.clip(jax.random.uniform(streams_of[6], (N_GX, N_GY, 2, CONTACTS), jnp.float32, -3.140625, 3.140625), -3.140625, 3.140625),
        "contact_arms": jnp.clip(jnp.exp(math.log(1.25) - 0.4462871 * jax.random.uniform(streams_of[7], (N_GX, N_GY, 2, CONTACTS), jnp.float32) ** block_levels(streams_of[7], (N_GX, N_GY, 2, CONTACTS), ((0, 8), (1, 32)), -0.2, 0.2)), 0.8, 1.25),
        "friction": jnp.clip(0.2 + 0.400000021 * jax.random.uniform(streams_of[8], (N_GX, N_GY, CONTACTS), jnp.float32) ** block_levels(streams_of[8], (N_GX, N_GY, CONTACTS), ((0, 8), (1, 32)), -0.2, 0.2), 0.2, 0.6),
        "approach": centred(streams_of[9], (N_GX, N_GY, CONTACTS), 0.5, 3.0, ((0, 8), (1, 32)), jnp.float32),
        "start_impulse": centred(streams_of[10], (N_GX, N_GY, 3, CONTACTS), 0.3, 3.0, ((0, 8), (1, 32)), jnp.float32),
    }


RELAX = 0.25
SMALLEST = 1e-20
FACE_STEPS = ((-1, 0), (1, 0), (0, -1), (0, 1))
CORNER_STEPS = ((-1, -1), (-1, 1), (1, -1), (1, 1))

def frames(angles):
    cos_polar = jnp.cos(angles[0])
    sin_polar = jnp.sin(angles[0])
    cos_azim = jnp.cos(angles[1])
    sin_azim = jnp.sin(angles[1])
    normal = jnp.stack([cos_polar * cos_azim, cos_polar * sin_azim, sin_polar])
    tan_a = jnp.stack([-sin_azim, cos_azim, jnp.zeros_like(cos_azim)])
    tan_b = jnp.stack([-sin_polar * cos_azim, -sin_polar * sin_azim, cos_polar])
    return (normal, tan_a, tan_b)

def mobility(radius):
    cubed = radius * radius * radius
    linear = 1.0 / cubed
    angular = 2.5 / (cubed * radius * radius)
    return jnp.stack([linear, linear, linear, angular, angular, angular])

def project(trial_n, trial_a, trial_b, coulomb):
    tangent_len = jnp.sqrt(trial_a * trial_a + trial_b * trial_b)
    inside = tangent_len <= coulomb * trial_n
    dead = coulomb * tangent_len <= -trial_n
    cone_level = (trial_n + coulomb * tangent_len) / (1.0 + coulomb * coulomb)
    factor = coulomb * cone_level / jnp.maximum(tangent_len, SMALLEST)
    push_n = jnp.where(inside, trial_n, jnp.where(dead, 0.0, cone_level))
    push_a = jnp.where(inside, trial_a, jnp.where(dead, 0.0, factor * trial_a))
    push_b = jnp.where(inside, trial_b, jnp.where(dead, 0.0, factor * trial_b))
    return jnp.stack([push_n, push_a, push_b])

def pulse_of(impulse_now, angles, arm_pair, owner_ids, other_ids):
    normal, tan_a, tan_b = frames(angles)
    force = impulse_now[0] * normal + impulse_now[1] * tan_a + impulse_now[2] * tan_b
    twist = impulse_now[1] * tan_b - impulse_now[2] * tan_a
    on_owner = jnp.concatenate([force, -arm_pair[0] * twist], axis=0)
    on_other = jnp.concatenate([-force, -arm_pair[1] * twist], axis=0)
    total = jnp.zeros((6, EXTENT), jnp.float32)
    return total.at[:, owner_ids].add(on_owner).at[:, other_ids].add(on_other)

def solve_contacts(extended, impulse_now, angles, arm_pair, owner_ids, other_ids, coulomb, approach_rate):
    normal, tan_a, tan_b = frames(angles)
    near_vel = jnp.take(extended, owner_ids, axis=1)
    far_vel = jnp.take(extended, other_ids, axis=1)
    slip_lin = near_vel[:3] - far_vel[:3]
    spin_sum = arm_pair[0] * near_vel[3:] + arm_pair[1] * far_vel[3:]
    normal_rate = lax.optimization_barrier(jnp.sum(normal * slip_lin, axis=0))
    rate_a = lax.optimization_barrier(jnp.sum(tan_a * slip_lin, axis=0)) - lax.optimization_barrier(jnp.sum(tan_b * spin_sum, axis=0))
    rate_b = lax.optimization_barrier(jnp.sum(tan_b * slip_lin, axis=0)) + lax.optimization_barrier(jnp.sum(tan_a * spin_sum, axis=0))
    arm_near = arm_pair[0] * arm_pair[0] * arm_pair[0]
    arm_far = arm_pair[1] * arm_pair[1] * arm_pair[1]
    relax_step = RELAX / (1.0 / arm_near + 1.0 / arm_far)
    fresh = project(impulse_now[0] - relax_step * (normal_rate + approach_rate), impulse_now[1] - relax_step * rate_a, impulse_now[2] - relax_step * rate_b, coulomb)
    return (fresh, pulse_of(fresh, angles, arm_pair, owner_ids, other_ids))

def shift_grid(values, row_step, col_step):
    padding = [(1, 1), (1, 1)] + [(0, 0)] * (values.ndim - 2)
    padded = jnp.pad(values, padding)
    return padded[1 + row_step:1 + row_step + values.shape[0], 1 + col_step:1 + col_step + values.shape[1]]

def listed(velocity, lists):
    return jnp.stack([jnp.take(velocity, lists[number], axis=1) for number in range(4)])

def add_at(own_pulse, lists, received):
    return own_pulse.at[:, lists].add(received)

def per_grid(func):
    return jax.vmap(jax.vmap(func))

def reference(free_velocity, body_radius, face_lists, corner_lists, owner_body, other_body, contact_angles, contact_arms, friction, approach, start_impulse):
    inverse = per_grid(mobility)(body_radius)
    corner_base = BODY_DEV + 4 * FACE_LEN

    def fetch_ghosts(velocity):
        face_parts = per_grid(listed)(velocity, face_lists)
        corner_parts = per_grid(listed)(velocity, corner_lists)
        pieces = [velocity]
        for number in range(4):
            pieces.append(shift_grid(face_parts[:, :, number ^ 1], *FACE_STEPS[number]))
        for number in range(4):
            pieces.append(shift_grid(corner_parts[:, :, 3 - number], *CORNER_STEPS[number]))
        return jnp.concatenate(pieces, axis=-1)

    def settle(pulse):
        own_pulse = pulse[..., :BODY_DEV]
        for number in range(4):
            first = BODY_DEV + (number ^ 1) * FACE_LEN
            received = shift_grid(pulse[..., first:first + FACE_LEN], *FACE_STEPS[number])
            own_pulse = per_grid(add_at)(own_pulse, face_lists[:, :, number], received)
        for number in range(4):
            first = corner_base + (3 - number) * CORNER_LEN
            received = shift_grid(pulse[..., first:first + CORNER_LEN], *CORNER_STEPS[number])
            own_pulse = per_grid(add_at)(own_pulse, corner_lists[:, :, number], received)
        return free_velocity + inverse * own_pulse
    impulse_now = start_impulse
    velocity = settle(per_grid(pulse_of)(impulse_now, contact_angles, contact_arms, owner_body, other_body))
    for sweep in range(SWEEPS):
        extended = fetch_ghosts(velocity)
        impulse_now, pulse = per_grid(solve_contacts)(extended, impulse_now, contact_angles, contact_arms, owner_body, other_body, friction, approach)
        velocity = settle(pulse)
    return (velocity, impulse_now)
```

```python
import jax
import jax.numpy as jnp
from jax import lax
from jax.experimental import pallas as pl
from jax.experimental.pallas import tpu as pltpu
from jax.sharding import PartitionSpec as P

SWEEPS = 4
RELAX = 0.25
SMALLEST = 1e-20

BODY = 2048
FACE = 256
CORNER = 32
CONTACTS = 4096
ROWS = CONTACTS // 128
LISTED = 4 * FACE + 4 * CORNER
LIST_ROWS = LISTED // 128
OWN_TILES = BODY // 128
WIDE = 256
OWN_WIDE = BODY // WIDE
ALL_WIDE = 14
MESSAGE = FACE + 128

F32 = jnp.float32
BF16 = jnp.bfloat16
I32 = jnp.int32

PLANES = (
    "n0", "n1", "n2", "a0", "a1", "b0", "b1", "b2",
    "arm0", "arm1", "relax", "mu", "bias",
)
PLANE = {name: place for place, name in enumerate(PLANES)}


def lanes_of(table, lane):
    numbers = lax.GatherDimensionNumbers(
        offset_dims=(),
        collapsed_slice_dims=(1,),
        start_index_map=(1,),
        operand_batching_dims=(0,),
        start_indices_batching_dims=(0,),
    )
    return lax.gather(
        table, lane[..., None], numbers, (1, 1),
        mode=lax.GatherScatterMode.PROMISE_IN_BOUNDS,
    )


def iota(shape, dim):
    return lax.broadcasted_iota(I32, shape, dim)


def halves(values):
    high = values.astype(BF16).astype(F32)
    return high, values - high


def plane(ref, number):
    return ref[number * ROWS:(number + 1) * ROWS, :]


def spread(ref, row, high_row, parts, blocks, column):
    picks = [high_row == block for block in range(blocks)]
    for part, value in enumerate(parts):
        zero = jnp.zeros_like(value)
        for pair in range(blocks // 2):
            both = jnp.concatenate(
                [
                    jnp.where(picks[2 * pair], value, zero),
                    jnp.where(picks[2 * pair + 1], value, zero),
                ],
                axis=0,
            )
            start = part * blocks * 8 + pair * 16
            ref[start:start + 16, column:column + 128] = both.astype(BF16)


def lane_hot(ref, low, rows):
    turned = jnp.transpose(low)
    along = iota((128, WIDE), 1)
    for row in range(rows):
        hot = jnp.broadcast_to(turned[:, row:row + 1], (128, WIDE)) == along
        ref[row * 128:(row + 1) * 128, :] = jnp.where(hot, 1.0, 0.0).astype(BF16)


def scatter_contacts(impulse, table, high, left_near, left_far, moved):
    p0, p1, p2 = impulse
    get = lambda name: plane(table, PLANE[name])
    a0, a1 = get("a0"), get("a1")
    b0, b1, b2 = get("b0"), get("b1"), get("b2")
    force = (
        p0 * get("n0") + p1 * a0 + p2 * b0,
        p0 * get("n1") + p1 * a1 + p2 * b1,
        p0 * get("n2") + p2 * b2,
    )
    twist = (p1 * b0 - p2 * a0, p1 * b1 - p2 * a1, p1 * b2)
    arm0, arm1 = -get("arm0"), -get("arm1")
    for comp in range(3):
        moved[0, pl.ds(comp, ROWS, stride=8), :] = force[comp]
        moved[1, pl.ds(comp, ROWS, stride=8), :] = -force[comp]
        moved[0, pl.ds(comp + 3, ROWS, stride=8), :] = arm0 * twist[comp]
        moved[1, pl.ds(comp + 3, ROWS, stride=8), :] = arm1 * twist[comp]
    for comp in (6, 7):
        moved[0, pl.ds(comp, ROWS, stride=8), :] = jnp.zeros((ROWS, 128), F32)
        moved[1, pl.ds(comp, ROWS, stride=8), :] = jnp.zeros((ROWS, 128), F32)
    for row in range(ROWS):
        near = moved[0, row * 8:(row + 1) * 8, :]
        far = moved[1, row * 8:(row + 1) * 8, :]
        spread(left_near, row, high[row:row + 1, :], halves(near), OWN_WIDE, row * 128)
        spread(
            left_far, row, high[ROWS + row:ROWS + row + 1, :], halves(far), ALL_WIDE, row * 128
        )


def pulses(impulse, table, high, hot_near, hot_far, own_out, up, down, left, right, scratch):
    left_near, left_far, moved = scratch
    scatter_contacts(impulse, table, high, left_near, left_far, moved)
    near = jnp.dot(left_near[...], hot_near[...], preferred_element_type=F32)
    far = jnp.dot(left_far[...], hot_far[...], preferred_element_type=F32)
    near = near[:OWN_WIDE * 8] + near[OWN_WIDE * 8:]
    far = far[:ALL_WIDE * 8] + far[ALL_WIDE * 8:]
    for block in range(OWN_WIDE):
        rows = slice(block * 8, block * 8 + 8)
        own_out[:, block * WIDE:(block + 1) * WIDE] = near[rows] + far[rows]
    ghost = [far[block * 8:block * 8 + 8] for block in range(OWN_WIDE, OWN_WIDE + 5)]
    send(ghost[0], ghost[1], ghost[2], ghost[3], ghost[4][:, :128], up, down, left, right)


def send(face0, face1, face2, face3, corners, up, down, left, right):
    slot = iota((8, 128), 1) // CORNER
    to_down = (slot == 0) | (slot == 2)
    up[:, :FACE] = face0
    up[:, FACE:] = jnp.where(to_down, 0.0, corners)
    down[:, :FACE] = face1
    down[:, FACE:] = jnp.where(to_down, corners, 0.0)
    left[...] = face2
    right[...] = face3


def prepare(
    angles, arms, mu, bias, impulse, owner, other, radius, faces, corners,
    table, places, high, inverse, impulse_out, hot_near, hot_far, hot_list, list_places,
    own_out, up, down, left, right,
    flat, left_near, left_far, moved,
):
    for row in range(ROWS):
        cut = slice(row * 128, (row + 1) * 128)
        flat[pl.ds(row, 2, stride=ROWS), :] = angles[:, cut]
        flat[pl.ds(2 * ROWS + row, 2, stride=ROWS), :] = arms[:, cut]
        flat[pl.ds(4 * ROWS + row, 3, stride=ROWS), :] = impulse[:, cut]
    polar, azim = plane(flat, 0), plane(flat, 1)
    arm0, arm1 = plane(flat, 2), plane(flat, 3)
    impulse_now = [plane(flat, 4 + comp) for comp in range(3)]
    cos_polar, sin_polar = jnp.cos(polar), jnp.sin(polar)
    cos_azim, sin_azim = jnp.cos(azim), jnp.sin(azim)
    cubed0 = arm0 * arm0 * arm0
    cubed1 = arm1 * arm1 * arm1
    values = {
        "n0": cos_polar * cos_azim, "n1": cos_polar * sin_azim, "n2": sin_polar,
        "a0": -sin_azim, "a1": cos_azim,
        "b0": -sin_polar * cos_azim, "b1": -sin_polar * sin_azim, "b2": cos_polar,
        "arm0": arm0, "arm1": arm1,
        "relax": RELAX / (1.0 / cubed0 + 1.0 / cubed1),
        "mu": mu[...], "bias": bias[...],
    }
    for name, value in values.items():
        number = PLANE[name]
        table[number * ROWS:(number + 1) * ROWS, :] = value
    for comp in range(3):
        impulse_out[comp * ROWS:(comp + 1) * ROWS, :] = impulse_now[comp]

    near_id = owner[...]
    far_id = other[...]
    extra = far_id - (BODY + 4 * FACE)
    block = extra >> 5
    slot = ((block & 1) << 1) | (block >> 1)
    in_block = extra & (CORNER - 1)
    is_corner = extra >= 0
    places[:ROWS, :] = near_id >> 7
    places[ROWS:2 * ROWS, :] = near_id & 127
    places[2 * ROWS:3 * ROWS, :] = far_id >> 7
    places[3 * ROWS:, :] = jnp.where(is_corner, slot * CORNER + in_block, far_id & 127)
    high[:ROWS, :] = near_id >> 8
    high[ROWS:, :] = far_id >> 8
    lane_hot(hot_near, near_id & 255, ROWS)
    lane_hot(
        hot_far, jnp.where(is_corner, (3 - slot) * CORNER + in_block, far_id & 255), ROWS
    )

    for number in range(4):
        for part in range(2):
            row = number * 2 + part
            list_places[row:row + 1, :] = faces[number:number + 1, part * 128:(part + 1) * 128]
    for place, number in enumerate((0, 2, 1, 3)):
        list_places[8:9, place * CORNER:(place + 1) * CORNER] = corners[number:number + 1, :]
    for place, number in enumerate((3, 1, 2, 0)):
        list_places[9:10, place * CORNER:(place + 1) * CORNER] = corners[number:number + 1, :]
    list_places[10:, :] = jnp.zeros((6, 128), I32)
    lane_hot(hot_list, list_places[...] & 255, LIST_ROWS)

    size = radius[...]
    cubed = size * size * size
    linear = 1.0 / cubed
    angular = 2.5 / (cubed * size * size)
    inverse[...] = jnp.where(iota((8, BODY), 0) < 3, linear, angular)
    pulses(
        impulse_now, table, high, hot_near, hot_far, own_out, up, down, left, right,
        (left_near, left_far, moved),
    )


def forward(flags, from_up, from_down, left, right, to_left, to_right):
    corners = masked(flags, 0, from_up[:, FACE:]) + masked(flags, 1, from_down[:, FACE:])
    to_left[:, :FACE] = left[...]
    to_right[:, :FACE] = right[...]
    to_left[:, FACE:] = corners
    to_right[:, FACE:] = corners


def masked(flags, number, value):
    return jnp.where(flags[number] > 0, value, jnp.zeros_like(value))


def received_tiles(flags, from_up, from_down, from_left, from_right):
    tiles = []
    for number, ref in enumerate((from_up, from_down, from_left, from_right)):
        for part in range(2):
            tiles.append(masked(flags, number, ref[:, part * 128:(part + 1) * 128]))
    early = iota((8, 128), 1) < 2 * CORNER
    tiles.append(
        jnp.where(
            early, masked(flags, 2, from_left[:, FACE:]), masked(flags, 3, from_right[:, FACE:])
        )
    )
    return tiles


def settled(flags, own, inverse, base, list_places, hot_list, from_up, from_down, from_left, from_right, left_list):
    tiles = received_tiles(flags, from_up, from_down, from_left, from_right)
    for row, tile in enumerate(tiles):
        high_row = list_places[row:row + 1, :] >> 8
        spread(left_list, row, high_row, halves(tile), OWN_WIDE, row * 128)
    added = jnp.dot(left_list[...], hot_list[...], preferred_element_type=F32)
    added = added[:OWN_WIDE * 8] + added[OWN_WIDE * 8:]
    blocks = []
    for block in range(OWN_WIDE):
        cut = slice(block * WIDE, (block + 1) * WIDE)
        total = own[:6, cut] + added[block * 8:block * 8 + 6]
        blocks.append(base[:, cut] + inverse[:6, cut] * total)
    return blocks


def settle(
    flags, own, inverse, base, list_places, hot_list, from_up, from_down, from_left, from_right,
    velocity, up, down, left, right, left_list,
):
    blocks = settled(
        flags, own, inverse, base, list_places, hot_list,
        from_up, from_down, from_left, from_right, left_list,
    )
    zero = jnp.zeros((2, WIDE), F32)
    for block, value in enumerate(blocks):
        velocity[:, block * WIDE:(block + 1) * WIDE] = jnp.concatenate([value, zero], axis=0)
    found = []
    for row in (0, 1, 2, 3, 4, 5, 6, 7, 9):
        entry = jnp.broadcast_to(list_places[row:row + 1, :], (8, 128))
        tile_id, lane = entry >> 7, entry & 127
        total = jnp.zeros((8, 128), F32)
        for tile in range(OWN_TILES):
            table = velocity[:, tile * 128:(tile + 1) * 128]
            total = jnp.where(tile_id == tile, lanes_of(table, lane), total)
        found.append(total)
    face = [jnp.concatenate(found[2 * k:2 * k + 2], axis=1) for k in range(4)]
    send(*face, found[8], up, down, left, right)


def settle_last(
    flags, own, inverse, base, list_places, hot_list, from_up, from_down, from_left, from_right,
    velocity, left_list,
):
    blocks = settled(
        flags, own, inverse, base, list_places, hot_list,
        from_up, from_down, from_left, from_right, left_list,
    )
    for block, value in enumerate(blocks):
        velocity[:, block * WIDE:(block + 1) * WIDE] = value


def pick(tables, tile_id, lane, firsts):
    totals = [jnp.zeros((ROWS, 128), F32) for _ in range(6)]
    for tile, table in zip(firsts, tables):
        here = tile_id == tile
        for comp in range(6):
            row = jnp.broadcast_to(table[comp:comp + 1, :], (ROWS, 128))
            totals[comp] = jnp.where(here, lanes_of(row, lane), totals[comp])
    return totals


def solved(flags, velocity, table, places, impulse, from_up, from_down, from_left, from_right):
    own_tables = [velocity[:, tile * 128:(tile + 1) * 128] for tile in range(OWN_TILES)]
    ghosts = received_tiles(flags, from_up, from_down, from_left, from_right)
    near = pick(own_tables, places[:ROWS, :], places[ROWS:2 * ROWS, :], range(OWN_TILES))
    far = pick(
        own_tables + ghosts, places[2 * ROWS:3 * ROWS, :], places[3 * ROWS:, :],
        range(OWN_TILES + 9),
    )
    get = lambda name: plane(table, PLANE[name])
    n0, n1, n2 = get("n0"), get("n1"), get("n2")
    a0, a1 = get("a0"), get("a1")
    b0, b1, b2 = get("b0"), get("b1"), get("b2")
    arm0, arm1, relax, mu = get("arm0"), get("arm1"), get("relax"), get("mu")
    w0, w1, w2 = [near[c] - far[c] for c in range(3)]
    s0, s1, s2 = [arm0 * near[c] + arm1 * far[c] for c in range(3, 6)]
    rate_n = n0 * w0 + n1 * w1 + n2 * w2
    rate_a = (a0 * w0 + a1 * w1) - (b0 * s0 + b1 * s1 + b2 * s2)
    rate_b = (b0 * w0 + b1 * w1 + b2 * w2) + (a0 * s0 + a1 * s1)
    trial_n = plane(impulse, 0) - relax * (rate_n + get("bias"))
    trial_a = plane(impulse, 1) - relax * rate_a
    trial_b = plane(impulse, 2) - relax * rate_b
    length = jnp.sqrt(trial_a * trial_a + trial_b * trial_b)
    inside = length <= mu * trial_n
    dead = mu * length <= -trial_n
    level = (trial_n + mu * length) / (1.0 + mu * mu)
    factor = mu * level / jnp.maximum(length, SMALLEST)
    choose = lambda kept, cone: jnp.where(inside, kept, jnp.where(dead, 0.0, cone))
    return [
        choose(trial_n, level), choose(trial_a, factor * trial_a), choose(trial_b, factor * trial_b)
    ]


def sweep(
    flags, velocity, table, places, high, hot_near, hot_far, impulse,
    from_up, from_down, from_left, from_right,
    impulse_out, own_out, up, down, left, right,
    left_near, left_far, moved,
):
    fresh = solved(
        flags, velocity, table, places, impulse, from_up, from_down, from_left, from_right
    )
    for comp in range(3):
        impulse_out[comp * ROWS:(comp + 1) * ROWS, :] = fresh[comp]
    pulses(
        fresh, table, high, hot_near, hot_far, own_out, up, down, left, right,
        (left_near, left_far, moved),
    )


def shape(*dims, kind=F32):
    return jax.ShapeDtypeStruct(dims, kind)


SENDS = (shape(8, MESSAGE), shape(8, MESSAGE), shape(8, FACE), shape(8, FACE))
LEFTS = (
    pltpu.VMEM((2 * OWN_WIDE * 8, CONTACTS), BF16),
    pltpu.VMEM((2 * ALL_WIDE * 8, CONTACTS), BF16),
    pltpu.VMEM((2, ROWS * 8, 128), F32),
)
LEFT_LIST = pltpu.VMEM((2 * OWN_WIDE * 8, LISTED), BF16)


def call(body, outs, scratch, flagged, *operands):
    vmem = pl.BlockSpec(memory_space=pltpu.VMEM)
    specs = [vmem] * len(operands)
    if flagged:
        specs[0] = pl.BlockSpec(memory_space=pltpu.SMEM)
    return pl.pallas_call(
        body,
        out_shape=outs,
        in_specs=specs,
        out_specs=[vmem] * len(outs),
        scratch_shapes=scratch,
        compiler_params=pltpu.CompilerParams(vmem_limit_bytes=24 * 1024 * 1024),
    )(*operands)


def ring(value, axis, step):
    size = lax.axis_size(axis)
    return lax.ppermute(value, axis, [(i, (i + step) % size) for i in range(size)])


def exchange(flags, up, down, left, right):
    from_up = ring(down, "gx", 1)
    from_down = ring(up, "gx", -1)
    to_left, to_right = call(
        forward, (shape(8, MESSAGE), shape(8, MESSAGE)), (), True,
        flags, from_up, from_down, left, right,
    )
    from_left = ring(to_right, "gy", 1)
    from_right = ring(to_left, "gy", -1)
    return from_up, from_down, from_left, from_right


def shards(
    free_velocity, body_radius, face_lists, corner_lists, owner_body, other_body,
    contact_angles, contact_arms, friction, approach, start_impulse,
):
    base = free_velocity[0, 0]
    row_at, row_count = lax.axis_index("gx"), lax.axis_size("gx")
    col_at, col_count = lax.axis_index("gy"), lax.axis_size("gy")
    flags = jnp.stack(
        [row_at > 0, row_at < row_count - 1, col_at > 0, col_at < col_count - 1]
    ).astype(I32)
    in_rows = lambda value: value[0, 0].reshape(ROWS, 128)
    (
        table, places, high, inverse, impulse, hot_near, hot_far, hot_list, list_places,
        own, up, down, left, right,
    ) = call(
        prepare,
        (
            shape(len(PLANES) * ROWS, 128),
            shape(4 * ROWS, 128, kind=I32),
            shape(2 * ROWS, 128, kind=I32),
            shape(8, BODY),
            shape(3 * ROWS, 128),
            shape(CONTACTS, WIDE, kind=BF16),
            shape(CONTACTS, WIDE, kind=BF16),
            shape(LISTED, WIDE, kind=BF16),
            shape(16, 128, kind=I32),
            shape(8, BODY),
        ) + SENDS,
        (pltpu.VMEM((7 * ROWS, 128), F32),) + LEFTS,
        False,
        contact_angles[0, 0], contact_arms[0, 0], in_rows(friction), in_rows(approach),
        start_impulse[0, 0], in_rows(owner_body), in_rows(other_body),
        body_radius[0], face_lists[0, 0], corner_lists[0, 0],
    )
    for number in range(SWEEPS + 1):
        got = exchange(flags, up, down, left, right)
        fixed = (flags, own, inverse, base, list_places, hot_list)
        if number == SWEEPS:
            (velocity,) = call(
                settle_last, (shape(6, BODY),), (LEFT_LIST,), True, *fixed, *got
            )
            break
        velocity, up, down, left, right = call(
            settle, (shape(8, BODY),) + SENDS, (LEFT_LIST,), True, *fixed, *got
        )
        got = exchange(flags, up, down, left, right)
        impulse, own, up, down, left, right = call(
            sweep, (shape(3 * ROWS, 128), shape(8, BODY)) + SENDS, LEFTS, True,
            flags, velocity, table, places, high, hot_near, hot_far, impulse, *got,
        )
    return velocity[None, None], impulse.reshape(1, 1, 3, CONTACTS)


def solution(mesh):
    in_specs = (
        P("gx", "gy", None, None),
        P("gx", "gy", None),
        P("gx", "gy", None, None),
        P("gx", "gy", None, None),
        P("gx", "gy", None),
        P("gx", "gy", None),
        P("gx", "gy", None, None),
        P("gx", "gy", None, None),
        P("gx", "gy", None),
        P("gx", "gy", None),
        P("gx", "gy", None, None),
    )
    out_specs = (P("gx", "gy", None, None), P("gx", "gy", None, None))
    return jax.shard_map(shards, mesh=mesh, in_specs=in_specs, out_specs=out_specs, check_vma=False)
```

```python
import jax
import jax.numpy as jnp
from jax import lax
from jax.experimental import pallas as pl
from jax.experimental.pallas import tpu as pltpu
from jax.sharding import PartitionSpec as P

SWEEPS = 4
RELAX = 0.25
SMALLEST = 1e-20

BODY = 2048
FACE = 256
CORNER = 32
CONTACTS = 4096
ROWS = CONTACTS // 128
LISTED = 4 * FACE + 4 * CORNER
LIST_ROWS = LISTED // 128
OWN_TILES = BODY // 128
WIDE = 256
OWN_WIDE = BODY // WIDE
GHOST_WIDE = 6
IMPULSE_ROWS = 3 * ROWS
MESSAGE = FACE + 128

F32 = jnp.float32
BF16 = jnp.bfloat16
I32 = jnp.int32

PLANES = (
    "n0", "n1", "n2", "a0", "a1", "b0", "b1", "b2",
    "arm0", "arm1", "relax", "mu", "bias",
)
PLANE = {name: place for place, name in enumerate(PLANES)}


def lanes_of(table, lane):
    numbers = lax.GatherDimensionNumbers(
        offset_dims=(),
        collapsed_slice_dims=(1,),
        start_index_map=(1,),
        operand_batching_dims=(0,),
        start_indices_batching_dims=(0,),
    )
    return lax.gather(
        table, lane[..., None], numbers, (1, 1),
        mode=lax.GatherScatterMode.PROMISE_IN_BOUNDS,
    )


def iota(shape, dim):
    return lax.broadcasted_iota(I32, shape, dim)


def halves(values):
    high = values.astype(BF16).astype(F32)
    return high, values - high


def plane(ref, number):
    return ref[number * ROWS:(number + 1) * ROWS, :]


def spread(ref, high_row, parts, blocks, column):
    picks = [high_row == block for block in blocks]
    for part, value in enumerate(parts):
        zero = jnp.zeros_like(value)
        for pair in range(len(blocks) // 2):
            both = jnp.concatenate(
                [
                    jnp.where(picks[2 * pair], value, zero),
                    jnp.where(picks[2 * pair + 1], value, zero),
                ],
                axis=0,
            )
            start = part * len(blocks) * 8 + pair * 16
            ref[start:start + 16, column:column + 128] = both.astype(BF16)


OWN_BLOCKS = tuple(range(OWN_WIDE))
GHOST_BLOCKS = tuple(range(OWN_WIDE, OWN_WIDE + GHOST_WIDE))


def lane_hot(ref, low, rows):
    turned = jnp.transpose(low)
    along = iota((128, WIDE), 1)
    for row in range(rows):
        hot = jnp.broadcast_to(turned[:, row:row + 1], (128, WIDE)) == along
        ref[row * 128:(row + 1) * 128, :] = jnp.where(hot, 1.0, 0.0).astype(BF16)


def product(left, hot, blocks):
    total = jnp.dot(left[...], hot, preferred_element_type=F32)
    return total[:blocks * 8] + total[blocks * 8:]


def end_pulses(impulse, table, near_out, far_out):
    p0, p1, p2 = impulse
    get = lambda name: plane(table, PLANE[name])
    a0, a1 = get("a0"), get("a1")
    b0, b1, b2 = get("b0"), get("b1"), get("b2")
    force = (
        p0 * get("n0") + p1 * a0 + p2 * b0,
        p0 * get("n1") + p1 * a1 + p2 * b1,
        p0 * get("n2") + p2 * b2,
    )
    twist = (p1 * b0 - p2 * a0, p1 * b1 - p2 * a1, p1 * b2)
    arm0, arm1 = -get("arm0"), -get("arm1")
    for comp in range(3):
        near_out[pl.ds(comp, ROWS, stride=8), :] = force[comp]
        far_out[pl.ds(comp, ROWS, stride=8), :] = -force[comp]
        near_out[pl.ds(comp + 3, ROWS, stride=8), :] = arm0 * twist[comp]
        far_out[pl.ds(comp + 3, ROWS, stride=8), :] = arm1 * twist[comp]
    for comp in (6, 7):
        near_out[pl.ds(comp, ROWS, stride=8), :] = jnp.zeros((ROWS, 128), F32)
        far_out[pl.ds(comp, ROWS, stride=8), :] = jnp.zeros((ROWS, 128), F32)


def spread_rows(left, values, high, blocks):
    for row in range(ROWS):
        value = values[row * 8:(row + 1) * 8, :]
        spread(left, high[row:row + 1, :], halves(value), blocks, row * 128)


def ghost_pulses(far, high_far, hot_far, up, down, left, right, left_ghost):
    spread_rows(left_ghost, far, high_far, GHOST_BLOCKS)
    total = product(left_ghost, hot_far[...], GHOST_WIDE)
    ghost = [total[block * 8:block * 8 + 8] for block in range(5)]
    send_gx(ghost[0], ghost[1], ghost[4][:, :128], up, down)
    left[...] = ghost[2]
    right[...] = ghost[3]


def send_gx(face0, face1, corners, up, down):
    slot = iota((8, 128), 1) // CORNER
    to_down = (slot == 0) | (slot == 2)
    up[:, :FACE] = face0
    up[:, FACE:] = jnp.where(to_down, 0.0, corners)
    down[:, :FACE] = face1
    down[:, FACE:] = jnp.where(to_down, corners, 0.0)


def prepare(
    angles_in, arms_in, mu_in, bias_in, impulse_in, owner_in, other_in,
    radius_in, faces_in, corners_in, base_in,
    table, places, high_far, impulse, hot_far, near_values, far_values,
    up, down, left, right,
    owner, radius, faces, corners, base,
    angles, arms, mu, bias, other, flat, left_ghost, sems,
):
    copies = [
        pltpu.make_async_copy(source, target, sems.at[number])
        for number, (source, target) in enumerate((
            (other_in, other), (angles_in, angles), (arms_in, arms), (mu_in, mu),
            (bias_in, bias), (impulse_in, impulse), (owner_in, owner), (radius_in, radius),
            (faces_in, faces), (corners_in, corners), (base_in, base),
        ))
    ]
    for copy in copies:
        copy.start()
    copies[0].wait()
    far_id = other[...]
    extra = far_id - (BODY + 4 * FACE)
    block = extra >> 5
    slot = ((block & 1) << 1) | (block >> 1)
    in_block = extra & (CORNER - 1)
    is_corner = extra >= 0
    places[2 * ROWS:3 * ROWS, :] = far_id >> 7
    places[3 * ROWS:, :] = jnp.where(is_corner, slot * CORNER + in_block, far_id & 127)
    high_far[...] = far_id >> 8
    lane_hot(
        hot_far, jnp.where(is_corner, (3 - slot) * CORNER + in_block, far_id & 255), ROWS
    )
    for copy in copies[1:]:
        copy.wait()
    near_id = owner[...]
    places[:ROWS, :] = near_id >> 7
    places[ROWS:2 * ROWS, :] = near_id & 127
    for row in range(ROWS):
        cut = slice(row * 128, (row + 1) * 128)
        flat[pl.ds(row, 2, stride=ROWS), :] = angles[:, cut]
        flat[pl.ds(2 * ROWS + row, 2, stride=ROWS), :] = arms[:, cut]
    polar, azim = plane(flat, 0), plane(flat, 1)
    arm0, arm1 = plane(flat, 2), plane(flat, 3)
    cos_polar, sin_polar = jnp.cos(polar), jnp.sin(polar)
    cos_azim, sin_azim = jnp.cos(azim), jnp.sin(azim)
    cubed0 = arm0 * arm0 * arm0
    cubed1 = arm1 * arm1 * arm1
    values = {
        "n0": cos_polar * cos_azim, "n1": cos_polar * sin_azim, "n2": sin_polar,
        "a0": -sin_azim, "a1": cos_azim,
        "b0": -sin_polar * cos_azim, "b1": -sin_polar * sin_azim, "b2": cos_polar,
        "arm0": arm0, "arm1": arm1,
        "relax": RELAX / (1.0 / cubed0 + 1.0 / cubed1),
        "mu": mu[...], "bias": bias[...],
    }
    for name, value in values.items():
        number = PLANE[name]
        table[number * ROWS:(number + 1) * ROWS, :] = value
    end_pulses([plane(impulse, comp) for comp in range(3)], table, near_values, far_values)
    ghost_pulses(far_values, high_far, hot_far, up, down, left, right, left_ghost)


def prepare_own(
    near_values, owner, radius, faces, corners, base_rows,
    pulse, high_near, hot_near, hot_list, list_places, inverse, base,
    left_near,
):
    near_id = owner[...]
    high_near[...] = near_id >> 8
    lane_hot(hot_near, near_id & 255, ROWS)
    for number in range(4):
        for part in range(2):
            row = number * 2 + part
            list_places[row:row + 1, :] = faces[number:number + 1, part * 128:(part + 1) * 128]
    for place, number in enumerate((0, 2, 1, 3)):
        list_places[8:9, place * CORNER:(place + 1) * CORNER] = corners[number:number + 1, :]
    for place, number in enumerate((3, 1, 2, 0)):
        list_places[9:10, place * CORNER:(place + 1) * CORNER] = corners[number:number + 1, :]
    list_places[10:, :] = jnp.zeros((6, 128), I32)
    lane_hot(hot_list, list_places[...] & 255, LIST_ROWS)

    size = radius[...]
    cubed = size * size * size
    linear = 1.0 / cubed
    angular = 2.5 / (cubed * size * size)
    inverse[...] = jnp.where(iota((8, BODY), 0) < 3, linear, angular)
    for tile in range(OWN_TILES):
        base[:, tile * 128:(tile + 1) * 128] = base_rows[pl.ds(tile, 6, stride=OWN_TILES), :]
    scatter_near(near_values, high_near, hot_near, pulse, left_near)


def store_blocks(pulse, total):
    for block in range(OWN_WIDE):
        pulse[:, block * WIDE:(block + 1) * WIDE] = total[block * 8:block * 8 + 8]


def scatter_near(values, high_near, hot_near, pulse, left_near):
    spread_rows(left_near, values, high_near, OWN_BLOCKS)
    store_blocks(pulse, product(left_near, hot_near[...], OWN_WIDE))


def masked(flags, number, value):
    return jnp.where(flags[number:number + 1, :] > 0, value, jnp.zeros_like(value))


def gx_tiles(flags, from_up, from_down):
    return [
        masked(flags, number, ref[:, part * 128:(part + 1) * 128])
        for number, ref in enumerate((from_up, from_down))
        for part in range(2)
    ]


def gy_tiles(flags, from_left, from_right):
    tiles = [
        masked(flags, number + 2, ref[:, part * 128:(part + 1) * 128])
        for number, ref in enumerate((from_left, from_right))
        for part in range(2)
    ]
    early = iota((8, 128), 1) < 2 * CORNER
    corners = jnp.where(early, from_left[:, FACE:], from_right[:, FACE:])
    return tiles + [masked(flags, 4, corners)]


def list_product(left_list, tiles, list_places, hot, first):
    for row, tile in enumerate(tiles):
        high_row = list_places[first + row:first + row + 1, :] >> 8
        spread(left_list, high_row, halves(tile), OWN_BLOCKS, row * 128)
    rows = slice(first * 128, (first + len(tiles)) * 128)
    return product(left_list, hot[rows, :], OWN_WIDE)


def scatter_far(
    flags, values, high_far, hot_far, near_pulse, list_places, hot_list, from_up, from_down,
    pulse, left_far, left_list,
):
    spread_rows(left_far, values, high_far, OWN_BLOCKS)
    total = product(left_far, hot_far[...], OWN_WIDE)
    total = total + list_product(
        left_list, gx_tiles(flags, from_up, from_down), list_places, hot_list, 0
    )
    for block in range(OWN_WIDE):
        cut = slice(block * WIDE, (block + 1) * WIDE)
        pulse[:, cut] = near_pulse[:, cut] + total[block * 8:block * 8 + 8]


def settled(flags, own, inverse, base, list_places, hot_list, from_left, from_right, left_list):
    added = list_product(
        left_list, gy_tiles(flags, from_left, from_right), list_places, hot_list, 4
    )
    blocks = []
    for block in range(OWN_WIDE):
        cut = slice(block * WIDE, (block + 1) * WIDE)
        total = own[:6, cut] + added[block * 8:block * 8 + 6]
        blocks.append(base[:, cut] + inverse[:6, cut] * total)
    return blocks


def listed(velocity, list_places, row):
    entry = jnp.broadcast_to(list_places[row:row + 1, :], (8, 128))
    tile_id, lane = entry >> 7, entry & 127
    total = jnp.zeros((8, 128), F32)
    for tile in range(OWN_TILES):
        table = velocity[:, tile * 128:(tile + 1) * 128]
        total = jnp.where(tile_id == tile, lanes_of(table, lane), total)
    return total


def settle(
    flags, own, inverse, base, list_places, hot_list, from_left, from_right,
    velocity, up, down, left_list,
):
    blocks = settled(
        flags, own, inverse, base, list_places, hot_list, from_left, from_right, left_list
    )
    zero = jnp.zeros((2, WIDE), F32)
    for block, value in enumerate(blocks):
        velocity[:, block * WIDE:(block + 1) * WIDE] = jnp.concatenate([value, zero], axis=0)
    found = [listed(velocity, list_places, row) for row in (0, 1, 2, 3, 9)]
    face = [jnp.concatenate(found[2 * k:2 * k + 2], axis=1) for k in range(2)]
    send_gx(*face, found[4], up, down)


def settle_last(
    flags, own, inverse, base, list_places, hot_list, from_left, from_right,
    velocity, left_list,
):
    blocks = settled(
        flags, own, inverse, base, list_places, hot_list, from_left, from_right, left_list
    )
    for block, value in enumerate(blocks):
        for part in range(2):
            tile = 2 * block + part
            velocity[pl.ds(tile, 6, stride=OWN_TILES), :] = value[:, part * 128:(part + 1) * 128]


def pick(tables, tile_id, lane, firsts, totals):
    for tile, table in zip(firsts, tables):
        here = tile_id == tile
        for comp in range(6):
            row = jnp.broadcast_to(table[comp:comp + 1, :], (ROWS, 128))
            totals[comp] = jnp.where(here, lanes_of(row, lane), totals[comp])
    return totals


def own_tables(velocity):
    return [velocity[:, tile * 128:(tile + 1) * 128] for tile in range(OWN_TILES)]


def blank():
    return [jnp.zeros((ROWS, 128), F32) for _ in range(6)]


def gather_near(velocity, places, list_places, near, left, right):
    for row, (ref, part) in enumerate(((left, 0), (left, 1), (right, 0), (right, 1))):
        ref[:, part * 128:(part + 1) * 128] = listed(velocity, list_places, 4 + row)
    found = pick(
        own_tables(velocity), places[:ROWS, :], places[ROWS:2 * ROWS, :], range(OWN_TILES), blank()
    )
    for comp in range(6):
        near[comp * ROWS:(comp + 1) * ROWS, :] = found[comp]


def gather_far(flags, velocity, places, from_up, from_down, far):
    found = pick(
        own_tables(velocity) + gx_tiles(flags, from_up, from_down),
        places[2 * ROWS:3 * ROWS, :], places[3 * ROWS:, :], range(OWN_TILES + 4), blank(),
    )
    for comp in range(6):
        far[comp * ROWS:(comp + 1) * ROWS, :] = found[comp]


def sweep(
    flags, near_ref, far_ref, table, places, high_far, hot_far, impulse, from_left, from_right,
    impulse_out, near_values, far_values, up, down, left, right, left_ghost,
):
    near = [plane(near_ref, comp) for comp in range(6)]
    far = pick(
        gy_tiles(flags, from_left, from_right),
        places[2 * ROWS:3 * ROWS, :], places[3 * ROWS:, :],
        range(OWN_TILES + 4, OWN_TILES + 9), [plane(far_ref, comp) for comp in range(6)],
    )
    get = lambda name: plane(table, PLANE[name])
    n0, n1, n2 = get("n0"), get("n1"), get("n2")
    a0, a1 = get("a0"), get("a1")
    b0, b1, b2 = get("b0"), get("b1"), get("b2")
    arm0, arm1, relax, mu = get("arm0"), get("arm1"), get("relax"), get("mu")
    w0, w1, w2 = [near[c] - far[c] for c in range(3)]
    s0, s1, s2 = [arm0 * near[c] + arm1 * far[c] for c in range(3, 6)]
    rate_n = n0 * w0 + n1 * w1 + n2 * w2
    rate_a = (a0 * w0 + a1 * w1) - (b0 * s0 + b1 * s1 + b2 * s2)
    rate_b = (b0 * w0 + b1 * w1 + b2 * w2) + (a0 * s0 + a1 * s1)
    trial_n = plane(impulse, 0) - relax * (rate_n + get("bias"))
    trial_a = plane(impulse, 1) - relax * rate_a
    trial_b = plane(impulse, 2) - relax * rate_b
    length = jnp.sqrt(trial_a * trial_a + trial_b * trial_b)
    inside = length <= mu * trial_n
    dead = mu * length <= -trial_n
    level = (trial_n + mu * length) / (1.0 + mu * mu)
    factor = mu * level / jnp.maximum(length, SMALLEST)
    choose = lambda kept, cone: jnp.where(inside, kept, jnp.where(dead, 0.0, cone))
    fresh = [
        choose(trial_n, level), choose(trial_a, factor * trial_a), choose(trial_b, factor * trial_b)
    ]
    for comp in range(3):
        impulse_out[comp * ROWS:(comp + 1) * ROWS, :] = fresh[comp]
    end_pulses(fresh, table, near_values, far_values)
    ghost_pulses(far_values, high_far, hot_far, up, down, left, right, left_ghost)


def shape(*dims, kind=F32):
    return jax.ShapeDtypeStruct(dims, kind)


FACES = (shape(8, FACE), shape(8, FACE))
GX_SENDS = (shape(8, MESSAGE), shape(8, MESSAGE))
VALUES = shape(8 * ROWS, 128)
PULSE = shape(8, BODY)
LEFT_OWN = pltpu.VMEM((2 * OWN_WIDE * 8, CONTACTS), BF16)
LEFT_GHOST = pltpu.VMEM((2 * GHOST_WIDE * 8, CONTACTS), BF16)


def left_list(tiles):
    return pltpu.VMEM((2 * OWN_WIDE * 8, tiles * 128), BF16)


def call(body, outs, scratch, *operands, space=pltpu.VMEM, cost=0):
    vmem = pl.BlockSpec(memory_space=pltpu.VMEM)
    return pl.pallas_call(
        body,
        out_shape=outs,
        in_specs=[pl.BlockSpec(memory_space=space)] * len(operands),
        out_specs=[vmem] * len(outs),
        scratch_shapes=scratch,
        compiler_params=pltpu.CompilerParams(vmem_limit_bytes=10 * 1024 * 1024),
    )(*operands)


def ring(value, axis, step):
    size = lax.axis_size(axis)
    return lax.ppermute(value, axis, [(i, (i + step) % size) for i in range(size)])


def along_gx(up, down):
    return ring(down, "gx", 1), ring(up, "gx", -1)


def along_gy(from_up, from_down, left, right):
    corners = from_up[:, FACE:] + from_down[:, FACE:]
    to_left = jnp.concatenate([left, corners], axis=1)
    to_right = jnp.concatenate([right, corners], axis=1)
    return ring(to_right, "gy", 1), ring(to_left, "gy", -1)


def presence():
    row_at, row_count = lax.axis_index("gx"), lax.axis_size("gx")
    col_at, col_count = lax.axis_index("gy"), lax.axis_size("gy")
    row, slot = iota((8, 128), 0), iota((8, 128), 1) // CORNER
    vertical = (row == 0) | ((row == 4) & ((slot == 0) | (slot == 2)))
    below = (row == 1) | ((row == 4) & ((slot == 1) | (slot == 3)))
    before = (row == 2) | ((row == 4) & (slot < 2))
    after = (row == 3) | ((row == 4) & (slot >= 2))
    absent = (
        (vertical & (row_at == 0)) | (below & (row_at == row_count - 1))
        | (before & (col_at == 0)) | (after & (col_at == col_count - 1))
    )
    return jnp.where(absent, 0.0, 1.0)


def shards(
    free_velocity, body_radius, face_lists, corner_lists, owner_body, other_body,
    contact_angles, contact_arms, friction, approach, start_impulse,
):
    flags = presence()
    in_rows = lambda value: value[0, 0].reshape(-1, 128)
    dma = pltpu.SemaphoreType.DMA
    (
        table, places, high_far, impulse, hot_far, near_values, far_values,
        up, down, left, right, owner, radius, faces, corners, base_rows,
    ) = call(
        prepare,
        (
            shape(len(PLANES) * ROWS, 128),
            shape(4 * ROWS, 128, kind=I32),
            shape(ROWS, 128, kind=I32),
            shape(IMPULSE_ROWS, 128),
            shape(CONTACTS, WIDE, kind=BF16),
            VALUES, VALUES,
        ) + GX_SENDS + FACES + (
            shape(ROWS, 128, kind=I32),
            shape(1, BODY),
            shape(4, FACE, kind=I32),
            shape(4, CORNER, kind=I32),
            shape(6 * OWN_TILES, 128),
        ),
        (
            pltpu.VMEM((2, CONTACTS), F32),
            pltpu.VMEM((2, CONTACTS), F32),
            pltpu.VMEM((ROWS, 128), F32),
            pltpu.VMEM((ROWS, 128), F32),
            pltpu.VMEM((ROWS, 128), I32),
            pltpu.VMEM((4 * ROWS, 128), F32),
            LEFT_GHOST,
            dma((11,)),
        ),
        contact_angles[0, 0], contact_arms[0, 0], in_rows(friction), in_rows(approach),
        in_rows(start_impulse), in_rows(owner_body), in_rows(other_body),
        body_radius[0], face_lists[0, 0], corner_lists[0, 0], in_rows(free_velocity),
        space=pltpu.HBM,
    )
    for number in range(SWEEPS + 1):
        from_up, from_down = along_gx(up, down)
        if number == 0:
            pulse, high_near, hot_near, hot_list, list_places, inverse, base = call(
                prepare_own,
                (
                    PULSE,
                    shape(ROWS, 128, kind=I32),
                    shape(CONTACTS, WIDE, kind=BF16),
                    shape(LISTED, WIDE, kind=BF16),
                    shape(16, 128, kind=I32),
                    PULSE,
                    shape(6, BODY),
                ),
                (LEFT_OWN,),
                near_values, owner, radius, faces, corners, base_rows,
            )
        else:
            (pulse,) = call(
                scatter_near, (PULSE,), (LEFT_OWN,), near_values, high_near, hot_near
            )
        from_left, from_right = along_gy(from_up, from_down, left, right)
        (own,) = call(
            scatter_far, (PULSE,), (LEFT_OWN, left_list(4)),
            flags, far_values, high_far, hot_far, pulse, list_places, hot_list, from_up, from_down,
        )
        fixed = (flags, own, inverse, base, list_places, hot_list, from_left, from_right)
        if number == SWEEPS:
            (velocity,) = call(
                settle_last, (shape(6 * OWN_TILES, 128),), (left_list(5),), *fixed
            )
            break
        velocity, up, down = call(settle, (PULSE,) + GX_SENDS, (left_list(5),), *fixed)
        from_up, from_down = along_gx(up, down)
        near, left, right = call(
            gather_near, (shape(6 * ROWS, 128),) + FACES, (), velocity, places, list_places
        )
        from_left, from_right = along_gy(from_up, from_down, left, right)
        (far,) = call(
            gather_far, (shape(6 * ROWS, 128),), (), flags, velocity, places, from_up, from_down
        )
        impulse, near_values, far_values, up, down, left, right = call(
            sweep, (shape(IMPULSE_ROWS, 128), VALUES, VALUES) + GX_SENDS + FACES, (LEFT_GHOST,),
            flags, near, far, table, places, high_far, hot_far, impulse, from_left, from_right,
        )
    return velocity.reshape(1, 1, 6, BODY), impulse.reshape(1, 1, 3, CONTACTS)

def solution(mesh):
    in_specs = (
        P("gx", "gy", None, None),
        P("gx", "gy", None),
        P("gx", "gy", None, None),
        P("gx", "gy", None, None),
        P("gx", "gy", None),
        P("gx", "gy", None),
        P("gx", "gy", None, None),
        P("gx", "gy", None, None),
        P("gx", "gy", None),
        P("gx", "gy", None),
        P("gx", "gy", None, None),
    )
    out_specs = (P("gx", "gy", None, None), P("gx", "gy", None, None))
    return jax.shard_map(shards, mesh=mesh, in_specs=in_specs, out_specs=out_specs, check_vma=False)
```

```python
import jax
import jax.numpy as jnp
from jax import lax
from jax.experimental import pallas as pl
from jax.experimental.pallas import tpu as pltpu
from jax.sharding import PartitionSpec as P

SWEEPS = 4
RELAX = 0.25
SMALLEST = 1e-20

BODY = 2048
FACE = 256
CORNER = 32
CONTACTS = 4096
ROWS = CONTACTS // 128
LISTED = 4 * FACE + 4 * CORNER
LIST_ROWS = LISTED // 128
OWN_TILES = BODY // 128
WIDE = 256
OWN_WIDE = BODY // WIDE
GHOST_WIDE = 6
IMPULSE_ROWS = 3 * ROWS
MESSAGE = FACE + 128

F32 = jnp.float32
BF16 = jnp.bfloat16
I32 = jnp.int32

PLANES = (
    "n0", "n1", "n2", "a0", "a1", "b0", "b1", "b2",
    "arm0", "arm1", "relax", "mu", "bias",
)
PLANE = {name: place for place, name in enumerate(PLANES)}


def lanes_of(table, lane):
    numbers = lax.GatherDimensionNumbers(
        offset_dims=(),
        collapsed_slice_dims=(1,),
        start_index_map=(1,),
        operand_batching_dims=(0,),
        start_indices_batching_dims=(0,),
    )
    return lax.gather(
        table, lane[..., None], numbers, (1, 1),
        mode=lax.GatherScatterMode.PROMISE_IN_BOUNDS,
    )


def iota(shape, dim):
    return lax.broadcasted_iota(I32, shape, dim)


def halves(values):
    high = values.astype(BF16).astype(F32)
    return high, values - high


def plane(ref, number):
    return ref[number * ROWS:(number + 1) * ROWS, :]


def spread(ref, high_row, parts, blocks, column):
    picks = [high_row == block for block in blocks]
    for part, value in enumerate(parts):
        zero = jnp.zeros_like(value)
        for pair in range(len(blocks) // 2):
            both = jnp.concatenate(
                [
                    jnp.where(picks[2 * pair], value, zero),
                    jnp.where(picks[2 * pair + 1], value, zero),
                ],
                axis=0,
            )
            start = part * len(blocks) * 8 + pair * 16
            ref[start:start + 16, column:column + 128] = both.astype(BF16)


OWN_BLOCKS = tuple(range(OWN_WIDE))
GHOST_BLOCKS = tuple(range(OWN_WIDE, OWN_WIDE + GHOST_WIDE))


def lane_hot(ref, low, rows):
    turned = jnp.transpose(low)
    along = iota((128, WIDE), 1)
    for row in range(rows):
        hot = jnp.broadcast_to(turned[:, row:row + 1], (128, WIDE)) == along
        ref[row * 128:(row + 1) * 128, :] = jnp.where(hot, 1.0, 0.0).astype(BF16)


def product(left, hot, blocks):
    total = jnp.dot(left[...], hot, preferred_element_type=F32)
    return total[:blocks * 8] + total[blocks * 8:]


def end_pulses(impulse, table, near_out, far_out):
    p0, p1, p2 = impulse
    get = lambda name: plane(table, PLANE[name])
    a0, a1 = get("a0"), get("a1")
    b0, b1, b2 = get("b0"), get("b1"), get("b2")
    force = (
        p0 * get("n0") + p1 * a0 + p2 * b0,
        p0 * get("n1") + p1 * a1 + p2 * b1,
        p0 * get("n2") + p2 * b2,
    )
    twist = (p1 * b0 - p2 * a0, p1 * b1 - p2 * a1, p1 * b2)
    arm0, arm1 = -get("arm0"), -get("arm1")
    for comp in range(3):
        near_out[pl.ds(comp, ROWS, stride=8), :] = force[comp]
        far_out[pl.ds(comp, ROWS, stride=8), :] = -force[comp]
        near_out[pl.ds(comp + 3, ROWS, stride=8), :] = arm0 * twist[comp]
        far_out[pl.ds(comp + 3, ROWS, stride=8), :] = arm1 * twist[comp]
    for comp in (6, 7):
        near_out[pl.ds(comp, ROWS, stride=8), :] = jnp.zeros((ROWS, 128), F32)
        far_out[pl.ds(comp, ROWS, stride=8), :] = jnp.zeros((ROWS, 128), F32)


def spread_rows(left, values, high, blocks):
    for row in range(ROWS):
        value = values[row * 8:(row + 1) * 8, :]
        spread(left, high[row:row + 1, :], halves(value), blocks, row * 128)


def ghost_pulses(flags, far, high_far, hot_far, gx_sends, gy_faces, left_ghost):
    spread_rows(left_ghost, far, high_far, GHOST_BLOCKS)
    total = product(left_ghost, hot_far[...], GHOST_WIDE)
    ghost = [total[block * 8:block * 8 + 8] for block in range(5)]
    send_gx(flags, ghost[0], ghost[1], ghost[4][:, :128], gx_sends)
    send_gy(flags, ghost[2], ghost[3], gy_faces)


def flag(flags, number, width=128):
    return jnp.broadcast_to(flags[number:number + 1, :1] > 0, (8, width))


def send_gx(flags, face0, face1, corners, sends):
    first, second = sends
    slot = iota((8, 128), 1) // CORNER
    to_down = (slot == 0) | (slot == 2)
    up = jnp.where(to_down | ~flag(flags, 0), 0.0, corners)
    down = jnp.where(to_down & flag(flags, 1), corners, 0.0)
    even = flag(flags, 5)
    wide = flag(flags, 5, FACE)
    first[:, :FACE] = jnp.where(wide, face1, face0)
    first[:, FACE:] = jnp.where(even, down, up)
    second[:, :FACE] = jnp.where(wide, face0, face1)
    second[:, FACE:] = jnp.where(even, up, down)


def send_gy(flags, face2, face3, faces):
    wide = flag(flags, 6, FACE)
    faces[0][...] = jnp.where(wide, face3, face2)
    faces[1][...] = jnp.where(wide, face2, face3)


def prepare(
    flags, angles_in, arms_in, mu_in, bias_in, impulse_in, owner_in, other_in,
    radius_in, faces_in, corners_in, base_in,
    table, places, high_far, impulse, hot_far, near_values, far_values,
    gx_first, gx_second, gy_first, gy_second,
    owner, radius, faces, corners, base,
    angles, arms, mu, bias, other, flat, left_ghost, sems,
):
    copies = [
        pltpu.make_async_copy(source, target, sems.at[number])
        for number, (source, target) in enumerate((
            (other_in, other), (angles_in, angles), (arms_in, arms), (mu_in, mu),
            (bias_in, bias), (impulse_in, impulse), (owner_in, owner), (radius_in, radius),
            (faces_in, faces), (corners_in, corners), (base_in, base),
        ))
    ]
    for copy in copies:
        copy.start()
    copies[0].wait()
    far_id = other[...]
    extra = far_id - (BODY + 4 * FACE)
    block = extra >> 5
    slot = ((block & 1) << 1) | (block >> 1)
    in_block = extra & (CORNER - 1)
    is_corner = extra >= 0
    places[2 * ROWS:3 * ROWS, :] = far_id >> 7
    places[3 * ROWS:, :] = jnp.where(is_corner, slot * CORNER + in_block, far_id & 127)
    high_far[...] = far_id >> 8
    lane_hot(
        hot_far, jnp.where(is_corner, (3 - slot) * CORNER + in_block, far_id & 255), ROWS
    )
    for copy in copies[1:]:
        copy.wait()
    near_id = owner[...]
    places[:ROWS, :] = near_id >> 7
    places[ROWS:2 * ROWS, :] = near_id & 127
    for row in range(ROWS):
        cut = slice(row * 128, (row + 1) * 128)
        flat[pl.ds(row, 2, stride=ROWS), :] = angles[:, cut]
        flat[pl.ds(2 * ROWS + row, 2, stride=ROWS), :] = arms[:, cut]
    polar, azim = plane(flat, 0), plane(flat, 1)
    arm0, arm1 = plane(flat, 2), plane(flat, 3)
    cos_polar, sin_polar = jnp.cos(polar), jnp.sin(polar)
    cos_azim, sin_azim = jnp.cos(azim), jnp.sin(azim)
    cubed0 = arm0 * arm0 * arm0
    cubed1 = arm1 * arm1 * arm1
    values = {
        "n0": cos_polar * cos_azim, "n1": cos_polar * sin_azim, "n2": sin_polar,
        "a0": -sin_azim, "a1": cos_azim,
        "b0": -sin_polar * cos_azim, "b1": -sin_polar * sin_azim, "b2": cos_polar,
        "arm0": arm0, "arm1": arm1,
        "relax": RELAX / (1.0 / cubed0 + 1.0 / cubed1),
        "mu": mu[...], "bias": bias[...],
    }
    for name, value in values.items():
        number = PLANE[name]
        table[number * ROWS:(number + 1) * ROWS, :] = value
    end_pulses([plane(impulse, comp) for comp in range(3)], table, near_values, far_values)
    ghost_pulses(
        flags, far_values, high_far, hot_far, (gx_first, gx_second), (gy_first, gy_second), left_ghost
    )


def prepare_own(
    near_values, owner, radius, faces, corners, base_rows,
    pulse, high_near, hot_near, hot_list, list_places, inverse, base,
    left_near,
):
    near_id = owner[...]
    high_near[...] = near_id >> 8
    lane_hot(hot_near, near_id & 255, ROWS)
    for number in range(4):
        for part in range(2):
            row = number * 2 + part
            list_places[row:row + 1, :] = faces[number:number + 1, part * 128:(part + 1) * 128]
    for place, number in enumerate((0, 2, 1, 3)):
        list_places[8:9, place * CORNER:(place + 1) * CORNER] = corners[number:number + 1, :]
    for place, number in enumerate((3, 1, 2, 0)):
        list_places[9:10, place * CORNER:(place + 1) * CORNER] = corners[number:number + 1, :]
    list_places[10:, :] = jnp.zeros((6, 128), I32)
    lane_hot(hot_list, list_places[...] & 255, LIST_ROWS)

    size = radius[...]
    cubed = size * size * size
    linear = 1.0 / cubed
    angular = 2.5 / (cubed * size * size)
    inverse[...] = jnp.where(iota((8, BODY), 0) < 3, linear, angular)
    for tile in range(OWN_TILES):
        base[:, tile * 128:(tile + 1) * 128] = base_rows[pl.ds(tile, 6, stride=OWN_TILES), :]
    scatter_near(near_values, high_near, hot_near, pulse, left_near)


def store_blocks(pulse, total):
    for block in range(OWN_WIDE):
        pulse[:, block * WIDE:(block + 1) * WIDE] = total[block * 8:block * 8 + 8]


def scatter_near(values, high_near, hot_near, pulse, left_near):
    spread_rows(left_near, values, high_near, OWN_BLOCKS)
    store_blocks(pulse, product(left_near, hot_near[...], OWN_WIDE))


def masked(flags, number, value):
    return jnp.where(flags[number:number + 1, :] > 0, value, jnp.zeros_like(value))


def gx_tiles(flags, first, second):
    tiles = []
    for part in range(2):
        cut = slice(part * 128, (part + 1) * 128)
        one, two = first[:, cut], second[:, cut]
        tiles.append((jnp.where(flag(flags, 5), one, two), jnp.where(flag(flags, 5), two, one)))
    up, down = zip(*tiles)
    return [masked(flags, 0, tile) for tile in up] + [masked(flags, 1, tile) for tile in down]


def gy_tiles(flags, first, second):
    tiles = []
    for part in range(2):
        cut = slice(part * 128, (part + 1) * 128)
        one, two = first[:, cut], second[:, cut]
        tiles.append((jnp.where(flag(flags, 6), one, two), jnp.where(flag(flags, 6), two, one)))
    left, right = zip(*tiles)
    corners = jnp.where(flags[7:8, :] > 0, first[:, FACE:], second[:, FACE:])
    return (
        [masked(flags, 2, tile) for tile in left] + [masked(flags, 3, tile) for tile in right]
        + [masked(flags, 4, corners)]
    )


def list_product(left_list, tiles, list_places, hot, first):
    for row, tile in enumerate(tiles):
        high_row = list_places[first + row:first + row + 1, :] >> 8
        spread(left_list, high_row, halves(tile), OWN_BLOCKS, row * 128)
    rows = slice(first * 128, (first + len(tiles)) * 128)
    return product(left_list, hot[rows, :], OWN_WIDE)


def scatter_far(
    flags, values, high_far, hot_far, near_pulse, list_places, hot_list, from_up, from_down,
    pulse, left_far, left_list,
):
    spread_rows(left_far, values, high_far, OWN_BLOCKS)
    total = product(left_far, hot_far[...], OWN_WIDE)
    total = total + list_product(
        left_list, gx_tiles(flags, from_up, from_down), list_places, hot_list, 0
    )
    for block in range(OWN_WIDE):
        cut = slice(block * WIDE, (block + 1) * WIDE)
        pulse[:, cut] = near_pulse[:, cut] + total[block * 8:block * 8 + 8]


def settled(flags, own, inverse, base, list_places, hot_list, from_left, from_right, left_list):
    added = list_product(
        left_list, gy_tiles(flags, from_left, from_right), list_places, hot_list, 4
    )
    blocks = []
    for block in range(OWN_WIDE):
        cut = slice(block * WIDE, (block + 1) * WIDE)
        total = own[:6, cut] + added[block * 8:block * 8 + 6]
        blocks.append(base[:, cut] + inverse[:6, cut] * total)
    return blocks


def listed(velocity, list_places, row):
    entry = jnp.broadcast_to(list_places[row:row + 1, :], (8, 128))
    tile_id, lane = entry >> 7, entry & 127
    total = jnp.zeros((8, 128), F32)
    for tile in range(OWN_TILES):
        table = velocity[:, tile * 128:(tile + 1) * 128]
        total = jnp.where(tile_id == tile, lanes_of(table, lane), total)
    return total


def settle(
    flags, own, inverse, base, list_places, hot_list, from_left, from_right,
    velocity, gx_first, gx_second, left_list,
):
    blocks = settled(
        flags, own, inverse, base, list_places, hot_list, from_left, from_right, left_list
    )
    zero = jnp.zeros((2, WIDE), F32)
    for block, value in enumerate(blocks):
        velocity[:, block * WIDE:(block + 1) * WIDE] = jnp.concatenate([value, zero], axis=0)
    found = [listed(velocity, list_places, row) for row in (0, 1, 2, 3, 9)]
    face = [jnp.concatenate(found[2 * k:2 * k + 2], axis=1) for k in range(2)]
    send_gx(flags, *face, found[4], (gx_first, gx_second))


def settle_last(
    flags, own, inverse, base, list_places, hot_list, from_left, from_right,
    velocity, left_list,
):
    blocks = settled(
        flags, own, inverse, base, list_places, hot_list, from_left, from_right, left_list
    )
    for block, value in enumerate(blocks):
        for part in range(2):
            tile = 2 * block + part
            velocity[pl.ds(tile, 6, stride=OWN_TILES), :] = value[:, part * 128:(part + 1) * 128]


def pick(tables, tile_id, lane, firsts, totals):
    for tile, table in zip(firsts, tables):
        here = tile_id == tile
        for comp in range(6):
            row = jnp.broadcast_to(table[comp:comp + 1, :], (ROWS, 128))
            totals[comp] = jnp.where(here, lanes_of(row, lane), totals[comp])
    return totals


def own_tables(velocity):
    return [velocity[:, tile * 128:(tile + 1) * 128] for tile in range(OWN_TILES)]


def blank():
    return [jnp.zeros((ROWS, 128), F32) for _ in range(6)]


def gather_near(flags, velocity, places, list_places, near, gy_first, gy_second):
    tiles = [listed(velocity, list_places, row) for row in range(4, 8)]
    send_gy(
        flags, jnp.concatenate(tiles[:2], axis=1), jnp.concatenate(tiles[2:], axis=1),
        (gy_first, gy_second),
    )
    found = pick(
        own_tables(velocity), places[:ROWS, :], places[ROWS:2 * ROWS, :], range(OWN_TILES), blank()
    )
    for comp in range(6):
        near[comp * ROWS:(comp + 1) * ROWS, :] = found[comp]


def gather_far(flags, velocity, places, from_up, from_down, far):
    found = pick(
        own_tables(velocity) + gx_tiles(flags, from_up, from_down),
        places[2 * ROWS:3 * ROWS, :], places[3 * ROWS:, :], range(OWN_TILES + 4), blank(),
    )
    for comp in range(6):
        far[comp * ROWS:(comp + 1) * ROWS, :] = found[comp]


def sweep(
    flags, near_ref, far_ref, table, places, high_far, hot_far, impulse, from_left, from_right,
    impulse_out, near_values, far_values, gx_first, gx_second, gy_first, gy_second, left_ghost,
):
    near = [plane(near_ref, comp) for comp in range(6)]
    far = pick(
        gy_tiles(flags, from_left, from_right),
        places[2 * ROWS:3 * ROWS, :], places[3 * ROWS:, :],
        range(OWN_TILES + 4, OWN_TILES + 9), [plane(far_ref, comp) for comp in range(6)],
    )
    get = lambda name: plane(table, PLANE[name])
    n0, n1, n2 = get("n0"), get("n1"), get("n2")
    a0, a1 = get("a0"), get("a1")
    b0, b1, b2 = get("b0"), get("b1"), get("b2")
    arm0, arm1, relax, mu = get("arm0"), get("arm1"), get("relax"), get("mu")
    w0, w1, w2 = [near[c] - far[c] for c in range(3)]
    s0, s1, s2 = [arm0 * near[c] + arm1 * far[c] for c in range(3, 6)]
    rate_n = n0 * w0 + n1 * w1 + n2 * w2
    rate_a = (a0 * w0 + a1 * w1) - (b0 * s0 + b1 * s1 + b2 * s2)
    rate_b = (b0 * w0 + b1 * w1 + b2 * w2) + (a0 * s0 + a1 * s1)
    trial_n = plane(impulse, 0) - relax * (rate_n + get("bias"))
    trial_a = plane(impulse, 1) - relax * rate_a
    trial_b = plane(impulse, 2) - relax * rate_b
    length = jnp.sqrt(trial_a * trial_a + trial_b * trial_b)
    inside = length <= mu * trial_n
    dead = mu * length <= -trial_n
    level = (trial_n + mu * length) / (1.0 + mu * mu)
    factor = mu * level / jnp.maximum(length, SMALLEST)
    choose = lambda kept, cone: jnp.where(inside, kept, jnp.where(dead, 0.0, cone))
    fresh = [
        choose(trial_n, level), choose(trial_a, factor * trial_a), choose(trial_b, factor * trial_b)
    ]
    for comp in range(3):
        impulse_out[comp * ROWS:(comp + 1) * ROWS, :] = fresh[comp]
    end_pulses(fresh, table, near_values, far_values)
    ghost_pulses(
        flags, far_values, high_far, hot_far, (gx_first, gx_second), (gy_first, gy_second), left_ghost
    )


def shape(*dims, kind=F32):
    return jax.ShapeDtypeStruct(dims, kind)


FACES = (shape(8, FACE), shape(8, FACE))
GX_SENDS = (shape(8, MESSAGE), shape(8, MESSAGE))
VALUES = shape(8 * ROWS, 128)
PULSE = shape(8, BODY)
LEFT_OWN = pltpu.VMEM((2 * OWN_WIDE * 8, CONTACTS), BF16)
LEFT_GHOST = pltpu.VMEM((2 * GHOST_WIDE * 8, CONTACTS), BF16)


def left_list(tiles):
    return pltpu.VMEM((2 * OWN_WIDE * 8, tiles * 128), BF16)


def call(body, outs, scratch, *operands, specs=None):
    vmem = pl.BlockSpec(memory_space=pltpu.VMEM)
    return pl.pallas_call(
        body,
        out_shape=outs,
        in_specs=specs or [vmem] * len(operands),
        out_specs=[vmem] * len(outs),
        scratch_shapes=scratch,
        compiler_params=pltpu.CompilerParams(vmem_limit_bytes=10 * 1024 * 1024),
    )(*operands)


def loop(value, back, lines, place):
    count, length = lines
    pairs = []
    for line in range(0, count, 2):
        ring = [place(line, step) for step in range(length)]
        ring += [place(line + 1, step) for step in reversed(range(length))]
        for here, there in zip(ring, ring[1:] + ring[:1]):
            pairs.append((there, here) if back else (here, there))
    return lax.ppermute(value, ("gx", "gy"), pairs)


def along_gx(first, second):
    rows, columns = lax.axis_size("gx"), lax.axis_size("gy")
    place = lambda line, step: step * columns + line
    lines = (columns, rows)
    return loop(first, False, lines, place), loop(second, True, lines, place)


def along_gy(got_first, got_second, face_first, face_second):
    rows, columns = lax.axis_size("gx"), lax.axis_size("gy")
    corners = got_first[:, FACE:] + got_second[:, FACE:]
    first = jnp.concatenate([face_first, corners], axis=1)
    second = jnp.concatenate([face_second, corners], axis=1)
    place = lambda line, step: line * columns + step
    lines = (rows, columns)
    return loop(first, False, lines, place), loop(second, True, lines, place)


def presence():
    row_at, row_count = lax.axis_index("gx"), lax.axis_size("gx")
    col_at, col_count = lax.axis_index("gy"), lax.axis_size("gy")
    row, slot = iota((8, 128), 0), iota((8, 128), 1) // CORNER
    above = (row == 0) | ((row == 4) & ((slot == 0) | (slot == 2)))
    below = (row == 1) | ((row == 4) & ((slot == 1) | (slot == 3)))
    before = (row == 2) | ((row == 4) & (slot < 2))
    after = (row == 3) | ((row == 4) & (slot >= 2))
    odd_row, odd_col = lax.rem(row_at, 2), lax.rem(col_at, 2)
    off = (
        (above & (row_at == 0)) | (below & (row_at == row_count - 1))
        | (before & (col_at == 0)) | (after & (col_at == col_count - 1))
        | ((row == 5) & (odd_col == 1)) | ((row == 6) & (odd_row == 1))
        | ((row == 7) & ((slot >> 1) != odd_row))
    )
    return jnp.where(off, 0.0, 1.0)


def shards(
    free_velocity, body_radius, face_lists, corner_lists, owner_body, other_body,
    contact_angles, contact_arms, friction, approach, start_impulse,
):
    flags = presence()
    in_rows = lambda value: value[0, 0].reshape(-1, 128)
    dma = pltpu.SemaphoreType.DMA
    raw = [
        pltpu.with_memory_space_constraint(value, pltpu.HBM)
        for value in (
            contact_angles[0, 0], contact_arms[0, 0], in_rows(friction), in_rows(approach),
            in_rows(start_impulse), in_rows(owner_body), in_rows(other_body),
            body_radius[0], face_lists[0, 0], corner_lists[0, 0], in_rows(free_velocity),
        )
    ]
    (
        table, places, high_far, impulse, hot_far, near_values, far_values,
        gx_first, gx_second, gy_first, gy_second, owner, radius, faces, corners, base_rows,
    ) = call(
        prepare,
        (
            shape(len(PLANES) * ROWS, 128),
            shape(4 * ROWS, 128, kind=I32),
            shape(ROWS, 128, kind=I32),
            shape(IMPULSE_ROWS, 128),
            shape(CONTACTS, WIDE, kind=BF16),
            VALUES, VALUES,
        ) + GX_SENDS + FACES + (
            shape(ROWS, 128, kind=I32),
            shape(1, BODY),
            shape(4, FACE, kind=I32),
            shape(4, CORNER, kind=I32),
            shape(6 * OWN_TILES, 128),
        ),
        (
            pltpu.VMEM((2, CONTACTS), F32),
            pltpu.VMEM((2, CONTACTS), F32),
            pltpu.VMEM((ROWS, 128), F32),
            pltpu.VMEM((ROWS, 128), F32),
            pltpu.VMEM((ROWS, 128), I32),
            pltpu.VMEM((4 * ROWS, 128), F32),
            LEFT_GHOST,
            dma((11,)),
        ),
        flags, *raw,
        specs=[pl.BlockSpec(memory_space=pltpu.VMEM)]
        + [pl.BlockSpec(memory_space=pltpu.HBM)] * len(raw),
    )
    for number in range(SWEEPS + 1):
        got = along_gx(gx_first, gx_second)
        if number == 0:
            pulse, high_near, hot_near, hot_list, list_places, inverse, base = call(
                prepare_own,
                (
                    PULSE,
                    shape(ROWS, 128, kind=I32),
                    shape(CONTACTS, WIDE, kind=BF16),
                    shape(LISTED, WIDE, kind=BF16),
                    shape(16, 128, kind=I32),
                    PULSE,
                    shape(6, BODY),
                ),
                (LEFT_OWN,),
                near_values, owner, radius, faces, corners, base_rows,
            )
        else:
            (pulse,) = call(
                scatter_near, (PULSE,), (LEFT_OWN,), near_values, high_near, hot_near
            )
        got_gy = along_gy(*got, gy_first, gy_second)
        (own,) = call(
            scatter_far, (PULSE,), (LEFT_OWN, left_list(4)),
            flags, far_values, high_far, hot_far, pulse, list_places, hot_list, *got,
        )
        fixed = (flags, own, inverse, base, list_places, hot_list, *got_gy)
        if number == SWEEPS:
            (velocity,) = call(
                settle_last, (shape(6 * OWN_TILES, 128),), (left_list(5),), *fixed
            )
            break
        velocity, gx_first, gx_second = call(
            settle, (PULSE,) + GX_SENDS, (left_list(5),), *fixed
        )
        got = along_gx(gx_first, gx_second)
        near, gy_first, gy_second = call(
            gather_near, (shape(6 * ROWS, 128),) + FACES, (), flags, velocity, places, list_places
        )
        got_gy = along_gy(*got, gy_first, gy_second)
        (far,) = call(
            gather_far, (shape(6 * ROWS, 128),), (), flags, velocity, places, *got
        )
        impulse, near_values, far_values, gx_first, gx_second, gy_first, gy_second = call(
            sweep, (shape(IMPULSE_ROWS, 128), VALUES, VALUES) + GX_SENDS + FACES, (LEFT_GHOST,),
            flags, near, far, table, places, high_far, hot_far, impulse, *got_gy,
        )
    return velocity.reshape(1, 1, 6, BODY), impulse.reshape(1, 1, 3, CONTACTS)

def solution(mesh):
    in_specs = (
        P("gx", "gy", None, None),
        P("gx", "gy", None),
        P("gx", "gy", None, None),
        P("gx", "gy", None, None),
        P("gx", "gy", None),
        P("gx", "gy", None),
        P("gx", "gy", None, None),
        P("gx", "gy", None, None),
        P("gx", "gy", None),
        P("gx", "gy", None),
        P("gx", "gy", None, None),
    )
    out_specs = (P("gx", "gy", None, None), P("gx", "gy", None, None))
    return jax.shard_map(shards, mesh=mesh, in_specs=in_specs, out_specs=out_specs, check_vma=False)
```

```python
import jax
import jax.numpy as jnp
from jax import lax
from jax.experimental import pallas as pl
from jax.experimental.pallas import tpu as pltpu
from jax.sharding import PartitionSpec as P

SWEEPS = 4
TURN = 1
RELAX = 0.25
SMALLEST = 1e-20

BODY = 2048
FACE = 256
CORNER = 32
CONTACTS = 4096
ROWS = CONTACTS // 128
LISTED = 4 * FACE + 4 * CORNER
LIST_ROWS = LISTED // 128
OWN_TILES = BODY // 128
WIDE = 256
OWN_WIDE = BODY // WIDE
GHOST_WIDE = 6
IMPULSE_ROWS = 3 * ROWS
MESSAGE = FACE + 128

F32 = jnp.float32
BF16 = jnp.bfloat16
I32 = jnp.int32

PLANES = (
    "n0", "n1", "n2", "a0", "a1", "b0", "b1", "b2",
    "arm0", "arm1", "relax", "mu", "bias",
)
PLANE = {name: place for place, name in enumerate(PLANES)}


def lanes_of(table, lane):
    numbers = lax.GatherDimensionNumbers(
        offset_dims=(),
        collapsed_slice_dims=(1,),
        start_index_map=(1,),
        operand_batching_dims=(0,),
        start_indices_batching_dims=(0,),
    )
    return lax.gather(
        table, lane[..., None], numbers, (1, 1),
        mode=lax.GatherScatterMode.PROMISE_IN_BOUNDS,
    )


def iota(shape, dim):
    return lax.broadcasted_iota(I32, shape, dim)


def halves(values):
    high = values.astype(BF16).astype(F32)
    return high, values - high


def plane(ref, number):
    return ref[number * ROWS:(number + 1) * ROWS, :]


def spread(ref, high_row, parts, blocks, column):
    picks = [high_row == block for block in blocks]
    for part, value in enumerate(parts):
        zero = jnp.zeros_like(value)
        for pair in range(len(blocks) // 2):
            both = jnp.concatenate(
                [
                    jnp.where(picks[2 * pair], value, zero),
                    jnp.where(picks[2 * pair + 1], value, zero),
                ],
                axis=0,
            )
            start = part * len(blocks) * 8 + pair * 16
            ref[start:start + 16, column:column + 128] = both.astype(BF16)


OWN_BLOCKS = tuple(range(OWN_WIDE))
GHOST_BLOCKS = tuple(range(OWN_WIDE, OWN_WIDE + GHOST_WIDE))


def lane_hot(ref, low, rows):
    turned = jnp.transpose(low)
    along = iota((128, WIDE), 1)
    for row in range(rows):
        hot = jnp.broadcast_to(turned[:, row:row + 1], (128, WIDE)) == along
        ref[row * 128:(row + 1) * 128, :] = jnp.where(hot, 1.0, 0.0).astype(BF16)


def product(left, hot, blocks):
    total = jnp.dot(left[...], hot, preferred_element_type=F32)
    return total[:blocks * 8] + total[blocks * 8:]


def end_pulses(impulse, table, near_out, far_out):
    p0, p1, p2 = impulse
    get = lambda name: plane(table, PLANE[name])
    a0, a1 = get("a0"), get("a1")
    b0, b1, b2 = get("b0"), get("b1"), get("b2")
    force = (
        p0 * get("n0") + p1 * a0 + p2 * b0,
        p0 * get("n1") + p1 * a1 + p2 * b1,
        p0 * get("n2") + p2 * b2,
    )
    twist = (p1 * b0 - p2 * a0, p1 * b1 - p2 * a1, p1 * b2)
    arm0, arm1 = -get("arm0"), -get("arm1")
    for comp in range(3):
        near_out[pl.ds(comp, ROWS, stride=8), :] = force[comp]
        far_out[pl.ds(comp, ROWS, stride=8), :] = -force[comp]
        near_out[pl.ds(comp + 3, ROWS, stride=8), :] = arm0 * twist[comp]
        far_out[pl.ds(comp + 3, ROWS, stride=8), :] = arm1 * twist[comp]
    for comp in (6, 7):
        near_out[pl.ds(comp, ROWS, stride=8), :] = jnp.zeros((ROWS, 128), F32)
        far_out[pl.ds(comp, ROWS, stride=8), :] = jnp.zeros((ROWS, 128), F32)


def spread_rows(left, values, high, blocks):
    for row in range(ROWS):
        value = values[row * 8:(row + 1) * 8, :]
        spread(left, high[row:row + 1, :], halves(value), blocks, row * 128)


def ghost_pulses(flags, far, high_far, hot_far, gx_sends, gy_faces, left_ghost):
    spread_rows(left_ghost, far, high_far, GHOST_BLOCKS)
    total = product(left_ghost, hot_far[...], GHOST_WIDE)
    ghost = [total[block * 8:block * 8 + 8] for block in range(5)]
    send_gx(flags, ghost[0], ghost[1], ghost[4][:, :128], gx_sends)
    send_gy(flags, ghost[2], ghost[3], gy_faces)


def flag(flags, number, width=128):
    return jnp.broadcast_to(flags[number:number + 1, :1] > 0, (8, width))


def send_gx(flags, face0, face1, corners, sends):
    first, second = sends
    slot = iota((8, 128), 1) // CORNER
    to_down = (slot == 0) | (slot == 2)
    up = jnp.where(to_down | ~flag(flags, 0), 0.0, corners)
    down = jnp.where(to_down & flag(flags, 1), corners, 0.0)
    even = flag(flags, 5)
    wide = flag(flags, 5, FACE)
    first[:, :FACE] = jnp.where(wide, face1, face0)
    first[:, FACE:] = jnp.where(even, down, up)
    second[:, :FACE] = jnp.where(wide, face0, face1)
    second[:, FACE:] = jnp.where(even, up, down)


def send_gy(flags, face2, face3, faces):
    wide = flag(flags, 6, FACE)
    faces[0][...] = jnp.where(wide, face3, face2)
    faces[1][...] = jnp.where(wide, face2, face3)


def prepare(
    flags, angles_in, arms_in, mu_in, bias_in, impulse_in, owner_in, other_in,
    radius_in, faces_in, corners_in, base_in,
    table, places, high_far, impulse, hot_far, near_values, far_values,
    gx_first, gx_second, gy_first, gy_second,
    owner, radius, faces, corners, base,
    angles, arms, mu, bias, other, flat, left_ghost, sems,
):
    copies = [
        pltpu.make_async_copy(source, target, sems.at[number])
        for number, (source, target) in enumerate((
            (other_in, other), (angles_in, angles), (arms_in, arms), (mu_in, mu),
            (bias_in, bias), (impulse_in, impulse), (owner_in, owner), (radius_in, radius),
            (faces_in, faces), (corners_in, corners), (base_in, base),
        ))
    ]
    for copy in copies:
        copy.start()
    copies[0].wait()
    far_id = other[...]
    extra = far_id - (BODY + 4 * FACE)
    block = extra >> 5
    slot = ((block & 1) << 1) | (block >> 1)
    in_block = extra & (CORNER - 1)
    is_corner = extra >= 0
    places[2 * ROWS:3 * ROWS, :] = far_id >> 7
    places[3 * ROWS:, :] = jnp.where(is_corner, slot * CORNER + in_block, far_id & 127)
    high_far[...] = far_id >> 8
    lane_hot(
        hot_far, jnp.where(is_corner, (3 - slot) * CORNER + in_block, far_id & 255), ROWS
    )
    for copy in copies[1:]:
        copy.wait()
    near_id = owner[...]
    places[:ROWS, :] = near_id >> 7
    places[ROWS:2 * ROWS, :] = near_id & 127
    for row in range(ROWS):
        cut = slice(row * 128, (row + 1) * 128)
        flat[pl.ds(row, 2, stride=ROWS), :] = angles[:, cut]
        flat[pl.ds(2 * ROWS + row, 2, stride=ROWS), :] = arms[:, cut]
    polar, azim = plane(flat, 0), plane(flat, 1)
    arm0, arm1 = plane(flat, 2), plane(flat, 3)
    cos_polar, sin_polar = jnp.cos(polar), jnp.sin(polar)
    cos_azim, sin_azim = jnp.cos(azim), jnp.sin(azim)
    cubed0 = arm0 * arm0 * arm0
    cubed1 = arm1 * arm1 * arm1
    values = {
        "n0": cos_polar * cos_azim, "n1": cos_polar * sin_azim, "n2": sin_polar,
        "a0": -sin_azim, "a1": cos_azim,
        "b0": -sin_polar * cos_azim, "b1": -sin_polar * sin_azim, "b2": cos_polar,
        "arm0": arm0, "arm1": arm1,
        "relax": RELAX / (1.0 / cubed0 + 1.0 / cubed1),
        "mu": mu[...], "bias": bias[...],
    }
    for name, value in values.items():
        number = PLANE[name]
        table[number * ROWS:(number + 1) * ROWS, :] = value
    end_pulses([plane(impulse, comp) for comp in range(3)], table, near_values, far_values)
    ghost_pulses(
        flags, far_values, high_far, hot_far, (gx_first, gx_second), (gy_first, gy_second), left_ghost
    )


def prepare_own(
    owner, radius, faces, corners, base_rows,
    high_near, hot_near, hot_list, list_places, inverse, base,
):
    near_id = owner[...]
    high_near[...] = near_id >> 8
    lane_hot(hot_near, near_id & 255, ROWS)
    for number in range(4):
        for part in range(2):
            row = number * 2 + part
            list_places[row:row + 1, :] = faces[number:number + 1, part * 128:(part + 1) * 128]
    for place, number in enumerate((0, 2, 1, 3)):
        list_places[8:9, place * CORNER:(place + 1) * CORNER] = corners[number:number + 1, :]
    for place, number in enumerate((3, 1, 2, 0)):
        list_places[9:10, place * CORNER:(place + 1) * CORNER] = corners[number:number + 1, :]
    list_places[10:, :] = jnp.zeros((6, 128), I32)
    lane_hot(hot_list, list_places[...] & 255, LIST_ROWS)

    size = radius[...]
    cubed = size * size * size
    linear = 1.0 / cubed
    angular = 2.5 / (cubed * size * size)
    inverse[...] = jnp.where(iota((8, BODY), 0) < 3, linear, angular)
    for tile in range(OWN_TILES):
        base[:, tile * 128:(tile + 1) * 128] = base_rows[pl.ds(tile, 6, stride=OWN_TILES), :]


def store_blocks(pulse, total):
    for block in range(OWN_WIDE):
        pulse[:, block * WIDE:(block + 1) * WIDE] = total[block * 8:block * 8 + 8]


def scatter_near(values, high_near, hot_near, pulse, left_near):
    spread_rows(left_near, values, high_near, OWN_BLOCKS)
    store_blocks(pulse, product(left_near, hot_near[...], OWN_WIDE))


def masked(flags, number, value):
    return jnp.where(flags[number:number + 1, :] > 0, value, jnp.zeros_like(value))


def gx_tiles(flags, first, second):
    tiles = []
    for part in range(2):
        cut = slice(part * 128, (part + 1) * 128)
        one, two = first[:, cut], second[:, cut]
        tiles.append((jnp.where(flag(flags, 5), one, two), jnp.where(flag(flags, 5), two, one)))
    up, down = zip(*tiles)
    return [masked(flags, 0, tile) for tile in up] + [masked(flags, 1, tile) for tile in down]


def gy_tiles(flags, first, second):
    tiles = []
    for part in range(2):
        cut = slice(part * 128, (part + 1) * 128)
        one, two = first[:, cut], second[:, cut]
        tiles.append((jnp.where(flag(flags, 6), one, two), jnp.where(flag(flags, 6), two, one)))
    left, right = zip(*tiles)
    corners = jnp.where(flags[7:8, :] > 0, first[:, FACE:], second[:, FACE:])
    return (
        [masked(flags, 2, tile) for tile in left] + [masked(flags, 3, tile) for tile in right]
        + [masked(flags, 4, corners)]
    )


def list_product(left_list, tiles, list_places, hot, first):
    for row, tile in enumerate(tiles):
        high_row = list_places[first + row:first + row + 1, :] >> 8
        spread(left_list, high_row, halves(tile), OWN_BLOCKS, row * 128)
    rows = slice(first * 128, (first + len(tiles)) * 128)
    return product(left_list, hot[rows, :], OWN_WIDE)


def scatter_far(
    flags, values, high_far, hot_far, near_pulse, list_places, hot_list, from_up, from_down,
    pulse, left_far, left_list,
):
    spread_rows(left_far, values, high_far, OWN_BLOCKS)
    total = product(left_far, hot_far[...], OWN_WIDE)
    total = total + list_product(
        left_list, gx_tiles(flags, from_up, from_down), list_places, hot_list, 0
    )
    for block in range(OWN_WIDE):
        cut = slice(block * WIDE, (block + 1) * WIDE)
        pulse[:, cut] = near_pulse[:, cut] + total[block * 8:block * 8 + 8]


def settled(flags, own, inverse, base, list_places, hot_list, from_left, from_right, left_list):
    added = list_product(
        left_list, gy_tiles(flags, from_left, from_right), list_places, hot_list, 4
    )
    blocks = []
    for block in range(OWN_WIDE):
        cut = slice(block * WIDE, (block + 1) * WIDE)
        total = own[:6, cut] + added[block * 8:block * 8 + 6]
        blocks.append(base[:, cut] + inverse[:6, cut] * total)
    return blocks


def listed(velocity, list_places, row):
    entry = jnp.broadcast_to(list_places[row:row + 1, :], (8, 128))
    tile_id, lane = entry >> 7, entry & 127
    total = jnp.zeros((8, 128), F32)
    for tile in range(OWN_TILES):
        table = velocity[:, tile * 128:(tile + 1) * 128]
        total = jnp.where(tile_id == tile, lanes_of(table, lane), total)
    return total


def settle(
    flags, own, inverse, base, list_places, hot_list, from_left, from_right,
    velocity, gx_first, gx_second, left_list,
):
    blocks = settled(
        flags, own, inverse, base, list_places, hot_list, from_left, from_right, left_list
    )
    zero = jnp.zeros((2, WIDE), F32)
    for block, value in enumerate(blocks):
        velocity[:, block * WIDE:(block + 1) * WIDE] = jnp.concatenate([value, zero], axis=0)
    found = [listed(velocity, list_places, row) for row in (0, 1, 2, 3, 9)]
    face = [jnp.concatenate(found[2 * k:2 * k + 2], axis=1) for k in range(2)]
    send_gx(flags, *face, found[4], (gx_first, gx_second))


def settle_last(
    flags, own, inverse, base, list_places, hot_list, from_left, from_right,
    velocity, left_list,
):
    blocks = settled(
        flags, own, inverse, base, list_places, hot_list, from_left, from_right, left_list
    )
    for block, value in enumerate(blocks):
        for part in range(2):
            tile = 2 * block + part
            velocity[pl.ds(tile, 6, stride=OWN_TILES), :] = value[:, part * 128:(part + 1) * 128]


def pick(tables, tile_id, lane, firsts, totals):
    for tile, table in zip(firsts, tables):
        here = tile_id == tile
        for comp in range(6):
            row = jnp.broadcast_to(table[comp:comp + 1, :], (ROWS, 128))
            totals[comp] = jnp.where(here, lanes_of(row, lane), totals[comp])
    return totals


def own_tables(velocity):
    return [velocity[:, tile * 128:(tile + 1) * 128] for tile in range(OWN_TILES)]


def blank():
    return [jnp.zeros((ROWS, 128), F32) for _ in range(6)]


def gather_near(flags, velocity, places, list_places, near, gy_first, gy_second):
    tiles = [listed(velocity, list_places, row) for row in range(4, 8)]
    send_gy(
        flags, jnp.concatenate(tiles[:2], axis=1), jnp.concatenate(tiles[2:], axis=1),
        (gy_first, gy_second),
    )
    found = pick(
        own_tables(velocity), places[:ROWS, :], places[ROWS:2 * ROWS, :], range(OWN_TILES), blank()
    )
    for comp in range(6):
        near[comp * ROWS:(comp + 1) * ROWS, :] = found[comp]


def gather_far(flags, velocity, places, from_up, from_down, far):
    found = pick(
        own_tables(velocity) + gx_tiles(flags, from_up, from_down),
        places[2 * ROWS:3 * ROWS, :], places[3 * ROWS:, :], range(OWN_TILES + 4), blank(),
    )
    for comp in range(6):
        far[comp * ROWS:(comp + 1) * ROWS, :] = found[comp]


def sweep(
    flags, near_ref, far_ref, table, places, high_far, hot_far, impulse, from_left, from_right,
    impulse_out, near_values, far_values, gx_first, gx_second, gy_first, gy_second, left_ghost,
):
    near = [plane(near_ref, comp) for comp in range(6)]
    far = pick(
        gy_tiles(flags, from_left, from_right),
        places[2 * ROWS:3 * ROWS, :], places[3 * ROWS:, :],
        range(OWN_TILES + 4, OWN_TILES + 9), [plane(far_ref, comp) for comp in range(6)],
    )
    get = lambda name: plane(table, PLANE[name])
    n0, n1, n2 = get("n0"), get("n1"), get("n2")
    a0, a1 = get("a0"), get("a1")
    b0, b1, b2 = get("b0"), get("b1"), get("b2")
    arm0, arm1, relax, mu = get("arm0"), get("arm1"), get("relax"), get("mu")
    w0, w1, w2 = [near[c] - far[c] for c in range(3)]
    s0, s1, s2 = [arm0 * near[c] + arm1 * far[c] for c in range(3, 6)]
    rate_n = n0 * w0 + n1 * w1 + n2 * w2
    rate_a = (a0 * w0 + a1 * w1) - (b0 * s0 + b1 * s1 + b2 * s2)
    rate_b = (b0 * w0 + b1 * w1 + b2 * w2) + (a0 * s0 + a1 * s1)
    trial_n = plane(impulse, 0) - relax * (rate_n + get("bias"))
    trial_a = plane(impulse, 1) - relax * rate_a
    trial_b = plane(impulse, 2) - relax * rate_b
    length = jnp.sqrt(trial_a * trial_a + trial_b * trial_b)
    inside = length <= mu * trial_n
    dead = mu * length <= -trial_n
    level = (trial_n + mu * length) / (1.0 + mu * mu)
    factor = mu * level / jnp.maximum(length, SMALLEST)
    choose = lambda kept, cone: jnp.where(inside, kept, jnp.where(dead, 0.0, cone))
    fresh = [
        choose(trial_n, level), choose(trial_a, factor * trial_a), choose(trial_b, factor * trial_b)
    ]
    for comp in range(3):
        impulse_out[comp * ROWS:(comp + 1) * ROWS, :] = fresh[comp]
    end_pulses(fresh, table, near_values, far_values)
    ghost_pulses(
        flags, far_values, high_far, hot_far, (gx_first, gx_second), (gy_first, gy_second), left_ghost
    )


def shape(*dims, kind=F32):
    return jax.ShapeDtypeStruct(dims, kind)


FACES = (shape(8, FACE), shape(8, FACE))
GX_SENDS = (shape(8, MESSAGE), shape(8, MESSAGE))
VALUES = shape(8 * ROWS, 128)
PULSE = shape(8, BODY)
LEFT_OWN = pltpu.VMEM((2 * OWN_WIDE * 8, CONTACTS), BF16)
LEFT_GHOST = pltpu.VMEM((2 * GHOST_WIDE * 8, CONTACTS), BF16)


def left_list(tiles):
    return pltpu.VMEM((2 * OWN_WIDE * 8, tiles * 128), BF16)


def turn_of(step):
    def turn(number, carry):
        for _ in range(TURN):
            carry = tuple(step(number, carry))
        return carry

    return turn


def call(body, outs, scratch, *operands, specs=None, aliases=None):
    vmem = pl.BlockSpec(memory_space=pltpu.VMEM)
    return pl.pallas_call(
        body,
        out_shape=outs,
        in_specs=specs or [vmem] * len(operands),
        out_specs=[vmem] * len(outs),
        scratch_shapes=scratch,
        input_output_aliases=aliases or {},
        compiler_params=pltpu.CompilerParams(vmem_limit_bytes=10 * 1024 * 1024),
    )(*operands)


def loop(value, back, lines, place):
    count, length = lines
    pairs = []
    for line in range(0, count, 2):
        ring = [place(line, step) for step in range(length)]
        ring += [place(line + 1, step) for step in reversed(range(length))]
        for here, there in zip(ring, ring[1:] + ring[:1]):
            pairs.append((there, here) if back else (here, there))
    return lax.ppermute(value, ("gx", "gy"), pairs)


def along_gx(first, second):
    rows, columns = lax.axis_size("gx"), lax.axis_size("gy")
    place = lambda line, step: step * columns + line
    lines = (columns, rows)
    return loop(first, False, lines, place), loop(second, True, lines, place)


def along_gy(got_first, got_second, face_first, face_second):
    rows, columns = lax.axis_size("gx"), lax.axis_size("gy")
    corners = got_first[:, FACE:] + got_second[:, FACE:]
    first = jnp.concatenate([face_first, corners], axis=1)
    second = jnp.concatenate([face_second, corners], axis=1)
    place = lambda line, step: line * columns + step
    lines = (rows, columns)
    return loop(first, False, lines, place), loop(second, True, lines, place)


def presence():
    row_at, row_count = lax.axis_index("gx"), lax.axis_size("gx")
    col_at, col_count = lax.axis_index("gy"), lax.axis_size("gy")
    row, slot = iota((8, 128), 0), iota((8, 128), 1) // CORNER
    above = (row == 0) | ((row == 4) & ((slot == 0) | (slot == 2)))
    below = (row == 1) | ((row == 4) & ((slot == 1) | (slot == 3)))
    before = (row == 2) | ((row == 4) & (slot < 2))
    after = (row == 3) | ((row == 4) & (slot >= 2))
    odd_row, odd_col = lax.rem(row_at, 2), lax.rem(col_at, 2)
    off = (
        (above & (row_at == 0)) | (below & (row_at == row_count - 1))
        | (before & (col_at == 0)) | (after & (col_at == col_count - 1))
        | ((row == 5) & (odd_col == 1)) | ((row == 6) & (odd_row == 1))
        | ((row == 7) & ((slot >> 1) != odd_row))
    )
    return jnp.where(off, 0.0, 1.0)


def shards(
    free_velocity, body_radius, face_lists, corner_lists, owner_body, other_body,
    contact_angles, contact_arms, friction, approach, start_impulse,
):
    flags = presence()
    in_rows = lambda value: value[0, 0].reshape(-1, 128)
    dma = pltpu.SemaphoreType.DMA
    raw = [
        pltpu.with_memory_space_constraint(value, pltpu.HBM)
        for value in (
            contact_angles[0, 0], contact_arms[0, 0], in_rows(friction), in_rows(approach),
            in_rows(start_impulse), in_rows(owner_body), in_rows(other_body),
            body_radius[0], face_lists[0, 0], corner_lists[0, 0], in_rows(free_velocity),
        )
    ]
    (
        table, places, high_far, impulse, hot_far, near_values, far_values,
        gx_first, gx_second, gy_first, gy_second, owner, radius, faces, corners, base_rows,
    ) = call(
        prepare,
        (
            shape(len(PLANES) * ROWS, 128),
            shape(4 * ROWS, 128, kind=I32),
            shape(ROWS, 128, kind=I32),
            shape(IMPULSE_ROWS, 128),
            shape(CONTACTS, WIDE, kind=BF16),
            VALUES, VALUES,
        ) + GX_SENDS + FACES + (
            shape(ROWS, 128, kind=I32),
            shape(1, BODY),
            shape(4, FACE, kind=I32),
            shape(4, CORNER, kind=I32),
            shape(6 * OWN_TILES, 128),
        ),
        (
            pltpu.VMEM((2, CONTACTS), F32),
            pltpu.VMEM((2, CONTACTS), F32),
            pltpu.VMEM((ROWS, 128), F32),
            pltpu.VMEM((ROWS, 128), F32),
            pltpu.VMEM((ROWS, 128), I32),
            pltpu.VMEM((4 * ROWS, 128), F32),
            LEFT_GHOST,
            dma((11,)),
        ),
        flags, *raw,
        specs=[pl.BlockSpec(memory_space=pltpu.VMEM)]
        + [pl.BlockSpec(memory_space=pltpu.HBM)] * len(raw),
    )
    high_near, hot_near, hot_list, list_places, inverse, base = call(
        prepare_own,
        (
            shape(ROWS, 128, kind=I32),
            shape(CONTACTS, WIDE, kind=BF16),
            shape(LISTED, WIDE, kind=BF16),
            shape(16, 128, kind=I32),
            PULSE,
            shape(6, BODY),
        ),
        (),
        owner, radius, faces, corners, base_rows,
    )

    def give_back(near_values, far_values, gx_first, gx_second, gy_first, gy_second):
        got = along_gx(gx_first, gx_second)
        (pulse,) = call(scatter_near, (PULSE,), (LEFT_OWN,), near_values, high_near, hot_near)
        got_gy = along_gy(*got, gy_first, gy_second)
        (own,) = call(
            scatter_far, (PULSE,), (LEFT_OWN, left_list(4)),
            flags, far_values, high_far, hot_far, pulse, list_places, hot_list, *got,
        )
        return (flags, own, inverse, base, list_places, hot_list, *got_gy)

    def one_sweep(number, carry):
        impulse, *sent = carry
        velocity, gx_first, gx_second = call(
            settle, (PULSE,) + GX_SENDS, (left_list(5),), *give_back(*sent)
        )
        got = along_gx(gx_first, gx_second)
        near, gy_first, gy_second = call(
            gather_near, (shape(6 * ROWS, 128),) + FACES, (), flags, velocity, places, list_places
        )
        got_gy = along_gy(*got, gy_first, gy_second)
        (far,) = call(
            gather_far, (shape(6 * ROWS, 128),), (), flags, velocity, places, *got
        )
        return call(
            sweep, (shape(IMPULSE_ROWS, 128), VALUES, VALUES) + GX_SENDS + FACES, (LEFT_GHOST,),
            flags, near, far, table, places, high_far, hot_far, impulse, *got_gy,
            aliases={7: 0},
        )

    carry = (impulse, near_values, far_values, gx_first, gx_second, gy_first, gy_second)
    impulse, *sent = lax.fori_loop(0, SWEEPS // TURN, turn_of(one_sweep), carry)
    (velocity,) = call(
        settle_last, (shape(6 * OWN_TILES, 128),), (left_list(5),), *give_back(*sent)
    )
    return velocity.reshape(1, 1, 6, BODY), impulse.reshape(1, 1, 3, CONTACTS)

def solution(mesh):
    in_specs = (
        P("gx", "gy", None, None),
        P("gx", "gy", None),
        P("gx", "gy", None, None),
        P("gx", "gy", None, None),
        P("gx", "gy", None),
        P("gx", "gy", None),
        P("gx", "gy", None, None),
        P("gx", "gy", None, None),
        P("gx", "gy", None),
        P("gx", "gy", None),
        P("gx", "gy", None, None),
    )
    out_specs = (P("gx", "gy", None, None), P("gx", "gy", None, None))
    return jax.shard_map(shards, mesh=mesh, in_specs=in_specs, out_specs=out_specs, check_vma=False)
```

```python
import jax
import jax.numpy as jnp
from jax import lax
from jax.experimental import pallas as pl
from jax.experimental.pallas import tpu as pltpu
from jax.sharding import PartitionSpec as P

SWEEPS = 4
RELAX = 0.25
SMALLEST = 1e-20

BODY = 2048
FACE = 256
CORNER = 32
CONTACTS = 4096
ROWS = CONTACTS // 128
LISTED = 4 * FACE + 4 * CORNER
LIST_ROWS = LISTED // 128
OWN_TILES = BODY // 128
WIDE = 256
OWN_WIDE = BODY // WIDE
GHOST_WIDE = 6
IMPULSE_ROWS = 3 * ROWS
MESSAGE = FACE + 128
CHUNK = 512
UNROLL = 2

F32 = jnp.float32
BF16 = jnp.bfloat16
I32 = jnp.int32

PLANES = (
    "n0", "n1", "n2", "a0", "a1", "b0", "b1", "b2",
    "arm0", "arm1", "relax", "mu", "bias",
)
PLANE = {name: place for place, name in enumerate(PLANES)}


def lanes_of(table, lane):
    numbers = lax.GatherDimensionNumbers(
        offset_dims=(),
        collapsed_slice_dims=(1,),
        start_index_map=(1,),
        operand_batching_dims=(0,),
        start_indices_batching_dims=(0,),
    )
    return lax.gather(
        table, lane[..., None], numbers, (1, 1),
        mode=lax.GatherScatterMode.PROMISE_IN_BOUNDS,
    )


def iota(shape, dim):
    return lax.broadcasted_iota(I32, shape, dim)


def halves(values):
    high = values.astype(BF16).astype(F32)
    return high, values - high


def plane(ref, number):
    return ref[number * ROWS:(number + 1) * ROWS, :]


def spread(ref, high_row, parts, blocks, column):
    picks = [high_row == block for block in blocks]
    for part, value in enumerate(parts):
        zero = jnp.zeros_like(value)
        for pair in range(len(blocks) // 2):
            both = jnp.concatenate(
                [
                    jnp.where(picks[2 * pair], value, zero),
                    jnp.where(picks[2 * pair + 1], value, zero),
                ],
                axis=0,
            )
            start = part * len(blocks) * 8 + pair * 16
            ref[start:start + 16, pl.ds(column, 128)] = both.astype(BF16)


OWN_BLOCKS = tuple(range(OWN_WIDE))
GHOST_BLOCKS = tuple(range(OWN_WIDE, OWN_WIDE + GHOST_WIDE))


def lane_hot(ref, low, rows):
    turned = jnp.transpose(low)
    along = iota((128, WIDE), 1)
    for row in range(rows):
        hot = jnp.broadcast_to(turned[:, row:row + 1], (128, WIDE)) == along
        ref[row * 128:(row + 1) * 128, :] = jnp.where(hot, 1.0, 0.0).astype(BF16)


def product(left, hot, blocks):
    total = jnp.dot(left[...], hot, preferred_element_type=F32)
    return total[:blocks * 8] + total[blocks * 8:]


def long_product(left, hot, blocks):
    def step(number, total):
        at = pl.multiple_of(number * CHUNK, CHUNK)
        return total + jnp.dot(
            left[:, pl.ds(at, CHUNK)], hot[pl.ds(at, CHUNK), :], preferred_element_type=F32
        )

    total = lax.fori_loop(
        0, CONTACTS // CHUNK, step, jnp.zeros((2 * blocks * 8, WIDE), F32)
    )
    return total[:blocks * 8] + total[blocks * 8:]


def end_pulses(impulse, table, near_out, far_out):
    p0, p1, p2 = impulse
    get = lambda name: plane(table, PLANE[name])
    a0, a1 = get("a0"), get("a1")
    b0, b1, b2 = get("b0"), get("b1"), get("b2")
    force = (
        p0 * get("n0") + p1 * a0 + p2 * b0,
        p0 * get("n1") + p1 * a1 + p2 * b1,
        p0 * get("n2") + p2 * b2,
    )
    twist = (p1 * b0 - p2 * a0, p1 * b1 - p2 * a1, p1 * b2)
    arm0, arm1 = -get("arm0"), -get("arm1")
    for comp in range(3):
        near_out[pl.ds(comp, ROWS, stride=8), :] = force[comp]
        far_out[pl.ds(comp, ROWS, stride=8), :] = -force[comp]
        near_out[pl.ds(comp + 3, ROWS, stride=8), :] = arm0 * twist[comp]
        far_out[pl.ds(comp + 3, ROWS, stride=8), :] = arm1 * twist[comp]
    for comp in (6, 7):
        near_out[pl.ds(comp, ROWS, stride=8), :] = jnp.zeros((ROWS, 128), F32)
        far_out[pl.ds(comp, ROWS, stride=8), :] = jnp.zeros((ROWS, 128), F32)


def spread_rows(left, values, high, blocks):
    def step(group, carry):
        for part in range(UNROLL):
            row = group * UNROLL + part
            value = values[pl.ds(pl.multiple_of(row * 8, 8), 8), :]
            column = pl.multiple_of(row * 128, 128)
            spread(left, high[pl.ds(row, 1), :], halves(value), blocks, column)
        return carry

    lax.fori_loop(0, ROWS // UNROLL, step, 0)


def ghost_pulses(flags, far, high_far, hot_far, gx_sends, gy_faces, left_ghost):
    spread_rows(left_ghost, far, high_far, GHOST_BLOCKS)
    total = long_product(left_ghost, hot_far, GHOST_WIDE)
    ghost = [total[block * 8:block * 8 + 8] for block in range(5)]
    send_gx(flags, ghost[0], ghost[1], ghost[4][:, :128], gx_sends)
    send_gy(flags, ghost[2], ghost[3], gy_faces)


def flag(flags, number, width=128):
    return jnp.broadcast_to(flags[number:number + 1, :1] > 0, (8, width))


def send_gx(flags, face0, face1, corners, sends):
    first, second = sends
    slot = iota((8, 128), 1) // CORNER
    to_down = (slot == 0) | (slot == 2)
    up = jnp.where(to_down | ~flag(flags, 0), 0.0, corners)
    down = jnp.where(to_down & flag(flags, 1), corners, 0.0)
    even = flag(flags, 5)
    wide = flag(flags, 5, FACE)
    first[:, :FACE] = jnp.where(wide, face1, face0)
    first[:, FACE:] = jnp.where(even, down, up)
    second[:, :FACE] = jnp.where(wide, face0, face1)
    second[:, FACE:] = jnp.where(even, up, down)


def send_gy(flags, face2, face3, faces):
    wide = flag(flags, 6, FACE)
    faces[0][...] = jnp.where(wide, face3, face2)
    faces[1][...] = jnp.where(wide, face2, face3)


def prepare(
    flags, angles_in, arms_in, mu_in, bias_in, impulse_in, owner_in, other_in,
    radius_in, faces_in, corners_in, base_in,
    table, places, high_far, impulse, hot_far, near_values, far_values,
    gx_first, gx_second, gy_first, gy_second,
    owner, radius, faces, corners, base,
    angles, arms, mu, bias, other, flat, left_ghost, sems,
):
    copies = [
        pltpu.make_async_copy(source, target, sems.at[number])
        for number, (source, target) in enumerate((
            (other_in, other), (angles_in, angles), (arms_in, arms), (mu_in, mu),
            (bias_in, bias), (impulse_in, impulse), (owner_in, owner), (radius_in, radius),
            (faces_in, faces), (corners_in, corners), (base_in, base),
        ))
    ]
    for copy in copies:
        copy.start()
    copies[0].wait()
    far_id = other[...]
    extra = far_id - (BODY + 4 * FACE)
    block = extra >> 5
    slot = ((block & 1) << 1) | (block >> 1)
    in_block = extra & (CORNER - 1)
    is_corner = extra >= 0
    places[2 * ROWS:3 * ROWS, :] = far_id >> 7
    places[3 * ROWS:, :] = jnp.where(is_corner, slot * CORNER + in_block, far_id & 127)
    high_far[...] = far_id >> 8
    lane_hot(
        hot_far, jnp.where(is_corner, (3 - slot) * CORNER + in_block, far_id & 255), ROWS
    )
    for copy in copies[1:]:
        copy.wait()
    near_id = owner[...]
    places[:ROWS, :] = near_id >> 7
    places[ROWS:2 * ROWS, :] = near_id & 127
    for row in range(ROWS):
        cut = slice(row * 128, (row + 1) * 128)
        flat[pl.ds(row, 2, stride=ROWS), :] = angles[:, cut]
        flat[pl.ds(2 * ROWS + row, 2, stride=ROWS), :] = arms[:, cut]
    polar, azim = plane(flat, 0), plane(flat, 1)
    arm0, arm1 = plane(flat, 2), plane(flat, 3)
    cos_polar, sin_polar = jnp.cos(polar), jnp.sin(polar)
    cos_azim, sin_azim = jnp.cos(azim), jnp.sin(azim)
    cubed0 = arm0 * arm0 * arm0
    cubed1 = arm1 * arm1 * arm1
    values = {
        "n0": cos_polar * cos_azim, "n1": cos_polar * sin_azim, "n2": sin_polar,
        "a0": -sin_azim, "a1": cos_azim,
        "b0": -sin_polar * cos_azim, "b1": -sin_polar * sin_azim, "b2": cos_polar,
        "arm0": arm0, "arm1": arm1,
        "relax": RELAX / (1.0 / cubed0 + 1.0 / cubed1),
        "mu": mu[...], "bias": bias[...],
    }
    for name, value in values.items():
        number = PLANE[name]
        table[number * ROWS:(number + 1) * ROWS, :] = value
    end_pulses([plane(impulse, comp) for comp in range(3)], table, near_values, far_values)
    ghost_pulses(
        flags, far_values, high_far, hot_far, (gx_first, gx_second), (gy_first, gy_second), left_ghost
    )


def prepare_own(
    near_values, owner, radius, faces, corners, base_rows,
    pulse, high_near, hot_near, hot_list, list_places, inverse, base,
    left_near,
):
    near_id = owner[...]
    high_near[...] = near_id >> 8
    lane_hot(hot_near, near_id & 255, ROWS)
    for number in range(4):
        for part in range(2):
            row = number * 2 + part
            list_places[row:row + 1, :] = faces[number:number + 1, part * 128:(part + 1) * 128]
    for place, number in enumerate((0, 2, 1, 3)):
        list_places[8:9, place * CORNER:(place + 1) * CORNER] = corners[number:number + 1, :]
    for place, number in enumerate((3, 1, 2, 0)):
        list_places[9:10, place * CORNER:(place + 1) * CORNER] = corners[number:number + 1, :]
    list_places[10:, :] = jnp.zeros((6, 128), I32)
    lane_hot(hot_list, list_places[...] & 255, LIST_ROWS)

    size = radius[...]
    cubed = size * size * size
    linear = 1.0 / cubed
    angular = 2.5 / (cubed * size * size)
    inverse[...] = jnp.where(iota((8, BODY), 0) < 3, linear, angular)
    for tile in range(OWN_TILES):
        base[:, tile * 128:(tile + 1) * 128] = base_rows[pl.ds(tile, 6, stride=OWN_TILES), :]
    scatter_near(near_values, high_near, hot_near, pulse, left_near)


def store_blocks(pulse, total):
    for block in range(OWN_WIDE):
        pulse[:, block * WIDE:(block + 1) * WIDE] = total[block * 8:block * 8 + 8]


def scatter_near(values, high_near, hot_near, pulse, left_near):
    spread_rows(left_near, values, high_near, OWN_BLOCKS)
    store_blocks(pulse, long_product(left_near, hot_near, OWN_WIDE))


def masked(flags, number, value):
    return jnp.where(flags[number:number + 1, :] > 0, value, jnp.zeros_like(value))


def gx_tiles(flags, first, second):
    tiles = []
    for part in range(2):
        cut = slice(part * 128, (part + 1) * 128)
        one, two = first[:, cut], second[:, cut]
        tiles.append((jnp.where(flag(flags, 5), one, two), jnp.where(flag(flags, 5), two, one)))
    up, down = zip(*tiles)
    return [masked(flags, 0, tile) for tile in up] + [masked(flags, 1, tile) for tile in down]


def gy_tiles(flags, first, second):
    tiles = []
    for part in range(2):
        cut = slice(part * 128, (part + 1) * 128)
        one, two = first[:, cut], second[:, cut]
        tiles.append((jnp.where(flag(flags, 6), one, two), jnp.where(flag(flags, 6), two, one)))
    left, right = zip(*tiles)
    corners = jnp.where(flags[7:8, :] > 0, first[:, FACE:], second[:, FACE:])
    return (
        [masked(flags, 2, tile) for tile in left] + [masked(flags, 3, tile) for tile in right]
        + [masked(flags, 4, corners)]
    )


def list_product(left_list, tiles, list_places, hot, first):
    for row, tile in enumerate(tiles):
        high_row = list_places[first + row:first + row + 1, :] >> 8
        spread(left_list, high_row, halves(tile), OWN_BLOCKS, row * 128)
    rows = slice(first * 128, (first + len(tiles)) * 128)
    return product(left_list, hot[rows, :], OWN_WIDE)


def scatter_far(
    flags, values, high_far, hot_far, near_pulse, list_places, hot_list, from_up, from_down,
    pulse, left_far, left_list,
):
    spread_rows(left_far, values, high_far, OWN_BLOCKS)
    total = long_product(left_far, hot_far, OWN_WIDE)
    total = total + list_product(
        left_list, gx_tiles(flags, from_up, from_down), list_places, hot_list, 0
    )
    for block in range(OWN_WIDE):
        cut = slice(block * WIDE, (block + 1) * WIDE)
        pulse[:, cut] = near_pulse[:, cut] + total[block * 8:block * 8 + 8]


def settled(flags, own, inverse, base, list_places, hot_list, from_left, from_right, left_list):
    added = list_product(
        left_list, gy_tiles(flags, from_left, from_right), list_places, hot_list, 4
    )
    blocks = []
    for block in range(OWN_WIDE):
        cut = slice(block * WIDE, (block + 1) * WIDE)
        total = own[:6, cut] + added[block * 8:block * 8 + 6]
        blocks.append(base[:, cut] + inverse[:6, cut] * total)
    return blocks


def listed(velocity, list_places, row):
    entry = jnp.broadcast_to(list_places[row:row + 1, :], (8, 128))
    tile_id, lane = entry >> 7, entry & 127
    total = jnp.zeros((8, 128), F32)
    for tile in range(OWN_TILES):
        table = velocity[:, tile * 128:(tile + 1) * 128]
        total = jnp.where(tile_id == tile, lanes_of(table, lane), total)
    return total


def settle(
    flags, own, inverse, base, list_places, hot_list, from_left, from_right,
    velocity, gx_first, gx_second, left_list,
):
    blocks = settled(
        flags, own, inverse, base, list_places, hot_list, from_left, from_right, left_list
    )
    zero = jnp.zeros((2, WIDE), F32)
    for block, value in enumerate(blocks):
        velocity[:, block * WIDE:(block + 1) * WIDE] = jnp.concatenate([value, zero], axis=0)
    found = [listed(velocity, list_places, row) for row in (0, 1, 2, 3, 9)]
    face = [jnp.concatenate(found[2 * k:2 * k + 2], axis=1) for k in range(2)]
    send_gx(flags, *face, found[4], (gx_first, gx_second))


def settle_last(
    flags, own, inverse, base, list_places, hot_list, from_left, from_right,
    velocity, left_list,
):
    blocks = settled(
        flags, own, inverse, base, list_places, hot_list, from_left, from_right, left_list
    )
    for block, value in enumerate(blocks):
        for part in range(2):
            tile = 2 * block + part
            velocity[pl.ds(tile, 6, stride=OWN_TILES), :] = value[:, part * 128:(part + 1) * 128]


def pick(tables, tile_id, lane, firsts, totals):
    for tile, table in zip(firsts, tables):
        here = tile_id == tile
        for comp in range(6):
            row = jnp.broadcast_to(table[comp:comp + 1, :], (ROWS, 128))
            totals[comp] = jnp.where(here, lanes_of(row, lane), totals[comp])
    return totals


def pick_own(velocity, tile_id, lane):
    def step(group, totals):
        tiles = [group * UNROLL + part for part in range(UNROLL)]
        tables = [velocity[:, pl.ds(pl.multiple_of(tile * 128, 128), 128)] for tile in tiles]
        return tuple(pick(tables, tile_id, lane, tiles, list(totals)))

    return list(lax.fori_loop(0, OWN_TILES // UNROLL, step, tuple(blank())))


def blank():
    return [jnp.zeros((ROWS, 128), F32) for _ in range(6)]


def gather_near(flags, velocity, places, list_places, near, gy_first, gy_second):
    tiles = [listed(velocity, list_places, row) for row in range(4, 8)]
    send_gy(
        flags, jnp.concatenate(tiles[:2], axis=1), jnp.concatenate(tiles[2:], axis=1),
        (gy_first, gy_second),
    )
    found = pick_own(velocity, places[:ROWS, :], places[ROWS:2 * ROWS, :])
    for comp in range(6):
        near[comp * ROWS:(comp + 1) * ROWS, :] = found[comp]


def gather_far(flags, velocity, places, from_up, from_down, far):
    tile_id, lane = places[2 * ROWS:3 * ROWS, :], places[3 * ROWS:, :]
    found = pick(
        gx_tiles(flags, from_up, from_down), tile_id, lane, range(OWN_TILES, OWN_TILES + 4),
        pick_own(velocity, tile_id, lane),
    )
    for comp in range(6):
        far[comp * ROWS:(comp + 1) * ROWS, :] = found[comp]


def sweep(
    flags, near_ref, far_ref, table, places, high_far, hot_far, impulse, from_left, from_right,
    impulse_out, near_values, far_values, gx_first, gx_second, gy_first, gy_second, left_ghost,
):
    near = [plane(near_ref, comp) for comp in range(6)]
    far = pick(
        gy_tiles(flags, from_left, from_right),
        places[2 * ROWS:3 * ROWS, :], places[3 * ROWS:, :],
        range(OWN_TILES + 4, OWN_TILES + 9), [plane(far_ref, comp) for comp in range(6)],
    )
    get = lambda name: plane(table, PLANE[name])
    n0, n1, n2 = get("n0"), get("n1"), get("n2")
    a0, a1 = get("a0"), get("a1")
    b0, b1, b2 = get("b0"), get("b1"), get("b2")
    arm0, arm1, relax, mu = get("arm0"), get("arm1"), get("relax"), get("mu")
    w0, w1, w2 = [near[c] - far[c] for c in range(3)]
    s0, s1, s2 = [arm0 * near[c] + arm1 * far[c] for c in range(3, 6)]
    rate_n = n0 * w0 + n1 * w1 + n2 * w2
    rate_a = (a0 * w0 + a1 * w1) - (b0 * s0 + b1 * s1 + b2 * s2)
    rate_b = (b0 * w0 + b1 * w1 + b2 * w2) + (a0 * s0 + a1 * s1)
    trial_n = plane(impulse, 0) - relax * (rate_n + get("bias"))
    trial_a = plane(impulse, 1) - relax * rate_a
    trial_b = plane(impulse, 2) - relax * rate_b
    length = jnp.sqrt(trial_a * trial_a + trial_b * trial_b)
    inside = length <= mu * trial_n
    dead = mu * length <= -trial_n
    level = (trial_n + mu * length) / (1.0 + mu * mu)
    factor = mu * level / jnp.maximum(length, SMALLEST)
    choose = lambda kept, cone: jnp.where(inside, kept, jnp.where(dead, 0.0, cone))
    fresh = [
        choose(trial_n, level), choose(trial_a, factor * trial_a), choose(trial_b, factor * trial_b)
    ]
    for comp in range(3):
        impulse_out[comp * ROWS:(comp + 1) * ROWS, :] = fresh[comp]
    end_pulses(fresh, table, near_values, far_values)
    ghost_pulses(
        flags, far_values, high_far, hot_far, (gx_first, gx_second), (gy_first, gy_second), left_ghost
    )


def shape(*dims, kind=F32):
    return jax.ShapeDtypeStruct(dims, kind)


FACES = (shape(8, FACE), shape(8, FACE))
GX_SENDS = (shape(8, MESSAGE), shape(8, MESSAGE))
VALUES = shape(8 * ROWS, 128)
PULSE = shape(8, BODY)
LEFT_OWN = pltpu.VMEM((2 * OWN_WIDE * 8, CONTACTS), BF16)
LEFT_GHOST = pltpu.VMEM((2 * GHOST_WIDE * 8, CONTACTS), BF16)


def left_list(tiles):
    return pltpu.VMEM((2 * OWN_WIDE * 8, tiles * 128), BF16)


def call(body, outs, scratch, *operands, specs=None):
    vmem = pl.BlockSpec(memory_space=pltpu.VMEM)
    return pl.pallas_call(
        body,
        out_shape=outs,
        in_specs=specs or [vmem] * len(operands),
        out_specs=[vmem] * len(outs),
        scratch_shapes=scratch,
        compiler_params=pltpu.CompilerParams(vmem_limit_bytes=10 * 1024 * 1024),
    )(*operands)


def loop(value, back, lines, place):
    count, length = lines
    pairs = []
    for line in range(0, count, 2):
        ring = [place(line, step) for step in range(length)]
        ring += [place(line + 1, step) for step in reversed(range(length))]
        for here, there in zip(ring, ring[1:] + ring[:1]):
            pairs.append((there, here) if back else (here, there))
    return lax.ppermute(value, ("gx", "gy"), pairs)


def along_gx(first, second):
    rows, columns = lax.axis_size("gx"), lax.axis_size("gy")
    place = lambda line, step: step * columns + line
    lines = (columns, rows)
    return loop(first, False, lines, place), loop(second, True, lines, place)


def along_gy(got_first, got_second, face_first, face_second):
    rows, columns = lax.axis_size("gx"), lax.axis_size("gy")
    corners = got_first[:, FACE:] + got_second[:, FACE:]
    first = jnp.concatenate([face_first, corners], axis=1)
    second = jnp.concatenate([face_second, corners], axis=1)
    place = lambda line, step: line * columns + step
    lines = (rows, columns)
    return loop(first, False, lines, place), loop(second, True, lines, place)


def presence():
    row_at, row_count = lax.axis_index("gx"), lax.axis_size("gx")
    col_at, col_count = lax.axis_index("gy"), lax.axis_size("gy")
    row, slot = iota((8, 128), 0), iota((8, 128), 1) // CORNER
    above = (row == 0) | ((row == 4) & ((slot == 0) | (slot == 2)))
    below = (row == 1) | ((row == 4) & ((slot == 1) | (slot == 3)))
    before = (row == 2) | ((row == 4) & (slot < 2))
    after = (row == 3) | ((row == 4) & (slot >= 2))
    odd_row, odd_col = lax.rem(row_at, 2), lax.rem(col_at, 2)
    off = (
        (above & (row_at == 0)) | (below & (row_at == row_count - 1))
        | (before & (col_at == 0)) | (after & (col_at == col_count - 1))
        | ((row == 5) & (odd_col == 1)) | ((row == 6) & (odd_row == 1))
        | ((row == 7) & ((slot >> 1) != odd_row))
    )
    return jnp.where(off, 0.0, 1.0)


def shards(
    free_velocity, body_radius, face_lists, corner_lists, owner_body, other_body,
    contact_angles, contact_arms, friction, approach, start_impulse,
):
    flags = presence()
    in_rows = lambda value: value[0, 0].reshape(-1, 128)
    dma = pltpu.SemaphoreType.DMA
    raw = [
        pltpu.with_memory_space_constraint(value, pltpu.HBM)
        for value in (
            contact_angles[0, 0], contact_arms[0, 0], in_rows(friction), in_rows(approach),
            in_rows(start_impulse), in_rows(owner_body), in_rows(other_body),
            body_radius[0], face_lists[0, 0], corner_lists[0, 0], in_rows(free_velocity),
        )
    ]
    (
        table, places, high_far, impulse, hot_far, near_values, far_values,
        gx_first, gx_second, gy_first, gy_second, owner, radius, faces, corners, base_rows,
    ) = call(
        prepare,
        (
            shape(len(PLANES) * ROWS, 128),
            shape(4 * ROWS, 128, kind=I32),
            shape(ROWS, 128, kind=I32),
            shape(IMPULSE_ROWS, 128),
            shape(CONTACTS, WIDE, kind=BF16),
            VALUES, VALUES,
        ) + GX_SENDS + FACES + (
            shape(ROWS, 128, kind=I32),
            shape(1, BODY),
            shape(4, FACE, kind=I32),
            shape(4, CORNER, kind=I32),
            shape(6 * OWN_TILES, 128),
        ),
        (
            pltpu.VMEM((2, CONTACTS), F32),
            pltpu.VMEM((2, CONTACTS), F32),
            pltpu.VMEM((ROWS, 128), F32),
            pltpu.VMEM((ROWS, 128), F32),
            pltpu.VMEM((ROWS, 128), I32),
            pltpu.VMEM((4 * ROWS, 128), F32),
            LEFT_GHOST,
            dma((11,)),
        ),
        flags, *raw,
        specs=[pl.BlockSpec(memory_space=pltpu.VMEM)]
        + [pl.BlockSpec(memory_space=pltpu.HBM)] * len(raw),
    )
    for number in range(SWEEPS + 1):
        got = along_gx(gx_first, gx_second)
        if number == 0:
            pulse, high_near, hot_near, hot_list, list_places, inverse, base = call(
                prepare_own,
                (
                    PULSE,
                    shape(ROWS, 128, kind=I32),
                    shape(CONTACTS, WIDE, kind=BF16),
                    shape(LISTED, WIDE, kind=BF16),
                    shape(16, 128, kind=I32),
                    PULSE,
                    shape(6, BODY),
                ),
                (LEFT_OWN,),
                near_values, owner, radius, faces, corners, base_rows,
            )
        else:
            (pulse,) = call(
                scatter_near, (PULSE,), (LEFT_OWN,), near_values, high_near, hot_near
            )
        got_gy = along_gy(*got, gy_first, gy_second)
        (own,) = call(
            scatter_far, (PULSE,), (LEFT_OWN, left_list(4)),
            flags, far_values, high_far, hot_far, pulse, list_places, hot_list, *got,
        )
        fixed = (flags, own, inverse, base, list_places, hot_list, *got_gy)
        if number == SWEEPS:
            (velocity,) = call(
                settle_last, (shape(6 * OWN_TILES, 128),), (left_list(5),), *fixed
            )
            break
        velocity, gx_first, gx_second = call(
            settle, (PULSE,) + GX_SENDS, (left_list(5),), *fixed
        )
        got = along_gx(gx_first, gx_second)
        near, gy_first, gy_second = call(
            gather_near, (shape(6 * ROWS, 128),) + FACES, (), flags, velocity, places, list_places
        )
        got_gy = along_gy(*got, gy_first, gy_second)
        (far,) = call(
            gather_far, (shape(6 * ROWS, 128),), (), flags, velocity, places, *got
        )
        impulse, near_values, far_values, gx_first, gx_second, gy_first, gy_second = call(
            sweep, (shape(IMPULSE_ROWS, 128), VALUES, VALUES) + GX_SENDS + FACES, (LEFT_GHOST,),
            flags, near, far, table, places, high_far, hot_far, impulse, *got_gy,
        )
    return velocity.reshape(1, 1, 6, BODY), impulse.reshape(1, 1, 3, CONTACTS)

def solution(mesh):
    in_specs = (
        P("gx", "gy", None, None),
        P("gx", "gy", None),
        P("gx", "gy", None, None),
        P("gx", "gy", None, None),
        P("gx", "gy", None),
        P("gx", "gy", None),
        P("gx", "gy", None, None),
        P("gx", "gy", None, None),
        P("gx", "gy", None),
        P("gx", "gy", None),
        P("gx", "gy", None, None),
    )
    out_specs = (P("gx", "gy", None, None), P("gx", "gy", None, None))
    return jax.shard_map(shards, mesh=mesh, in_specs=in_specs, out_specs=out_specs, check_vma=False)
```

```python
import jax
import jax.numpy as jnp
from jax import lax
from jax.experimental import pallas as pl
from jax.experimental.pallas import tpu as pltpu
from jax.sharding import PartitionSpec as P

SWEEPS = 4
RELAX = 0.25
SMALLEST = 1e-20

BODY = 2048
FACE = 256
CORNER = 32
CONTACTS = 4096
ROWS = CONTACTS // 128
LISTED = 4 * FACE + 4 * CORNER
LIST_ROWS = LISTED // 128
OWN_TILES = BODY // 128
WIDE = 256
OWN_WIDE = BODY // WIDE
GHOST_WIDE = 6
IMPULSE_ROWS = 3 * ROWS
MESSAGE = FACE + 128

F32 = jnp.float32
BF16 = jnp.bfloat16
I32 = jnp.int32

PLANES = (
    "n0", "n1", "n2", "a0", "a1", "b0", "b1", "b2",
    "arm0", "arm1", "relax", "mu", "bias",
)
PLANE = {name: place for place, name in enumerate(PLANES)}


def lanes_of(table, lane):
    numbers = lax.GatherDimensionNumbers(
        offset_dims=(),
        collapsed_slice_dims=(1,),
        start_index_map=(1,),
        operand_batching_dims=(0,),
        start_indices_batching_dims=(0,),
    )
    return lax.gather(
        table, lane[..., None], numbers, (1, 1),
        mode=lax.GatherScatterMode.PROMISE_IN_BOUNDS,
    )


def iota(shape, dim):
    return lax.broadcasted_iota(I32, shape, dim)


def halves(values):
    high = values.astype(BF16).astype(F32)
    return high, values - high


def plane(ref, number):
    return ref[number * ROWS:(number + 1) * ROWS, :]


def spread(ref, high_row, parts, blocks, column):
    picks = [high_row == block for block in blocks]
    for part, value in enumerate(parts):
        zero = jnp.zeros_like(value)
        for pair in range(len(blocks) // 2):
            both = jnp.concatenate(
                [
                    jnp.where(picks[2 * pair], value, zero),
                    jnp.where(picks[2 * pair + 1], value, zero),
                ],
                axis=0,
            )
            start = part * len(blocks) * 8 + pair * 16
            ref[start:start + 16, column:column + 128] = both.astype(BF16)


OWN_BLOCKS = tuple(range(OWN_WIDE))
GHOST_BLOCKS = tuple(range(OWN_WIDE, OWN_WIDE + GHOST_WIDE))


def lane_hot(ref, low, rows):
    turned = jnp.transpose(low)
    along = iota((128, WIDE), 1)
    for row in range(rows):
        hot = jnp.broadcast_to(turned[:, row:row + 1], (128, WIDE)) == along
        ref[row * 128:(row + 1) * 128, :] = jnp.where(hot, 1.0, 0.0).astype(BF16)


def product(left, hot, blocks):
    total = jnp.dot(left[...], hot, preferred_element_type=F32)
    return total[:blocks * 8] + total[blocks * 8:]


def end_pulses(impulse, table, near_out, far_out):
    p0, p1, p2 = impulse
    get = lambda name: plane(table, PLANE[name])
    a0, a1 = get("a0"), get("a1")
    b0, b1, b2 = get("b0"), get("b1"), get("b2")
    force = (
        p0 * get("n0") + p1 * a0 + p2 * b0,
        p0 * get("n1") + p1 * a1 + p2 * b1,
        p0 * get("n2") + p2 * b2,
    )
    twist = (p1 * b0 - p2 * a0, p1 * b1 - p2 * a1, p1 * b2)
    arm0, arm1 = -get("arm0"), -get("arm1")
    for comp in range(3):
        near_out[pl.ds(comp, ROWS, stride=8), :] = force[comp]
        far_out[pl.ds(comp, ROWS, stride=8), :] = -force[comp]
        near_out[pl.ds(comp + 3, ROWS, stride=8), :] = arm0 * twist[comp]
        far_out[pl.ds(comp + 3, ROWS, stride=8), :] = arm1 * twist[comp]
    for comp in (6, 7):
        near_out[pl.ds(comp, ROWS, stride=8), :] = jnp.zeros((ROWS, 128), F32)
        far_out[pl.ds(comp, ROWS, stride=8), :] = jnp.zeros((ROWS, 128), F32)


def spread_rows(left, values, high, blocks):
    for row in range(ROWS):
        value = values[row * 8:(row + 1) * 8, :]
        spread(left, high[row:row + 1, :], halves(value), blocks, row * 128)


def ghost_pulses(flags, far, high_far, hot_far, gx_sends, gy_faces, left_ghost):
    spread_rows(left_ghost, far, high_far, GHOST_BLOCKS)
    total = product(left_ghost, hot_far[...], GHOST_WIDE)
    ghost = [total[block * 8:block * 8 + 8] for block in range(5)]
    send_gx(flags, ghost[0], ghost[1], ghost[4][:, :128], gx_sends)
    send_gy(flags, ghost[2], ghost[3], gy_faces)


def flag(flags, number, width=128):
    return jnp.broadcast_to(flags[number:number + 1, :1] > 0, (8, width))


def send_gx(flags, face0, face1, corners, sends):
    first, second = sends
    slot = iota((8, 128), 1) // CORNER
    to_down = (slot == 0) | (slot == 2)
    up = jnp.where(to_down | ~flag(flags, 0), 0.0, corners)
    down = jnp.where(to_down & flag(flags, 1), corners, 0.0)
    first[:, :FACE] = face1
    first[:, FACE:] = down
    second[:, :FACE] = face0
    second[:, FACE:] = up


def send_gy(flags, face2, face3, faces):
    wide = flag(flags, 6, FACE)
    faces[0][...] = jnp.where(wide, face3, face2)
    faces[1][...] = jnp.where(wide, face2, face3)


def prepare(
    flags, angles_in, arms_in, mu_in, bias_in, impulse_in, owner_in, other_in,
    radius_in, faces_in, corners_in, base_in,
    table, places, high_far, impulse, hot_far, near_values, far_values,
    gx_first, gx_second, gy_first, gy_second,
    owner, radius, faces, corners, base,
    angles, arms, mu, bias, other, flat, left_ghost, sems,
):
    copies = [
        pltpu.make_async_copy(source, target, sems.at[number])
        for number, (source, target) in enumerate((
            (other_in, other), (angles_in, angles), (arms_in, arms), (mu_in, mu),
            (bias_in, bias), (impulse_in, impulse), (owner_in, owner), (radius_in, radius),
            (faces_in, faces), (corners_in, corners), (base_in, base),
        ))
    ]
    for copy in copies:
        copy.start()
    copies[0].wait()
    far_id = other[...]
    extra = far_id - (BODY + 4 * FACE)
    block = extra >> 5
    slot = ((block & 1) << 1) | (block >> 1)
    in_block = extra & (CORNER - 1)
    is_corner = extra >= 0
    places[2 * ROWS:3 * ROWS, :] = far_id >> 7
    places[3 * ROWS:, :] = jnp.where(is_corner, slot * CORNER + in_block, far_id & 127)
    high_far[...] = far_id >> 8
    lane_hot(
        hot_far, jnp.where(is_corner, (3 - slot) * CORNER + in_block, far_id & 255), ROWS
    )
    for copy in copies[1:]:
        copy.wait()
    near_id = owner[...]
    places[:ROWS, :] = near_id >> 7
    places[ROWS:2 * ROWS, :] = near_id & 127
    for row in range(ROWS):
        cut = slice(row * 128, (row + 1) * 128)
        flat[pl.ds(row, 2, stride=ROWS), :] = angles[:, cut]
        flat[pl.ds(2 * ROWS + row, 2, stride=ROWS), :] = arms[:, cut]
    polar, azim = plane(flat, 0), plane(flat, 1)
    arm0, arm1 = plane(flat, 2), plane(flat, 3)
    cos_polar, sin_polar = jnp.cos(polar), jnp.sin(polar)
    cos_azim, sin_azim = jnp.cos(azim), jnp.sin(azim)
    cubed0 = arm0 * arm0 * arm0
    cubed1 = arm1 * arm1 * arm1
    values = {
        "n0": cos_polar * cos_azim, "n1": cos_polar * sin_azim, "n2": sin_polar,
        "a0": -sin_azim, "a1": cos_azim,
        "b0": -sin_polar * cos_azim, "b1": -sin_polar * sin_azim, "b2": cos_polar,
        "arm0": arm0, "arm1": arm1,
        "relax": RELAX / (1.0 / cubed0 + 1.0 / cubed1),
        "mu": mu[...], "bias": bias[...],
    }
    for name, value in values.items():
        number = PLANE[name]
        table[number * ROWS:(number + 1) * ROWS, :] = value
    end_pulses([plane(impulse, comp) for comp in range(3)], table, near_values, far_values)
    ghost_pulses(
        flags, far_values, high_far, hot_far, (gx_first, gx_second), (gy_first, gy_second), left_ghost
    )


def prepare_own(
    near_values, owner, radius, faces, corners, base_rows,
    pulse, high_near, hot_near, hot_list, list_places, inverse, base,
    left_near,
):
    near_id = owner[...]
    high_near[...] = near_id >> 8
    lane_hot(hot_near, near_id & 255, ROWS)
    for number in range(4):
        for part in range(2):
            row = number * 2 + part
            list_places[row:row + 1, :] = faces[number:number + 1, part * 128:(part + 1) * 128]
    for place, number in enumerate((0, 2, 1, 3)):
        list_places[8:9, place * CORNER:(place + 1) * CORNER] = corners[number:number + 1, :]
    for place, number in enumerate((3, 1, 2, 0)):
        list_places[9:10, place * CORNER:(place + 1) * CORNER] = corners[number:number + 1, :]
    list_places[10:, :] = jnp.zeros((6, 128), I32)
    lane_hot(hot_list, list_places[...] & 255, LIST_ROWS)

    size = radius[...]
    cubed = size * size * size
    linear = 1.0 / cubed
    angular = 2.5 / (cubed * size * size)
    inverse[...] = jnp.where(iota((8, BODY), 0) < 3, linear, angular)
    for tile in range(OWN_TILES):
        base[:, tile * 128:(tile + 1) * 128] = base_rows[pl.ds(tile, 6, stride=OWN_TILES), :]
    scatter_near(near_values, high_near, hot_near, pulse, left_near)


def store_blocks(pulse, total):
    for block in range(OWN_WIDE):
        pulse[:, block * WIDE:(block + 1) * WIDE] = total[block * 8:block * 8 + 8]


def scatter_near(values, high_near, hot_near, pulse, left_near):
    spread_rows(left_near, values, high_near, OWN_BLOCKS)
    store_blocks(pulse, product(left_near, hot_near[...], OWN_WIDE))


def masked(flags, number, value):
    return jnp.where(flags[number:number + 1, :] > 0, value, jnp.zeros_like(value))


def gx_tiles(flags, first, second):
    return [
        masked(flags, number, ref[:, part * 128:(part + 1) * 128])
        for number, ref in enumerate((first, second))
        for part in range(2)
    ]


def gy_tiles(flags, first, second):
    tiles = []
    for part in range(2):
        cut = slice(part * 128, (part + 1) * 128)
        one, two = first[:, cut], second[:, cut]
        tiles.append((jnp.where(flag(flags, 6), one, two), jnp.where(flag(flags, 6), two, one)))
    left, right = zip(*tiles)
    corners = jnp.where(flags[7:8, :] > 0, first[:, FACE:], second[:, FACE:])
    return (
        [masked(flags, 2, tile) for tile in left] + [masked(flags, 3, tile) for tile in right]
        + [masked(flags, 4, corners)]
    )


def list_product(left_list, tiles, list_places, hot, first):
    for row, tile in enumerate(tiles):
        high_row = list_places[first + row:first + row + 1, :] >> 8
        spread(left_list, high_row, halves(tile), OWN_BLOCKS, row * 128)
    rows = slice(first * 128, (first + len(tiles)) * 128)
    return product(left_list, hot[rows, :], OWN_WIDE)


def scatter_far(
    flags, values, high_far, hot_far, near_pulse, list_places, hot_list, from_up, from_down,
    pulse, left_far, left_list,
):
    spread_rows(left_far, values, high_far, OWN_BLOCKS)
    total = product(left_far, hot_far[...], OWN_WIDE)
    total = total + list_product(
        left_list, gx_tiles(flags, from_up, from_down), list_places, hot_list, 0
    )
    for block in range(OWN_WIDE):
        cut = slice(block * WIDE, (block + 1) * WIDE)
        pulse[:, cut] = near_pulse[:, cut] + total[block * 8:block * 8 + 8]


def settled(flags, own, inverse, base, list_places, hot_list, from_left, from_right, left_list):
    added = list_product(
        left_list, gy_tiles(flags, from_left, from_right), list_places, hot_list, 4
    )
    blocks = []
    for block in range(OWN_WIDE):
        cut = slice(block * WIDE, (block + 1) * WIDE)
        total = own[:6, cut] + added[block * 8:block * 8 + 6]
        blocks.append(base[:, cut] + inverse[:6, cut] * total)
    return blocks


def listed(velocity, list_places, row):
    entry = jnp.broadcast_to(list_places[row:row + 1, :], (8, 128))
    tile_id, lane = entry >> 7, entry & 127
    total = jnp.zeros((8, 128), F32)
    for tile in range(OWN_TILES):
        table = velocity[:, tile * 128:(tile + 1) * 128]
        total = jnp.where(tile_id == tile, lanes_of(table, lane), total)
    return total


def settle(
    flags, own, inverse, base, list_places, hot_list, from_left, from_right,
    velocity, gx_first, gx_second, left_list,
):
    blocks = settled(
        flags, own, inverse, base, list_places, hot_list, from_left, from_right, left_list
    )
    zero = jnp.zeros((2, WIDE), F32)
    for block, value in enumerate(blocks):
        velocity[:, block * WIDE:(block + 1) * WIDE] = jnp.concatenate([value, zero], axis=0)
    found = [listed(velocity, list_places, row) for row in (0, 1, 2, 3, 9)]
    face = [jnp.concatenate(found[2 * k:2 * k + 2], axis=1) for k in range(2)]
    send_gx(flags, *face, found[4], (gx_first, gx_second))


def settle_last(
    flags, own, inverse, base, list_places, hot_list, from_left, from_right,
    velocity, left_list,
):
    blocks = settled(
        flags, own, inverse, base, list_places, hot_list, from_left, from_right, left_list
    )
    for block, value in enumerate(blocks):
        for part in range(2):
            tile = 2 * block + part
            velocity[pl.ds(tile, 6, stride=OWN_TILES), :] = value[:, part * 128:(part + 1) * 128]


def pick(tables, tile_id, lane, firsts, totals):
    for tile, table in zip(firsts, tables):
        here = tile_id == tile
        for comp in range(6):
            row = jnp.broadcast_to(table[comp:comp + 1, :], (ROWS, 128))
            totals[comp] = jnp.where(here, lanes_of(row, lane), totals[comp])
    return totals


def own_tables(velocity):
    return [velocity[:, tile * 128:(tile + 1) * 128] for tile in range(OWN_TILES)]


def blank():
    return [jnp.zeros((ROWS, 128), F32) for _ in range(6)]


def gather_near(flags, velocity, places, list_places, near, gy_first, gy_second):
    tiles = [listed(velocity, list_places, row) for row in range(4, 8)]
    send_gy(
        flags, jnp.concatenate(tiles[:2], axis=1), jnp.concatenate(tiles[2:], axis=1),
        (gy_first, gy_second),
    )
    found = pick(
        own_tables(velocity), places[:ROWS, :], places[ROWS:2 * ROWS, :], range(OWN_TILES), blank()
    )
    for comp in range(6):
        near[comp * ROWS:(comp + 1) * ROWS, :] = found[comp]


def gather_far(flags, velocity, places, from_up, from_down, far):
    found = pick(
        own_tables(velocity) + gx_tiles(flags, from_up, from_down),
        places[2 * ROWS:3 * ROWS, :], places[3 * ROWS:, :], range(OWN_TILES + 4), blank(),
    )
    for comp in range(6):
        far[comp * ROWS:(comp + 1) * ROWS, :] = found[comp]


def sweep(
    flags, near_ref, far_ref, table, places, high_far, hot_far, impulse, from_left, from_right,
    impulse_out, near_values, far_values, gx_first, gx_second, gy_first, gy_second, left_ghost,
):
    near = [plane(near_ref, comp) for comp in range(6)]
    far = pick(
        gy_tiles(flags, from_left, from_right),
        places[2 * ROWS:3 * ROWS, :], places[3 * ROWS:, :],
        range(OWN_TILES + 4, OWN_TILES + 9), [plane(far_ref, comp) for comp in range(6)],
    )
    get = lambda name: plane(table, PLANE[name])
    n0, n1, n2 = get("n0"), get("n1"), get("n2")
    a0, a1 = get("a0"), get("a1")
    b0, b1, b2 = get("b0"), get("b1"), get("b2")
    arm0, arm1, relax, mu = get("arm0"), get("arm1"), get("relax"), get("mu")
    w0, w1, w2 = [near[c] - far[c] for c in range(3)]
    s0, s1, s2 = [arm0 * near[c] + arm1 * far[c] for c in range(3, 6)]
    rate_n = n0 * w0 + n1 * w1 + n2 * w2
    rate_a = (a0 * w0 + a1 * w1) - (b0 * s0 + b1 * s1 + b2 * s2)
    rate_b = (b0 * w0 + b1 * w1 + b2 * w2) + (a0 * s0 + a1 * s1)
    trial_n = plane(impulse, 0) - relax * (rate_n + get("bias"))
    trial_a = plane(impulse, 1) - relax * rate_a
    trial_b = plane(impulse, 2) - relax * rate_b
    length = jnp.sqrt(trial_a * trial_a + trial_b * trial_b)
    inside = length <= mu * trial_n
    dead = mu * length <= -trial_n
    level = (trial_n + mu * length) / (1.0 + mu * mu)
    factor = mu * level / jnp.maximum(length, SMALLEST)
    choose = lambda kept, cone: jnp.where(inside, kept, jnp.where(dead, 0.0, cone))
    fresh = [
        choose(trial_n, level), choose(trial_a, factor * trial_a), choose(trial_b, factor * trial_b)
    ]
    for comp in range(3):
        impulse_out[comp * ROWS:(comp + 1) * ROWS, :] = fresh[comp]
    end_pulses(fresh, table, near_values, far_values)
    ghost_pulses(
        flags, far_values, high_far, hot_far, (gx_first, gx_second), (gy_first, gy_second), left_ghost
    )


def shape(*dims, kind=F32):
    return jax.ShapeDtypeStruct(dims, kind)


FACES = (shape(8, FACE), shape(8, FACE))
GX_SENDS = (shape(8, MESSAGE), shape(8, MESSAGE))
VALUES = shape(8 * ROWS, 128)
PULSE = shape(8, BODY)
LEFT_OWN = pltpu.VMEM((2 * OWN_WIDE * 8, CONTACTS), BF16)
LEFT_GHOST = pltpu.VMEM((2 * GHOST_WIDE * 8, CONTACTS), BF16)


def left_list(tiles):
    return pltpu.VMEM((2 * OWN_WIDE * 8, tiles * 128), BF16)


def call(body, outs, scratch, *operands, specs=None):
    vmem = pl.BlockSpec(memory_space=pltpu.VMEM)
    return pl.pallas_call(
        body,
        out_shape=outs,
        in_specs=specs or [vmem] * len(operands),
        out_specs=[vmem] * len(outs),
        scratch_shapes=scratch,
        compiler_params=pltpu.CompilerParams(vmem_limit_bytes=10 * 1024 * 1024),
    )(*operands)


def loop(value, back, lines, place):
    count, length = lines
    pairs = []
    for line in range(0, count, 2):
        ring = [place(line, step) for step in range(length)]
        ring += [place(line + 1, step) for step in reversed(range(length))]
        for here, there in zip(ring, ring[1:] + ring[:1]):
            pairs.append((there, here) if back else (here, there))
    return lax.ppermute(value, ("gx", "gy"), pairs)


def along_gx(first, second):
    size = lax.axis_size("gx")
    down = [(i, (i + 1) % size) for i in range(size)]
    up = [(j, i) for i, j in down]
    return lax.ppermute(first, "gx", down), lax.ppermute(second, "gx", up)


def along_gy(got_first, got_second, face_first, face_second):
    rows, columns = lax.axis_size("gx"), lax.axis_size("gy")
    corners = got_first[:, FACE:] + got_second[:, FACE:]
    first = jnp.concatenate([face_first, corners], axis=1)
    second = jnp.concatenate([face_second, corners], axis=1)
    place = lambda line, step: line * columns + step
    lines = (rows, columns)
    return loop(first, False, lines, place), loop(second, True, lines, place)


def presence():
    row_at, row_count = lax.axis_index("gx"), lax.axis_size("gx")
    col_at, col_count = lax.axis_index("gy"), lax.axis_size("gy")
    row, slot = iota((8, 128), 0), iota((8, 128), 1) // CORNER
    above = (row == 0) | ((row == 4) & ((slot == 0) | (slot == 2)))
    below = (row == 1) | ((row == 4) & ((slot == 1) | (slot == 3)))
    before = (row == 2) | ((row == 4) & (slot < 2))
    after = (row == 3) | ((row == 4) & (slot >= 2))
    odd_row = lax.rem(row_at, 2)
    off = (
        (above & (row_at == 0)) | (below & (row_at == row_count - 1))
        | (before & (col_at == 0)) | (after & (col_at == col_count - 1))
        | ((row == 6) & (odd_row == 1))
        | ((row == 7) & ((slot >> 1) != odd_row))
    )
    return jnp.where(off, 0.0, 1.0)


def shards(
    free_velocity, body_radius, face_lists, corner_lists, owner_body, other_body,
    contact_angles, contact_arms, friction, approach, start_impulse,
):
    flags = presence()
    in_rows = lambda value: value[0, 0].reshape(-1, 128)
    dma = pltpu.SemaphoreType.DMA
    raw = [
        pltpu.with_memory_space_constraint(value, pltpu.HBM)
        for value in (
            contact_angles[0, 0], contact_arms[0, 0], in_rows(friction), in_rows(approach),
            in_rows(start_impulse), in_rows(owner_body), in_rows(other_body),
            body_radius[0], face_lists[0, 0], corner_lists[0, 0], in_rows(free_velocity),
        )
    ]
    (
        table, places, high_far, impulse, hot_far, near_values, far_values,
        gx_first, gx_second, gy_first, gy_second, owner, radius, faces, corners, base_rows,
    ) = call(
        prepare,
        (
            shape(len(PLANES) * ROWS, 128),
            shape(4 * ROWS, 128, kind=I32),
            shape(ROWS, 128, kind=I32),
            shape(IMPULSE_ROWS, 128),
            shape(CONTACTS, WIDE, kind=BF16),
            VALUES, VALUES,
        ) + GX_SENDS + FACES + (
            shape(ROWS, 128, kind=I32),
            shape(1, BODY),
            shape(4, FACE, kind=I32),
            shape(4, CORNER, kind=I32),
            shape(6 * OWN_TILES, 128),
        ),
        (
            pltpu.VMEM((2, CONTACTS), F32),
            pltpu.VMEM((2, CONTACTS), F32),
            pltpu.VMEM((ROWS, 128), F32),
            pltpu.VMEM((ROWS, 128), F32),
            pltpu.VMEM((ROWS, 128), I32),
            pltpu.VMEM((4 * ROWS, 128), F32),
            LEFT_GHOST,
            dma((11,)),
        ),
        flags, *raw,
        specs=[pl.BlockSpec(memory_space=pltpu.VMEM)]
        + [pl.BlockSpec(memory_space=pltpu.HBM)] * len(raw),
    )
    for number in range(SWEEPS + 1):
        got = along_gx(gx_first, gx_second)
        if number == 0:
            pulse, high_near, hot_near, hot_list, list_places, inverse, base = call(
                prepare_own,
                (
                    PULSE,
                    shape(ROWS, 128, kind=I32),
                    shape(CONTACTS, WIDE, kind=BF16),
                    shape(LISTED, WIDE, kind=BF16),
                    shape(16, 128, kind=I32),
                    PULSE,
                    shape(6, BODY),
                ),
                (LEFT_OWN,),
                near_values, owner, radius, faces, corners, base_rows,
            )
        else:
            (pulse,) = call(
                scatter_near, (PULSE,), (LEFT_OWN,), near_values, high_near, hot_near
            )
        got_gy = along_gy(*got, gy_first, gy_second)
        (own,) = call(
            scatter_far, (PULSE,), (LEFT_OWN, left_list(4)),
            flags, far_values, high_far, hot_far, pulse, list_places, hot_list, *got,
        )
        fixed = (flags, own, inverse, base, list_places, hot_list, *got_gy)
        if number == SWEEPS:
            (velocity,) = call(
                settle_last, (shape(6 * OWN_TILES, 128),), (left_list(5),), *fixed
            )
            break
        velocity, gx_first, gx_second = call(
            settle, (PULSE,) + GX_SENDS, (left_list(5),), *fixed
        )
        got = along_gx(gx_first, gx_second)
        near, gy_first, gy_second = call(
            gather_near, (shape(6 * ROWS, 128),) + FACES, (), flags, velocity, places, list_places
        )
        got_gy = along_gy(*got, gy_first, gy_second)
        (far,) = call(
            gather_far, (shape(6 * ROWS, 128),), (), flags, velocity, places, *got
        )
        impulse, near_values, far_values, gx_first, gx_second, gy_first, gy_second = call(
            sweep, (shape(IMPULSE_ROWS, 128), VALUES, VALUES) + GX_SENDS + FACES, (LEFT_GHOST,),
            flags, near, far, table, places, high_far, hot_far, impulse, *got_gy,
        )
    return velocity.reshape(1, 1, 6, BODY), impulse.reshape(1, 1, 3, CONTACTS)

def solution(mesh):
    in_specs = (
        P("gx", "gy", None, None),
        P("gx", "gy", None),
        P("gx", "gy", None, None),
        P("gx", "gy", None, None),
        P("gx", "gy", None),
        P("gx", "gy", None),
        P("gx", "gy", None, None),
        P("gx", "gy", None, None),
        P("gx", "gy", None),
        P("gx", "gy", None),
        P("gx", "gy", None, None),
    )
    out_specs = (P("gx", "gy", None, None), P("gx", "gy", None, None))
    return jax.shard_map(shards, mesh=mesh, in_specs=in_specs, out_specs=out_specs, check_vma=False)
```

```python
import jax
import jax.numpy as jnp
from jax import lax
from jax.experimental import pallas as pl
from jax.experimental.pallas import tpu as pltpu
from jax.sharding import PartitionSpec as P

SWEEPS = 4
RELAX = 0.25
SMALLEST = 1e-20

BODY = 2048
FACE = 256
CORNER = 32
CONTACTS = 4096
ROWS = CONTACTS // 128
LISTED = 4 * FACE + 4 * CORNER
LIST_ROWS = LISTED // 128
OWN_TILES = BODY // 128
WIDE = 256
OWN_WIDE = BODY // WIDE
IMPULSE_ROWS = 3 * ROWS
MESSAGE = FACE + 128

F32 = jnp.float32
BF16 = jnp.bfloat16
I32 = jnp.int32

PLANES = (
    "n0", "n1", "n2", "a0", "a1", "b0", "b1", "b2",
    "arm0", "arm1", "relax", "mu", "bias",
)
PLANE = {name: place for place, name in enumerate(PLANES)}


def lanes_of(table, lane):
    numbers = lax.GatherDimensionNumbers(
        offset_dims=(),
        collapsed_slice_dims=(1,),
        start_index_map=(1,),
        operand_batching_dims=(0,),
        start_indices_batching_dims=(0,),
    )
    return lax.gather(
        table, lane[..., None], numbers, (1, 1),
        mode=lax.GatherScatterMode.PROMISE_IN_BOUNDS,
    )


def iota(shape, dim):
    return lax.broadcasted_iota(I32, shape, dim)


def halves(values):
    high = values.astype(BF16).astype(F32)
    return high, values - high


def plane(ref, number):
    return ref[number * ROWS:(number + 1) * ROWS, :]


def spread(ref, high_row, parts, blocks, column):
    picks = [high_row == block for block in blocks]
    for part, value in enumerate(parts):
        zero = jnp.zeros_like(value)
        for pair in range(len(blocks) // 2):
            both = jnp.concatenate(
                [
                    jnp.where(picks[2 * pair], value, zero),
                    jnp.where(picks[2 * pair + 1], value, zero),
                ],
                axis=0,
            )
            start = part * len(blocks) * 8 + pair * 16
            ref[start:start + 16, column:column + 128] = both.astype(BF16)


OWN_BLOCKS = tuple(range(OWN_WIDE))
GX_BLOCKS = (OWN_WIDE, OWN_WIDE + 1, OWN_WIDE + 4, OWN_WIDE + 5)
GY_BLOCKS = (OWN_WIDE + 2, OWN_WIDE + 3)


def lane_hot(ref, low, rows):
    turned = jnp.transpose(low)
    along = iota((128, WIDE), 1)
    for row in range(rows):
        hot = jnp.broadcast_to(turned[:, row:row + 1], (128, WIDE)) == along
        ref[row * 128:(row + 1) * 128, :] = jnp.where(hot, 1.0, 0.0).astype(BF16)


def product(left, hot, blocks):
    total = jnp.dot(left[...], hot, preferred_element_type=F32)
    return total[:blocks * 8] + total[blocks * 8:]


def end_pulses(impulse, table, out, arm, sign):
    p0, p1, p2 = impulse
    get = lambda name: plane(table, PLANE[name])
    a0, a1 = get("a0"), get("a1")
    b0, b1, b2 = get("b0"), get("b1"), get("b2")
    force = (
        p0 * get("n0") + p1 * a0 + p2 * b0,
        p0 * get("n1") + p1 * a1 + p2 * b1,
        p0 * get("n2") + p2 * b2,
    )
    twist = (p1 * b0 - p2 * a0, p1 * b1 - p2 * a1, p1 * b2)
    arm = -get(arm)
    for comp in range(3):
        out[pl.ds(comp, ROWS, stride=8), :] = sign * force[comp]
        out[pl.ds(comp + 3, ROWS, stride=8), :] = arm * twist[comp]
    for comp in (6, 7):
        out[pl.ds(comp, ROWS, stride=8), :] = jnp.zeros((ROWS, 128), F32)


def spread_rows(left, values, high, blocks):
    for row in range(ROWS):
        value = values[row * 8:(row + 1) * 8, :]
        spread(left, high[row:row + 1, :], halves(value), blocks, row * 128)


def ghost_pulses(flags, far, high_far, hot_far, gx_sends, left_ghost):
    spread_rows(left_ghost, far, high_far, GX_BLOCKS)
    total = product(left_ghost, hot_far[...], len(GX_BLOCKS))
    send_gx(flags, total[:8], total[8:16], total[16:24, :128], gx_sends)


def ghost_faces(flags, far, high_far, hot_far, gy_faces, left_gy):
    spread_rows(left_gy, far, high_far, GY_BLOCKS)
    total = product(left_gy, hot_far[...], len(GY_BLOCKS))
    send_gy(flags, total[:8], total[8:], gy_faces)


def flag(flags, number, width=128):
    return jnp.broadcast_to(flags[number:number + 1, :1] > 0, (8, width))


def send_gx(flags, face0, face1, corners, sends):
    first, second = sends
    slot = iota((8, 128), 1) // CORNER
    to_down = (slot == 0) | (slot == 2)
    up = jnp.where(to_down | ~flag(flags, 0), 0.0, corners)
    down = jnp.where(to_down & flag(flags, 1), corners, 0.0)
    first[:, :FACE] = face1
    first[:, FACE:] = down
    second[:, :FACE] = face0
    second[:, FACE:] = up


def send_gy(flags, face2, face3, faces):
    wide = flag(flags, 6, FACE)
    faces[0][...] = jnp.where(wide, face3, face2)
    faces[1][...] = jnp.where(wide, face2, face3)


def prepare(
    flags, angles_in, arms_in, mu_in, bias_in, impulse_in, owner_in, other_in,
    radius_in, faces_in, corners_in, base_in,
    table, places, high_far, impulse, hot_far, far_values,
    gx_first, gx_second,
    owner, radius, faces, corners, base,
    angles, arms, mu, bias, other, flat, left_ghost, sems,
):
    copies = [
        pltpu.make_async_copy(source, target, sems.at[number])
        for number, (source, target) in enumerate((
            (other_in, other), (angles_in, angles), (arms_in, arms), (mu_in, mu),
            (bias_in, bias), (impulse_in, impulse), (owner_in, owner), (radius_in, radius),
            (faces_in, faces), (corners_in, corners), (base_in, base),
        ))
    ]
    for copy in copies:
        copy.start()
    copies[0].wait()
    far_id = other[...]
    extra = far_id - (BODY + 4 * FACE)
    block = extra >> 5
    slot = ((block & 1) << 1) | (block >> 1)
    in_block = extra & (CORNER - 1)
    is_corner = extra >= 0
    places[2 * ROWS:3 * ROWS, :] = far_id >> 7
    places[3 * ROWS:, :] = jnp.where(is_corner, slot * CORNER + in_block, far_id & 127)
    high_far[...] = far_id >> 8
    lane_hot(
        hot_far, jnp.where(is_corner, (3 - slot) * CORNER + in_block, far_id & 255), ROWS
    )
    for copy in copies[1:]:
        copy.wait()
    near_id = owner[...]
    places[:ROWS, :] = near_id >> 7
    places[ROWS:2 * ROWS, :] = near_id & 127
    for row in range(ROWS):
        cut = slice(row * 128, (row + 1) * 128)
        flat[pl.ds(row, 2, stride=ROWS), :] = angles[:, cut]
        flat[pl.ds(2 * ROWS + row, 2, stride=ROWS), :] = arms[:, cut]
    polar, azim = plane(flat, 0), plane(flat, 1)
    arm0, arm1 = plane(flat, 2), plane(flat, 3)
    cos_polar, sin_polar = jnp.cos(polar), jnp.sin(polar)
    cos_azim, sin_azim = jnp.cos(azim), jnp.sin(azim)
    cubed0 = arm0 * arm0 * arm0
    cubed1 = arm1 * arm1 * arm1
    values = {
        "n0": cos_polar * cos_azim, "n1": cos_polar * sin_azim, "n2": sin_polar,
        "a0": -sin_azim, "a1": cos_azim,
        "b0": -sin_polar * cos_azim, "b1": -sin_polar * sin_azim, "b2": cos_polar,
        "arm0": arm0, "arm1": arm1,
        "relax": RELAX / (1.0 / cubed0 + 1.0 / cubed1),
        "mu": mu[...], "bias": bias[...],
    }
    for name, value in values.items():
        number = PLANE[name]
        table[number * ROWS:(number + 1) * ROWS, :] = value
    end_pulses([plane(impulse, comp) for comp in range(3)], table, far_values, "arm1", -1.0)
    ghost_pulses(flags, far_values, high_far, hot_far, (gx_first, gx_second), left_ghost)


def prepare_own(
    flags, far_values, high_far, hot_far, impulse, table, owner, radius, faces, corners, base_rows,
    gy_first, gy_second, pulse, high_near, hot_near, hot_list, list_places, inverse, base,
    near_values, left_near, left_gy,
):
    ghost_faces(flags, far_values, high_far, hot_far, (gy_first, gy_second), left_gy)
    near_id = owner[...]
    high_near[...] = near_id >> 8
    lane_hot(hot_near, near_id & 255, ROWS)
    for number in range(4):
        for part in range(2):
            row = number * 2 + part
            list_places[row:row + 1, :] = faces[number:number + 1, part * 128:(part + 1) * 128]
    for place, number in enumerate((0, 2, 1, 3)):
        list_places[8:9, place * CORNER:(place + 1) * CORNER] = corners[number:number + 1, :]
    for place, number in enumerate((3, 1, 2, 0)):
        list_places[9:10, place * CORNER:(place + 1) * CORNER] = corners[number:number + 1, :]
    list_places[10:, :] = jnp.zeros((6, 128), I32)
    lane_hot(hot_list, list_places[...] & 255, LIST_ROWS)

    size = radius[...]
    cubed = size * size * size
    linear = 1.0 / cubed
    angular = 2.5 / (cubed * size * size)
    inverse[...] = jnp.where(iota((8, BODY), 0) < 3, linear, angular)
    for tile in range(OWN_TILES):
        base[:, tile * 128:(tile + 1) * 128] = base_rows[pl.ds(tile, 6, stride=OWN_TILES), :]
    near_pulses(impulse, table, high_near, hot_near, pulse, near_values, left_near)


def store_blocks(pulse, total):
    for block in range(OWN_WIDE):
        pulse[:, block * WIDE:(block + 1) * WIDE] = total[block * 8:block * 8 + 8]


def near_pulses(impulse, table, high_near, hot_near, pulse, values, left_near):
    end_pulses([plane(impulse, comp) for comp in range(3)], table, values, "arm0", 1.0)
    spread_rows(left_near, values, high_near, OWN_BLOCKS)
    store_blocks(pulse, product(left_near, hot_near[...], OWN_WIDE))


def scatter_near(
    flags, far_values, high_far, hot_far, impulse, table, high_near, hot_near,
    gy_first, gy_second, pulse, near_values, left_near, left_gy,
):
    ghost_faces(flags, far_values, high_far, hot_far, (gy_first, gy_second), left_gy)
    near_pulses(impulse, table, high_near, hot_near, pulse, near_values, left_near)


def masked(flags, number, value):
    return jnp.where(flags[number:number + 1, :] > 0, value, jnp.zeros_like(value))


def gx_tiles(flags, first, second):
    return [
        masked(flags, number, ref[:, part * 128:(part + 1) * 128])
        for number, ref in enumerate((first, second))
        for part in range(2)
    ]


def gy_tiles(flags, first, second):
    tiles = []
    for part in range(2):
        cut = slice(part * 128, (part + 1) * 128)
        one, two = first[:, cut], second[:, cut]
        tiles.append((jnp.where(flag(flags, 6), one, two), jnp.where(flag(flags, 6), two, one)))
    left, right = zip(*tiles)
    corners = jnp.where(flags[7:8, :] > 0, first[:, FACE:], second[:, FACE:])
    return (
        [masked(flags, 2, tile) for tile in left] + [masked(flags, 3, tile) for tile in right]
        + [masked(flags, 4, corners)]
    )


def list_product(left_list, tiles, list_places, hot, first):
    for row, tile in enumerate(tiles):
        high_row = list_places[first + row:first + row + 1, :] >> 8
        spread(left_list, high_row, halves(tile), OWN_BLOCKS, row * 128)
    rows = slice(first * 128, (first + len(tiles)) * 128)
    return product(left_list, hot[rows, :], OWN_WIDE)


def scatter_far(
    flags, values, high_far, hot_far, near_pulse, list_places, hot_list, from_up, from_down,
    pulse, left_far, left_list,
):
    spread_rows(left_far, values, high_far, OWN_BLOCKS)
    total = product(left_far, hot_far[...], OWN_WIDE)
    total = total + list_product(
        left_list, gx_tiles(flags, from_up, from_down), list_places, hot_list, 0
    )
    for block in range(OWN_WIDE):
        cut = slice(block * WIDE, (block + 1) * WIDE)
        pulse[:, cut] = near_pulse[:, cut] + total[block * 8:block * 8 + 8]


def settled(flags, own, inverse, base, list_places, hot_list, from_left, from_right, left_list):
    added = list_product(
        left_list, gy_tiles(flags, from_left, from_right), list_places, hot_list, 4
    )
    blocks = []
    for block in range(OWN_WIDE):
        cut = slice(block * WIDE, (block + 1) * WIDE)
        total = own[:6, cut] + added[block * 8:block * 8 + 6]
        blocks.append(base[:, cut] + inverse[:6, cut] * total)
    return blocks


def listed(velocity, list_places, row):
    entry = jnp.broadcast_to(list_places[row:row + 1, :], (8, 128))
    tile_id, lane = entry >> 7, entry & 127
    total = jnp.zeros((8, 128), F32)
    for tile in range(OWN_TILES):
        table = velocity[:, tile * 128:(tile + 1) * 128]
        total = jnp.where(tile_id == tile, lanes_of(table, lane), total)
    return total


def settle(
    flags, own, inverse, base, list_places, hot_list, from_left, from_right,
    velocity, gx_first, gx_second, left_list,
):
    blocks = settled(
        flags, own, inverse, base, list_places, hot_list, from_left, from_right, left_list
    )
    zero = jnp.zeros((2, WIDE), F32)
    for block, value in enumerate(blocks):
        velocity[:, block * WIDE:(block + 1) * WIDE] = jnp.concatenate([value, zero], axis=0)
    found = [listed(velocity, list_places, row) for row in (0, 1, 2, 3, 9)]
    face = [jnp.concatenate(found[2 * k:2 * k + 2], axis=1) for k in range(2)]
    send_gx(flags, *face, found[4], (gx_first, gx_second))


def settle_last(
    flags, own, inverse, base, list_places, hot_list, from_left, from_right,
    velocity, left_list,
):
    blocks = settled(
        flags, own, inverse, base, list_places, hot_list, from_left, from_right, left_list
    )
    for block, value in enumerate(blocks):
        for part in range(2):
            tile = 2 * block + part
            velocity[pl.ds(tile, 6, stride=OWN_TILES), :] = value[:, part * 128:(part + 1) * 128]


def pick(tables, tile_id, lane, firsts, totals):
    for tile, table in zip(firsts, tables):
        here = tile_id == tile
        for comp in range(6):
            row = jnp.broadcast_to(table[comp:comp + 1, :], (ROWS, 128))
            totals[comp] = jnp.where(here, lanes_of(row, lane), totals[comp])
    return totals


def own_tables(velocity):
    return [velocity[:, tile * 128:(tile + 1) * 128] for tile in range(OWN_TILES)]


def blank():
    return [jnp.zeros((ROWS, 128), F32) for _ in range(6)]


def gather_near(flags, velocity, places, list_places, near, gy_first, gy_second):
    tiles = [listed(velocity, list_places, row) for row in range(4, 8)]
    send_gy(
        flags, jnp.concatenate(tiles[:2], axis=1), jnp.concatenate(tiles[2:], axis=1),
        (gy_first, gy_second),
    )
    found = pick(
        own_tables(velocity), places[:ROWS, :], places[ROWS:2 * ROWS, :], range(OWN_TILES), blank()
    )
    for comp in range(6):
        near[comp * ROWS:(comp + 1) * ROWS, :] = found[comp]


def gather_far(flags, velocity, places, from_up, from_down, far):
    found = pick(
        own_tables(velocity) + gx_tiles(flags, from_up, from_down),
        places[2 * ROWS:3 * ROWS, :], places[3 * ROWS:, :], range(OWN_TILES + 4), blank(),
    )
    for comp in range(6):
        far[comp * ROWS:(comp + 1) * ROWS, :] = found[comp]


def sweep(
    flags, near_ref, far_ref, table, places, high_far, hot_far, impulse, from_left, from_right,
    impulse_out, far_values, gx_first, gx_second, left_ghost,
):
    near = [plane(near_ref, comp) for comp in range(6)]
    far = pick(
        gy_tiles(flags, from_left, from_right),
        places[2 * ROWS:3 * ROWS, :], places[3 * ROWS:, :],
        range(OWN_TILES + 4, OWN_TILES + 9), [plane(far_ref, comp) for comp in range(6)],
    )
    get = lambda name: plane(table, PLANE[name])
    n0, n1, n2 = get("n0"), get("n1"), get("n2")
    a0, a1 = get("a0"), get("a1")
    b0, b1, b2 = get("b0"), get("b1"), get("b2")
    arm0, arm1, relax, mu = get("arm0"), get("arm1"), get("relax"), get("mu")
    w0, w1, w2 = [near[c] - far[c] for c in range(3)]
    s0, s1, s2 = [arm0 * near[c] + arm1 * far[c] for c in range(3, 6)]
    rate_n = n0 * w0 + n1 * w1 + n2 * w2
    rate_a = (a0 * w0 + a1 * w1) - (b0 * s0 + b1 * s1 + b2 * s2)
    rate_b = (b0 * w0 + b1 * w1 + b2 * w2) + (a0 * s0 + a1 * s1)
    trial_n = plane(impulse, 0) - relax * (rate_n + get("bias"))
    trial_a = plane(impulse, 1) - relax * rate_a
    trial_b = plane(impulse, 2) - relax * rate_b
    length = jnp.sqrt(trial_a * trial_a + trial_b * trial_b)
    inside = length <= mu * trial_n
    dead = mu * length <= -trial_n
    level = (trial_n + mu * length) / (1.0 + mu * mu)
    factor = mu * level / jnp.maximum(length, SMALLEST)
    choose = lambda kept, cone: jnp.where(inside, kept, jnp.where(dead, 0.0, cone))
    fresh = [
        choose(trial_n, level), choose(trial_a, factor * trial_a), choose(trial_b, factor * trial_b)
    ]
    for comp in range(3):
        impulse_out[comp * ROWS:(comp + 1) * ROWS, :] = fresh[comp]
    end_pulses(fresh, table, far_values, "arm1", -1.0)
    ghost_pulses(flags, far_values, high_far, hot_far, (gx_first, gx_second), left_ghost)


def shape(*dims, kind=F32):
    return jax.ShapeDtypeStruct(dims, kind)


FACES = (shape(8, FACE), shape(8, FACE))
GX_SENDS = (shape(8, MESSAGE), shape(8, MESSAGE))
VALUES = shape(8 * ROWS, 128)
PULSE = shape(8, BODY)
LEFT_OWN = pltpu.VMEM((2 * OWN_WIDE * 8, CONTACTS), BF16)
LEFT_GHOST = pltpu.VMEM((2 * len(GX_BLOCKS) * 8, CONTACTS), BF16)
NEAR = (
    pltpu.VMEM((8 * ROWS, 128), F32), LEFT_OWN, pltpu.VMEM((2 * len(GY_BLOCKS) * 8, CONTACTS), BF16)
)


def left_list(tiles):
    return pltpu.VMEM((2 * OWN_WIDE * 8, tiles * 128), BF16)


def call(body, outs, scratch, *operands, specs=None):
    vmem = pl.BlockSpec(memory_space=pltpu.VMEM)
    return pl.pallas_call(
        body,
        out_shape=outs,
        in_specs=specs or [vmem] * len(operands),
        out_specs=[vmem] * len(outs),
        scratch_shapes=scratch,
        compiler_params=pltpu.CompilerParams(vmem_limit_bytes=10 * 1024 * 1024),
    )(*operands)


def loop(value, back, lines, place):
    count, length = lines
    pairs = []
    for line in range(0, count, 2):
        ring = [place(line, step) for step in range(length)]
        ring += [place(line + 1, step) for step in reversed(range(length))]
        for here, there in zip(ring, ring[1:] + ring[:1]):
            pairs.append((there, here) if back else (here, there))
    return lax.ppermute(value, ("gx", "gy"), pairs)


def along_gx(first, second):
    size = lax.axis_size("gx")
    down = [(i, (i + 1) % size) for i in range(size)]
    up = [(j, i) for i, j in down]
    return lax.ppermute(first, "gx", down), lax.ppermute(second, "gx", up)


def along_gy(got_first, got_second, face_first, face_second):
    rows, columns = lax.axis_size("gx"), lax.axis_size("gy")
    corners = got_first[:, FACE:] + got_second[:, FACE:]
    first = jnp.concatenate([face_first, corners], axis=1)
    second = jnp.concatenate([face_second, corners], axis=1)
    place = lambda line, step: line * columns + step
    lines = (rows, columns)
    return loop(first, False, lines, place), loop(second, True, lines, place)


def presence():
    row_at, row_count = lax.axis_index("gx"), lax.axis_size("gx")
    col_at, col_count = lax.axis_index("gy"), lax.axis_size("gy")
    row, slot = iota((8, 128), 0), iota((8, 128), 1) // CORNER
    above = (row == 0) | ((row == 4) & ((slot == 0) | (slot == 2)))
    below = (row == 1) | ((row == 4) & ((slot == 1) | (slot == 3)))
    before = (row == 2) | ((row == 4) & (slot < 2))
    after = (row == 3) | ((row == 4) & (slot >= 2))
    odd_row = lax.rem(row_at, 2)
    off = (
        (above & (row_at == 0)) | (below & (row_at == row_count - 1))
        | (before & (col_at == 0)) | (after & (col_at == col_count - 1))
        | ((row == 6) & (odd_row == 1))
        | ((row == 7) & ((slot >> 1) != odd_row))
    )
    return jnp.where(off, 0.0, 1.0)


def shards(
    free_velocity, body_radius, face_lists, corner_lists, owner_body, other_body,
    contact_angles, contact_arms, friction, approach, start_impulse,
):
    flags = presence()
    in_rows = lambda value: value[0, 0].reshape(-1, 128)
    dma = pltpu.SemaphoreType.DMA
    raw = [
        pltpu.with_memory_space_constraint(value, pltpu.HBM)
        for value in (
            contact_angles[0, 0], contact_arms[0, 0], in_rows(friction), in_rows(approach),
            in_rows(start_impulse), in_rows(owner_body), in_rows(other_body),
            body_radius[0], face_lists[0, 0], corner_lists[0, 0], in_rows(free_velocity),
        )
    ]
    (
        table, places, high_far, impulse, hot_far, far_values,
        gx_first, gx_second, owner, radius, faces, corners, base_rows,
    ) = call(
        prepare,
        (
            shape(len(PLANES) * ROWS, 128),
            shape(4 * ROWS, 128, kind=I32),
            shape(ROWS, 128, kind=I32),
            shape(IMPULSE_ROWS, 128),
            shape(CONTACTS, WIDE, kind=BF16),
            VALUES,
        ) + GX_SENDS + (
            shape(ROWS, 128, kind=I32),
            shape(1, BODY),
            shape(4, FACE, kind=I32),
            shape(4, CORNER, kind=I32),
            shape(6 * OWN_TILES, 128),
        ),
        (
            pltpu.VMEM((2, CONTACTS), F32),
            pltpu.VMEM((2, CONTACTS), F32),
            pltpu.VMEM((ROWS, 128), F32),
            pltpu.VMEM((ROWS, 128), F32),
            pltpu.VMEM((ROWS, 128), I32),
            pltpu.VMEM((4 * ROWS, 128), F32),
            LEFT_GHOST,
            dma((11,)),
        ),
        flags, *raw,
        specs=[pl.BlockSpec(memory_space=pltpu.VMEM)]
        + [pl.BlockSpec(memory_space=pltpu.HBM)] * len(raw),
    )
    for number in range(SWEEPS + 1):
        got = along_gx(gx_first, gx_second)
        if number == 0:
            gy_first, gy_second, pulse, high_near, hot_near, hot_list, list_places, inverse, base = call(
                prepare_own,
                FACES + (
                    PULSE,
                    shape(ROWS, 128, kind=I32),
                    shape(CONTACTS, WIDE, kind=BF16),
                    shape(LISTED, WIDE, kind=BF16),
                    shape(16, 128, kind=I32),
                    PULSE,
                    shape(6, BODY),
                ),
                NEAR,
                flags, far_values, high_far, hot_far, impulse, table,
                owner, radius, faces, corners, base_rows,
            )
        else:
            gy_first, gy_second, pulse = call(
                scatter_near, FACES + (PULSE,), NEAR,
                flags, far_values, high_far, hot_far, impulse, table, high_near, hot_near,
            )
        got_gy = along_gy(*got, gy_first, gy_second)
        (own,) = call(
            scatter_far, (PULSE,), (LEFT_OWN, left_list(4)),
            flags, far_values, high_far, hot_far, pulse, list_places, hot_list, *got,
        )
        fixed = (flags, own, inverse, base, list_places, hot_list, *got_gy)
        if number == SWEEPS:
            (velocity,) = call(
                settle_last, (shape(6 * OWN_TILES, 128),), (left_list(5),), *fixed
            )
            break
        velocity, gx_first, gx_second = call(
            settle, (PULSE,) + GX_SENDS, (left_list(5),), *fixed
        )
        got = along_gx(gx_first, gx_second)
        near, gy_first, gy_second = call(
            gather_near, (shape(6 * ROWS, 128),) + FACES, (), flags, velocity, places, list_places
        )
        got_gy = along_gy(*got, gy_first, gy_second)
        (far,) = call(
            gather_far, (shape(6 * ROWS, 128),), (), flags, velocity, places, *got
        )
        impulse, far_values, gx_first, gx_second = call(
            sweep, (shape(IMPULSE_ROWS, 128), VALUES) + GX_SENDS, (LEFT_GHOST,),
            flags, near, far, table, places, high_far, hot_far, impulse, *got_gy,
        )
    return velocity.reshape(1, 1, 6, BODY), impulse.reshape(1, 1, 3, CONTACTS)

def solution(mesh):
    in_specs = (
        P("gx", "gy", None, None),
        P("gx", "gy", None),
        P("gx", "gy", None, None),
        P("gx", "gy", None, None),
        P("gx", "gy", None),
        P("gx", "gy", None),
        P("gx", "gy", None, None),
        P("gx", "gy", None, None),
        P("gx", "gy", None),
        P("gx", "gy", None),
        P("gx", "gy", None, None),
    )
    out_specs = (P("gx", "gy", None, None), P("gx", "gy", None, None))
    return jax.shard_map(shards, mesh=mesh, in_specs=in_specs, out_specs=out_specs, check_vma=False)
```

```python
import jax
import jax.numpy as jnp
from jax import lax
from jax.experimental import pallas as pl
from jax.experimental.pallas import tpu as pltpu
from jax.sharding import PartitionSpec as P

SWEEPS = 4
SWAPS = (False, True, False, True, False, True, False, True, False, False)
RELAX = 0.25
SMALLEST = 1e-20

BODY = 2048
FACE = 256
CORNER = 32
CONTACTS = 4096
ROWS = CONTACTS // 128
LISTED = 4 * FACE + 4 * CORNER
LIST_ROWS = LISTED // 128
OWN_TILES = BODY // 128
WIDE = 256
OWN_WIDE = BODY // WIDE
GHOST_WIDE = 6
IMPULSE_ROWS = 3 * ROWS
MESSAGE = FACE + 128

F32 = jnp.float32
BF16 = jnp.bfloat16
I32 = jnp.int32

PLANES = (
    "n0", "n1", "n2", "a0", "a1", "b0", "b1", "b2",
    "arm0", "arm1", "relax", "mu", "bias",
)
PLANE = {name: place for place, name in enumerate(PLANES)}


def lanes_of(table, lane):
    numbers = lax.GatherDimensionNumbers(
        offset_dims=(),
        collapsed_slice_dims=(1,),
        start_index_map=(1,),
        operand_batching_dims=(0,),
        start_indices_batching_dims=(0,),
    )
    return lax.gather(
        table, lane[..., None], numbers, (1, 1),
        mode=lax.GatherScatterMode.PROMISE_IN_BOUNDS,
    )


def iota(shape, dim):
    return lax.broadcasted_iota(I32, shape, dim)


def halves(values):
    high = values.astype(BF16).astype(F32)
    return high, values - high


def plane(ref, number):
    return ref[number * ROWS:(number + 1) * ROWS, :]


def spread(ref, high_row, parts, blocks, column):
    picks = [high_row == block for block in blocks]
    for part, value in enumerate(parts):
        zero = jnp.zeros_like(value)
        for pair in range(len(blocks) // 2):
            both = jnp.concatenate(
                [
                    jnp.where(picks[2 * pair], value, zero),
                    jnp.where(picks[2 * pair + 1], value, zero),
                ],
                axis=0,
            )
            start = part * len(blocks) * 8 + pair * 16
            ref[start:start + 16, column:column + 128] = both.astype(BF16)


OWN_BLOCKS = tuple(range(OWN_WIDE))
GHOST_BLOCKS = tuple(range(OWN_WIDE, OWN_WIDE + GHOST_WIDE))


def lane_hot(ref, low, rows):
    turned = jnp.transpose(low)
    along = iota((128, WIDE), 1)
    for row in range(rows):
        hot = jnp.broadcast_to(turned[:, row:row + 1], (128, WIDE)) == along
        ref[row * 128:(row + 1) * 128, :] = jnp.where(hot, 1.0, 0.0).astype(BF16)


def product(left, hot, blocks):
    total = jnp.dot(left[...], hot, preferred_element_type=F32)
    return total[:blocks * 8] + total[blocks * 8:]


def end_pulses(impulse, table, near_out, far_out):
    p0, p1, p2 = impulse
    get = lambda name: plane(table, PLANE[name])
    a0, a1 = get("a0"), get("a1")
    b0, b1, b2 = get("b0"), get("b1"), get("b2")
    force = (
        p0 * get("n0") + p1 * a0 + p2 * b0,
        p0 * get("n1") + p1 * a1 + p2 * b1,
        p0 * get("n2") + p2 * b2,
    )
    twist = (p1 * b0 - p2 * a0, p1 * b1 - p2 * a1, p1 * b2)
    arm0, arm1 = -get("arm0"), -get("arm1")
    for comp in range(3):
        near_out[pl.ds(comp, ROWS, stride=8), :] = force[comp]
        far_out[pl.ds(comp, ROWS, stride=8), :] = -force[comp]
        near_out[pl.ds(comp + 3, ROWS, stride=8), :] = arm0 * twist[comp]
        far_out[pl.ds(comp + 3, ROWS, stride=8), :] = arm1 * twist[comp]
    for comp in (6, 7):
        near_out[pl.ds(comp, ROWS, stride=8), :] = jnp.zeros((ROWS, 128), F32)
        far_out[pl.ds(comp, ROWS, stride=8), :] = jnp.zeros((ROWS, 128), F32)


def spread_rows(left, values, high, blocks):
    for row in range(ROWS):
        value = values[row * 8:(row + 1) * 8, :]
        spread(left, high[row:row + 1, :], halves(value), blocks, row * 128)


def ghost_pulses(flags, far, high_far, hot_far, gx_sends, gy_faces, left_ghost):
    spread_rows(left_ghost, far, high_far, GHOST_BLOCKS)
    total = product(left_ghost, hot_far[...], GHOST_WIDE)
    ghost = [total[block * 8:block * 8 + 8] for block in range(5)]
    send_gx(flags, ghost[0], ghost[1], ghost[4][:, :128], gx_sends)
    send_gy(flags, ghost[2], ghost[3], gy_faces)


def flag(flags, number, width=128):
    return jnp.broadcast_to(flags[number:number + 1, :1] > 0, (8, width))


def send_gx(flags, face0, face1, corners, sends):
    first, second = sends
    slot = iota((8, 128), 1) // CORNER
    to_down = (slot == 0) | (slot == 2)
    up = jnp.where(to_down | ~flag(flags, 0), 0.0, corners)
    down = jnp.where(to_down & flag(flags, 1), corners, 0.0)
    ahead, wide = flag(flags, 5), flag(flags, 5, FACE)
    first[:, :FACE] = jnp.where(wide, face1, face0)
    first[:, FACE:] = jnp.where(ahead, down, up)
    second[:, :FACE] = jnp.where(wide, face0, face1)
    second[:, FACE:] = jnp.where(ahead, up, down)


def send_gy(flags, face2, face3, faces):
    wide = flag(flags, 6, FACE)
    faces[0][...] = jnp.where(wide, face3, face2)
    faces[1][...] = jnp.where(wide, face2, face3)


def prepare(
    flags, angles_in, arms_in, mu_in, bias_in, impulse_in, owner_in, other_in,
    radius_in, faces_in, corners_in, base_in,
    table, places, high_far, impulse, hot_far, near_values, far_values,
    gx_first, gx_second, gy_first, gy_second,
    owner, radius, faces, corners, base,
    angles, arms, mu, bias, other, flat, left_ghost, sems,
):
    copies = [
        pltpu.make_async_copy(source, target, sems.at[number])
        for number, (source, target) in enumerate((
            (other_in, other), (angles_in, angles), (arms_in, arms), (mu_in, mu),
            (bias_in, bias), (impulse_in, impulse), (owner_in, owner), (radius_in, radius),
            (faces_in, faces), (corners_in, corners), (base_in, base),
        ))
    ]
    for copy in copies:
        copy.start()
    copies[0].wait()
    far_id = other[...]
    extra = far_id - (BODY + 4 * FACE)
    block = extra >> 5
    slot = ((block & 1) << 1) | (block >> 1)
    in_block = extra & (CORNER - 1)
    is_corner = extra >= 0
    places[2 * ROWS:3 * ROWS, :] = far_id >> 7
    places[3 * ROWS:, :] = jnp.where(is_corner, slot * CORNER + in_block, far_id & 127)
    high_far[...] = far_id >> 8
    lane_hot(
        hot_far, jnp.where(is_corner, (3 - slot) * CORNER + in_block, far_id & 255), ROWS
    )
    for copy in copies[1:]:
        copy.wait()
    near_id = owner[...]
    places[:ROWS, :] = near_id >> 7
    places[ROWS:2 * ROWS, :] = near_id & 127
    for row in range(ROWS):
        cut = slice(row * 128, (row + 1) * 128)
        flat[pl.ds(row, 2, stride=ROWS), :] = angles[:, cut]
        flat[pl.ds(2 * ROWS + row, 2, stride=ROWS), :] = arms[:, cut]
    polar, azim = plane(flat, 0), plane(flat, 1)
    arm0, arm1 = plane(flat, 2), plane(flat, 3)
    cos_polar, sin_polar = jnp.cos(polar), jnp.sin(polar)
    cos_azim, sin_azim = jnp.cos(azim), jnp.sin(azim)
    cubed0 = arm0 * arm0 * arm0
    cubed1 = arm1 * arm1 * arm1
    values = {
        "n0": cos_polar * cos_azim, "n1": cos_polar * sin_azim, "n2": sin_polar,
        "a0": -sin_azim, "a1": cos_azim,
        "b0": -sin_polar * cos_azim, "b1": -sin_polar * sin_azim, "b2": cos_polar,
        "arm0": arm0, "arm1": arm1,
        "relax": RELAX / (1.0 / cubed0 + 1.0 / cubed1),
        "mu": mu[...], "bias": bias[...],
    }
    for name, value in values.items():
        number = PLANE[name]
        table[number * ROWS:(number + 1) * ROWS, :] = value
    end_pulses([plane(impulse, comp) for comp in range(3)], table, near_values, far_values)
    ghost_pulses(
        flags, far_values, high_far, hot_far, (gx_first, gx_second), (gy_first, gy_second), left_ghost
    )


def prepare_own(
    near_values, owner, radius, faces, corners, base_rows,
    pulse, high_near, hot_near, hot_list, list_places, inverse, base,
    left_near,
):
    near_id = owner[...]
    high_near[...] = near_id >> 8
    lane_hot(hot_near, near_id & 255, ROWS)
    for number in range(4):
        for part in range(2):
            row = number * 2 + part
            list_places[row:row + 1, :] = faces[number:number + 1, part * 128:(part + 1) * 128]
    for place, number in enumerate((0, 2, 1, 3)):
        list_places[8:9, place * CORNER:(place + 1) * CORNER] = corners[number:number + 1, :]
    for place, number in enumerate((3, 1, 2, 0)):
        list_places[9:10, place * CORNER:(place + 1) * CORNER] = corners[number:number + 1, :]
    list_places[10:, :] = jnp.zeros((6, 128), I32)
    lane_hot(hot_list, list_places[...] & 255, LIST_ROWS)

    size = radius[...]
    cubed = size * size * size
    linear = 1.0 / cubed
    angular = 2.5 / (cubed * size * size)
    inverse[...] = jnp.where(iota((8, BODY), 0) < 3, linear, angular)
    for tile in range(OWN_TILES):
        base[:, tile * 128:(tile + 1) * 128] = base_rows[pl.ds(tile, 6, stride=OWN_TILES), :]
    scatter_near(near_values, high_near, hot_near, pulse, left_near)


def store_blocks(pulse, total):
    for block in range(OWN_WIDE):
        pulse[:, block * WIDE:(block + 1) * WIDE] = total[block * 8:block * 8 + 8]


def scatter_near(values, high_near, hot_near, pulse, left_near):
    spread_rows(left_near, values, high_near, OWN_BLOCKS)
    store_blocks(pulse, product(left_near, hot_near[...], OWN_WIDE))


def masked(flags, number, value):
    return jnp.where(flags[number:number + 1, :] > 0, value, jnp.zeros_like(value))


def gx_tiles(flags, first, second):
    from_above = jnp.broadcast_to(flags[5:6, 127:] > 0, (8, 128))
    tiles = []
    for part in range(2):
        cut = slice(part * 128, (part + 1) * 128)
        one, two = first[:, cut], second[:, cut]
        tiles.append((jnp.where(from_above, one, two), jnp.where(from_above, two, one)))
    up, down = zip(*tiles)
    return [masked(flags, 0, tile) for tile in up] + [masked(flags, 1, tile) for tile in down]


def gy_tiles(flags, first, second):
    tiles = []
    for part in range(2):
        cut = slice(part * 128, (part + 1) * 128)
        one, two = first[:, cut], second[:, cut]
        tiles.append((jnp.where(flag(flags, 6), one, two), jnp.where(flag(flags, 6), two, one)))
    left, right = zip(*tiles)
    corners = jnp.where(flags[7:8, :] > 0, first[:, FACE:], second[:, FACE:])
    return (
        [masked(flags, 2, tile) for tile in left] + [masked(flags, 3, tile) for tile in right]
        + [masked(flags, 4, corners)]
    )


def list_product(left_list, tiles, list_places, hot, first):
    for row, tile in enumerate(tiles):
        high_row = list_places[first + row:first + row + 1, :] >> 8
        spread(left_list, high_row, halves(tile), OWN_BLOCKS, row * 128)
    rows = slice(first * 128, (first + len(tiles)) * 128)
    return product(left_list, hot[rows, :], OWN_WIDE)


def scatter_far(
    flags, values, high_far, hot_far, near_pulse, list_places, hot_list, from_up, from_down,
    pulse, left_far, left_list,
):
    spread_rows(left_far, values, high_far, OWN_BLOCKS)
    total = product(left_far, hot_far[...], OWN_WIDE)
    total = total + list_product(
        left_list, gx_tiles(flags, from_up, from_down), list_places, hot_list, 0
    )
    for block in range(OWN_WIDE):
        cut = slice(block * WIDE, (block + 1) * WIDE)
        pulse[:, cut] = near_pulse[:, cut] + total[block * 8:block * 8 + 8]


def settled(flags, own, inverse, base, list_places, hot_list, from_left, from_right, left_list):
    added = list_product(
        left_list, gy_tiles(flags, from_left, from_right), list_places, hot_list, 4
    )
    blocks = []
    for block in range(OWN_WIDE):
        cut = slice(block * WIDE, (block + 1) * WIDE)
        total = own[:6, cut] + added[block * 8:block * 8 + 6]
        blocks.append(base[:, cut] + inverse[:6, cut] * total)
    return blocks


def listed(velocity, list_places, row):
    entry = jnp.broadcast_to(list_places[row:row + 1, :], (8, 128))
    tile_id, lane = entry >> 7, entry & 127
    total = jnp.zeros((8, 128), F32)
    for tile in range(OWN_TILES):
        table = velocity[:, tile * 128:(tile + 1) * 128]
        total = jnp.where(tile_id == tile, lanes_of(table, lane), total)
    return total


def settle(
    flags, own, inverse, base, list_places, hot_list, from_left, from_right,
    velocity, gx_first, gx_second, left_list,
):
    blocks = settled(
        flags, own, inverse, base, list_places, hot_list, from_left, from_right, left_list
    )
    zero = jnp.zeros((2, WIDE), F32)
    for block, value in enumerate(blocks):
        velocity[:, block * WIDE:(block + 1) * WIDE] = jnp.concatenate([value, zero], axis=0)
    found = [listed(velocity, list_places, row) for row in (0, 1, 2, 3, 9)]
    face = [jnp.concatenate(found[2 * k:2 * k + 2], axis=1) for k in range(2)]
    send_gx(flags, *face, found[4], (gx_first, gx_second))


def settle_last(
    flags, own, inverse, base, list_places, hot_list, from_left, from_right,
    velocity, left_list,
):
    blocks = settled(
        flags, own, inverse, base, list_places, hot_list, from_left, from_right, left_list
    )
    for block, value in enumerate(blocks):
        for part in range(2):
            tile = 2 * block + part
            velocity[pl.ds(tile, 6, stride=OWN_TILES), :] = value[:, part * 128:(part + 1) * 128]


def pick(tables, tile_id, lane, firsts, totals):
    for tile, table in zip(firsts, tables):
        here = tile_id == tile
        for comp in range(6):
            row = jnp.broadcast_to(table[comp:comp + 1, :], (ROWS, 128))
            totals[comp] = jnp.where(here, lanes_of(row, lane), totals[comp])
    return totals


def own_tables(velocity):
    return [velocity[:, tile * 128:(tile + 1) * 128] for tile in range(OWN_TILES)]


def blank():
    return [jnp.zeros((ROWS, 128), F32) for _ in range(6)]


def gather_near(flags, velocity, places, list_places, near, gy_first, gy_second):
    tiles = [listed(velocity, list_places, row) for row in range(4, 8)]
    send_gy(
        flags, jnp.concatenate(tiles[:2], axis=1), jnp.concatenate(tiles[2:], axis=1),
        (gy_first, gy_second),
    )
    found = pick(
        own_tables(velocity), places[:ROWS, :], places[ROWS:2 * ROWS, :], range(OWN_TILES), blank()
    )
    for comp in range(6):
        near[comp * ROWS:(comp + 1) * ROWS, :] = found[comp]


def gather_far(flags, velocity, places, from_up, from_down, far):
    found = pick(
        own_tables(velocity) + gx_tiles(flags, from_up, from_down),
        places[2 * ROWS:3 * ROWS, :], places[3 * ROWS:, :], range(OWN_TILES + 4), blank(),
    )
    for comp in range(6):
        far[comp * ROWS:(comp + 1) * ROWS, :] = found[comp]


def sweep(
    flags, near_ref, far_ref, table, places, high_far, hot_far, impulse, from_left, from_right,
    impulse_out, near_values, far_values, gx_first, gx_second, gy_first, gy_second, left_ghost,
):
    near = [plane(near_ref, comp) for comp in range(6)]
    far = pick(
        gy_tiles(flags, from_left, from_right),
        places[2 * ROWS:3 * ROWS, :], places[3 * ROWS:, :],
        range(OWN_TILES + 4, OWN_TILES + 9), [plane(far_ref, comp) for comp in range(6)],
    )
    get = lambda name: plane(table, PLANE[name])
    n0, n1, n2 = get("n0"), get("n1"), get("n2")
    a0, a1 = get("a0"), get("a1")
    b0, b1, b2 = get("b0"), get("b1"), get("b2")
    arm0, arm1, relax, mu = get("arm0"), get("arm1"), get("relax"), get("mu")
    w0, w1, w2 = [near[c] - far[c] for c in range(3)]
    s0, s1, s2 = [arm0 * near[c] + arm1 * far[c] for c in range(3, 6)]
    rate_n = n0 * w0 + n1 * w1 + n2 * w2
    rate_a = (a0 * w0 + a1 * w1) - (b0 * s0 + b1 * s1 + b2 * s2)
    rate_b = (b0 * w0 + b1 * w1 + b2 * w2) + (a0 * s0 + a1 * s1)
    trial_n = plane(impulse, 0) - relax * (rate_n + get("bias"))
    trial_a = plane(impulse, 1) - relax * rate_a
    trial_b = plane(impulse, 2) - relax * rate_b
    length = jnp.sqrt(trial_a * trial_a + trial_b * trial_b)
    inside = length <= mu * trial_n
    dead = mu * length <= -trial_n
    level = (trial_n + mu * length) / (1.0 + mu * mu)
    factor = mu * level / jnp.maximum(length, SMALLEST)
    choose = lambda kept, cone: jnp.where(inside, kept, jnp.where(dead, 0.0, cone))
    fresh = [
        choose(trial_n, level), choose(trial_a, factor * trial_a), choose(trial_b, factor * trial_b)
    ]
    for comp in range(3):
        impulse_out[comp * ROWS:(comp + 1) * ROWS, :] = fresh[comp]
    end_pulses(fresh, table, near_values, far_values)
    ghost_pulses(
        flags, far_values, high_far, hot_far, (gx_first, gx_second), (gy_first, gy_second), left_ghost
    )


def shape(*dims, kind=F32):
    return jax.ShapeDtypeStruct(dims, kind)


FACES = (shape(8, FACE), shape(8, FACE))
GX_SENDS = (shape(8, MESSAGE), shape(8, MESSAGE))
VALUES = shape(8 * ROWS, 128)
PULSE = shape(8, BODY)
LEFT_OWN = pltpu.VMEM((2 * OWN_WIDE * 8, CONTACTS), BF16)
LEFT_GHOST = pltpu.VMEM((2 * GHOST_WIDE * 8, CONTACTS), BF16)


def left_list(tiles):
    return pltpu.VMEM((2 * OWN_WIDE * 8, tiles * 128), BF16)


def call(body, outs, scratch, *operands, specs=None):
    vmem = pl.BlockSpec(memory_space=pltpu.VMEM)
    return pl.pallas_call(
        body,
        out_shape=outs,
        in_specs=specs or [vmem] * len(operands),
        out_specs=[vmem] * len(outs),
        scratch_shapes=scratch,
        compiler_params=pltpu.CompilerParams(vmem_limit_bytes=10 * 1024 * 1024),
    )(*operands)


def loop(value, back, lines, place):
    count, length = lines
    pairs = []
    for line in range(0, count, 2):
        ring = [place(line, step) for step in range(length)]
        ring += [place(line + 1, step) for step in reversed(range(length))]
        for here, there in zip(ring, ring[1:] + ring[:1]):
            pairs.append((there, here) if back else (here, there))
    return lax.ppermute(value, ("gx", "gy"), pairs)


def along_gx(swap, first, second):
    rows, columns = lax.axis_size("gx"), lax.axis_size("gy")
    if not swap:
        down = [(i, (i + 1) % rows) for i in range(rows)]
        up = [(j, i) for i, j in down]
        return lax.ppermute(first, "gx", down), lax.ppermute(second, "gx", up)
    outer, inner = [], []
    for row in range(rows):
        for column in range(columns):
            here = row * columns + column
            near = row ^ 1
            far = row - 1 if row % 2 == 0 else row + 1
            inner.append((here, near * columns + column))
            if 0 <= far < rows:
                outer.append((here, far * columns + column))
            else:
                outer.append((here, row * columns + (column ^ 1)))
    axes = ("gx", "gy")
    return lax.ppermute(first, axes, outer), lax.ppermute(second, axes, inner)


def along_gy(got_first, got_second, face_first, face_second):
    rows, columns = lax.axis_size("gx"), lax.axis_size("gy")
    corners = got_first[:, FACE:] + got_second[:, FACE:]
    first = jnp.concatenate([face_first, corners], axis=1)
    second = jnp.concatenate([face_second, corners], axis=1)
    place = lambda line, step: line * columns + step
    lines = (rows, columns)
    return loop(first, False, lines, place), loop(second, True, lines, place)


def presence(swap):
    row_at, row_count = lax.axis_index("gx"), lax.axis_size("gx")
    col_at, col_count = lax.axis_index("gy"), lax.axis_size("gy")
    row, slot = iota((8, 128), 0), iota((8, 128), 1) // CORNER
    above = (row == 0) | ((row == 4) & ((slot == 0) | (slot == 2)))
    below = (row == 1) | ((row == 4) & ((slot == 1) | (slot == 3)))
    before = (row == 2) | ((row == 4) & (slot < 2))
    after = (row == 3) | ((row == 4) & (slot >= 2))
    odd_row = lax.rem(row_at, 2)
    off = (
        (above & (row_at == 0)) | (below & (row_at == row_count - 1))
        | (before & (col_at == 0)) | (after & (col_at == col_count - 1))
        | ((row == 6) & (odd_row == 1))
        | ((row == 5) & (swap & ((slot >> 1) == odd_row)))
        | ((row == 7) & ((slot >> 1) != odd_row))
    )
    return jnp.where(off, 0.0, 1.0)


def shards(
    free_velocity, body_radius, face_lists, corner_lists, owner_body, other_body,
    contact_angles, contact_arms, friction, approach, start_impulse,
):
    kinds = [presence(swap) for swap in (False, True)]
    in_rows = lambda value: value[0, 0].reshape(-1, 128)
    dma = pltpu.SemaphoreType.DMA
    raw = [
        pltpu.with_memory_space_constraint(value, pltpu.HBM)
        for value in (
            contact_angles[0, 0], contact_arms[0, 0], in_rows(friction), in_rows(approach),
            in_rows(start_impulse), in_rows(owner_body), in_rows(other_body),
            body_radius[0], face_lists[0, 0], corner_lists[0, 0], in_rows(free_velocity),
        )
    ]
    (
        table, places, high_far, impulse, hot_far, near_values, far_values,
        gx_first, gx_second, gy_first, gy_second, owner, radius, faces, corners, base_rows,
    ) = call(
        prepare,
        (
            shape(len(PLANES) * ROWS, 128),
            shape(4 * ROWS, 128, kind=I32),
            shape(ROWS, 128, kind=I32),
            shape(IMPULSE_ROWS, 128),
            shape(CONTACTS, WIDE, kind=BF16),
            VALUES, VALUES,
        ) + GX_SENDS + FACES + (
            shape(ROWS, 128, kind=I32),
            shape(1, BODY),
            shape(4, FACE, kind=I32),
            shape(4, CORNER, kind=I32),
            shape(6 * OWN_TILES, 128),
        ),
        (
            pltpu.VMEM((2, CONTACTS), F32),
            pltpu.VMEM((2, CONTACTS), F32),
            pltpu.VMEM((ROWS, 128), F32),
            pltpu.VMEM((ROWS, 128), F32),
            pltpu.VMEM((ROWS, 128), I32),
            pltpu.VMEM((4 * ROWS, 128), F32),
            LEFT_GHOST,
            dma((11,)),
        ),
        kinds[SWAPS[0]], *raw,
        specs=[pl.BlockSpec(memory_space=pltpu.VMEM)]
        + [pl.BlockSpec(memory_space=pltpu.HBM)] * len(raw),
    )
    for number in range(SWEEPS + 1):
        back, fetch = SWAPS[2 * number:2 * number + 2]
        follow = SWAPS[2 * number + 2] if number < SWEEPS else False
        got = along_gx(back, gx_first, gx_second)
        if number == 0:
            pulse, high_near, hot_near, hot_list, list_places, inverse, base = call(
                prepare_own,
                (
                    PULSE,
                    shape(ROWS, 128, kind=I32),
                    shape(CONTACTS, WIDE, kind=BF16),
                    shape(LISTED, WIDE, kind=BF16),
                    shape(16, 128, kind=I32),
                    PULSE,
                    shape(6, BODY),
                ),
                (LEFT_OWN,),
                near_values, owner, radius, faces, corners, base_rows,
            )
        else:
            (pulse,) = call(
                scatter_near, (PULSE,), (LEFT_OWN,), near_values, high_near, hot_near
            )
        got_gy = along_gy(*got, gy_first, gy_second)
        (own,) = call(
            scatter_far, (PULSE,), (LEFT_OWN, left_list(4)),
            kinds[back], far_values, high_far, hot_far, pulse, list_places, hot_list, *got,
        )
        fixed = (kinds[fetch], own, inverse, base, list_places, hot_list, *got_gy)
        if number == SWEEPS:
            (velocity,) = call(
                settle_last, (shape(6 * OWN_TILES, 128),), (left_list(5),), *fixed
            )
            break
        velocity, gx_first, gx_second = call(
            settle, (PULSE,) + GX_SENDS, (left_list(5),), *fixed
        )
        got = along_gx(fetch, gx_first, gx_second)
        near, gy_first, gy_second = call(
            gather_near, (shape(6 * ROWS, 128),) + FACES, (), kinds[fetch], velocity, places, list_places
        )
        got_gy = along_gy(*got, gy_first, gy_second)
        (far,) = call(
            gather_far, (shape(6 * ROWS, 128),), (), kinds[fetch], velocity, places, *got
        )
        impulse, near_values, far_values, gx_first, gx_second, gy_first, gy_second = call(
            sweep, (shape(IMPULSE_ROWS, 128), VALUES, VALUES) + GX_SENDS + FACES, (LEFT_GHOST,),
            kinds[follow], near, far, table, places, high_far, hot_far, impulse, *got_gy,
        )
    return velocity.reshape(1, 1, 6, BODY), impulse.reshape(1, 1, 3, CONTACTS)

def solution(mesh):
    in_specs = (
        P("gx", "gy", None, None),
        P("gx", "gy", None),
        P("gx", "gy", None, None),
        P("gx", "gy", None, None),
        P("gx", "gy", None),
        P("gx", "gy", None),
        P("gx", "gy", None, None),
        P("gx", "gy", None, None),
        P("gx", "gy", None),
        P("gx", "gy", None),
        P("gx", "gy", None, None),
    )
    out_specs = (P("gx", "gy", None, None), P("gx", "gy", None, None))
    return jax.shard_map(shards, mesh=mesh, in_specs=in_specs, out_specs=out_specs, check_vma=False)
```

```python
import jax
import jax.numpy as jnp
from jax import lax
from jax.experimental import pallas as pl
from jax.experimental.pallas import tpu as pltpu
from jax.sharding import PartitionSpec as P

SWEEPS = 4
SWAPS = (False, True, False, True, True, True, False, True, False, False)
RELAX = 0.25
SMALLEST = 1e-20

BODY = 2048
FACE = 256
CORNER = 32
CONTACTS = 4096
ROWS = CONTACTS // 128
LISTED = 4 * FACE + 4 * CORNER
LIST_ROWS = LISTED // 128
OWN_TILES = BODY // 128
WIDE = 256
OWN_WIDE = BODY // WIDE
GHOST_WIDE = 6
IMPULSE_ROWS = 3 * ROWS
MESSAGE = FACE + 128

F32 = jnp.float32
BF16 = jnp.bfloat16
I32 = jnp.int32

PLANES = (
    "n0", "n1", "n2", "a0", "a1", "b0", "b1", "b2",
    "arm0", "arm1", "relax", "mu", "bias",
)
PLANE = {name: place for place, name in enumerate(PLANES)}


def lanes_of(table, lane):
    numbers = lax.GatherDimensionNumbers(
        offset_dims=(),
        collapsed_slice_dims=(1,),
        start_index_map=(1,),
        operand_batching_dims=(0,),
        start_indices_batching_dims=(0,),
    )
    return lax.gather(
        table, lane[..., None], numbers, (1, 1),
        mode=lax.GatherScatterMode.PROMISE_IN_BOUNDS,
    )


def iota(shape, dim):
    return lax.broadcasted_iota(I32, shape, dim)


def halves(values):
    high = values.astype(BF16).astype(F32)
    return high, values - high


def plane(ref, number):
    return ref[number * ROWS:(number + 1) * ROWS, :]


def spread(ref, high_row, parts, blocks, column):
    picks = [high_row == block for block in blocks]
    for part, value in enumerate(parts):
        zero = jnp.zeros_like(value)
        for pair in range(len(blocks) // 2):
            both = jnp.concatenate(
                [
                    jnp.where(picks[2 * pair], value, zero),
                    jnp.where(picks[2 * pair + 1], value, zero),
                ],
                axis=0,
            )
            start = part * len(blocks) * 8 + pair * 16
            ref[start:start + 16, column:column + 128] = both.astype(BF16)


OWN_BLOCKS = tuple(range(OWN_WIDE))
GHOST_BLOCKS = tuple(range(OWN_WIDE, OWN_WIDE + GHOST_WIDE))


def lane_hot(ref, low, rows):
    turned = jnp.transpose(low)
    along = iota((128, WIDE), 1)
    for row in range(rows):
        hot = jnp.broadcast_to(turned[:, row:row + 1], (128, WIDE)) == along
        ref[row * 128:(row + 1) * 128, :] = jnp.where(hot, 1.0, 0.0).astype(BF16)


def product(left, hot, blocks):
    total = jnp.dot(left[...], hot, preferred_element_type=F32)
    return total[:blocks * 8] + total[blocks * 8:]


def end_pulses(impulse, table, near_out, far_out):
    p0, p1, p2 = impulse
    get = lambda name: plane(table, PLANE[name])
    a0, a1 = get("a0"), get("a1")
    b0, b1, b2 = get("b0"), get("b1"), get("b2")
    force = (
        p0 * get("n0") + p1 * a0 + p2 * b0,
        p0 * get("n1") + p1 * a1 + p2 * b1,
        p0 * get("n2") + p2 * b2,
    )
    twist = (p1 * b0 - p2 * a0, p1 * b1 - p2 * a1, p1 * b2)
    arm0, arm1 = -get("arm0"), -get("arm1")
    for comp in range(3):
        near_out[pl.ds(comp, ROWS, stride=8), :] = force[comp]
        far_out[pl.ds(comp, ROWS, stride=8), :] = -force[comp]
        near_out[pl.ds(comp + 3, ROWS, stride=8), :] = arm0 * twist[comp]
        far_out[pl.ds(comp + 3, ROWS, stride=8), :] = arm1 * twist[comp]
    for comp in (6, 7):
        near_out[pl.ds(comp, ROWS, stride=8), :] = jnp.zeros((ROWS, 128), F32)
        far_out[pl.ds(comp, ROWS, stride=8), :] = jnp.zeros((ROWS, 128), F32)


def spread_rows(left, values, high, blocks):
    for row in range(ROWS):
        value = values[row * 8:(row + 1) * 8, :]
        spread(left, high[row:row + 1, :], halves(value), blocks, row * 128)


def ghost_pulses(flags, far, high_far, hot_far, gx_sends, gy_faces, left_ghost):
    spread_rows(left_ghost, far, high_far, GHOST_BLOCKS)
    total = product(left_ghost, hot_far[...], GHOST_WIDE)
    ghost = [total[block * 8:block * 8 + 8] for block in range(5)]
    send_gx(flags, ghost[0], ghost[1], ghost[4][:, :128], gx_sends)
    send_gy(flags, ghost[2], ghost[3], gy_faces)


def flag(flags, number, width=128):
    return jnp.broadcast_to(flags[number:number + 1, :1] > 0, (8, width))


def send_gx(flags, face0, face1, corners, sends):
    first, second = sends
    slot = iota((8, 128), 1) // CORNER
    to_down = (slot == 0) | (slot == 2)
    up = jnp.where(to_down | ~flag(flags, 0), 0.0, corners)
    down = jnp.where(to_down & flag(flags, 1), corners, 0.0)
    ahead, wide = flag(flags, 5), flag(flags, 5, FACE)
    first[:, :FACE] = jnp.where(wide, face1, face0)
    first[:, FACE:] = jnp.where(ahead, down, up)
    second[:, :FACE] = jnp.where(wide, face0, face1)
    second[:, FACE:] = jnp.where(ahead, up, down)


def send_gy(flags, face2, face3, faces):
    wide = flag(flags, 6, FACE)
    faces[0][...] = jnp.where(wide, face3, face2)
    faces[1][...] = jnp.where(wide, face2, face3)


def prepare(
    flags, angles_in, arms_in, mu_in, bias_in, impulse_in, owner_in, other_in,
    radius_in, faces_in, corners_in, base_in,
    table, places, high_far, impulse, hot_far, near_values, far_values,
    gx_first, gx_second, gy_first, gy_second,
    owner, radius, faces, corners, base,
    angles, arms, mu, bias, other, flat, left_ghost, sems,
):
    copies = [
        pltpu.make_async_copy(source, target, sems.at[number])
        for number, (source, target) in enumerate((
            (other_in, other), (angles_in, angles), (arms_in, arms), (mu_in, mu),
            (bias_in, bias), (impulse_in, impulse), (owner_in, owner), (radius_in, radius),
            (faces_in, faces), (corners_in, corners), (base_in, base),
        ))
    ]
    for copy in copies:
        copy.start()
    copies[0].wait()
    far_id = other[...]
    extra = far_id - (BODY + 4 * FACE)
    block = extra >> 5
    slot = ((block & 1) << 1) | (block >> 1)
    in_block = extra & (CORNER - 1)
    is_corner = extra >= 0
    places[2 * ROWS:3 * ROWS, :] = far_id >> 7
    places[3 * ROWS:, :] = jnp.where(is_corner, slot * CORNER + in_block, far_id & 127)
    high_far[...] = far_id >> 8
    lane_hot(
        hot_far, jnp.where(is_corner, (3 - slot) * CORNER + in_block, far_id & 255), ROWS
    )
    for copy in copies[1:]:
        copy.wait()
    near_id = owner[...]
    places[:ROWS, :] = near_id >> 7
    places[ROWS:2 * ROWS, :] = near_id & 127
    for row in range(ROWS):
        cut = slice(row * 128, (row + 1) * 128)
        flat[pl.ds(row, 2, stride=ROWS), :] = angles[:, cut]
        flat[pl.ds(2 * ROWS + row, 2, stride=ROWS), :] = arms[:, cut]
    polar, azim = plane(flat, 0), plane(flat, 1)
    arm0, arm1 = plane(flat, 2), plane(flat, 3)
    cos_polar, sin_polar = jnp.cos(polar), jnp.sin(polar)
    cos_azim, sin_azim = jnp.cos(azim), jnp.sin(azim)
    cubed0 = arm0 * arm0 * arm0
    cubed1 = arm1 * arm1 * arm1
    values = {
        "n0": cos_polar * cos_azim, "n1": cos_polar * sin_azim, "n2": sin_polar,
        "a0": -sin_azim, "a1": cos_azim,
        "b0": -sin_polar * cos_azim, "b1": -sin_polar * sin_azim, "b2": cos_polar,
        "arm0": arm0, "arm1": arm1,
        "relax": RELAX / (1.0 / cubed0 + 1.0 / cubed1),
        "mu": mu[...], "bias": bias[...],
    }
    for name, value in values.items():
        number = PLANE[name]
        table[number * ROWS:(number + 1) * ROWS, :] = value
    end_pulses([plane(impulse, comp) for comp in range(3)], table, near_values, far_values)
    ghost_pulses(
        flags, far_values, high_far, hot_far, (gx_first, gx_second), (gy_first, gy_second), left_ghost
    )


def prepare_own(
    near_values, owner, radius, faces, corners, base_rows,
    pulse, high_near, hot_near, hot_list, list_places, inverse, base,
    left_near,
):
    near_id = owner[...]
    high_near[...] = near_id >> 8
    lane_hot(hot_near, near_id & 255, ROWS)
    for number in range(4):
        for part in range(2):
            row = number * 2 + part
            list_places[row:row + 1, :] = faces[number:number + 1, part * 128:(part + 1) * 128]
    for place, number in enumerate((0, 2, 1, 3)):
        list_places[8:9, place * CORNER:(place + 1) * CORNER] = corners[number:number + 1, :]
    for place, number in enumerate((3, 1, 2, 0)):
        list_places[9:10, place * CORNER:(place + 1) * CORNER] = corners[number:number + 1, :]
    list_places[10:, :] = jnp.zeros((6, 128), I32)
    lane_hot(hot_list, list_places[...] & 255, LIST_ROWS)

    size = radius[...]
    cubed = size * size * size
    linear = 1.0 / cubed
    angular = 2.5 / (cubed * size * size)
    inverse[...] = jnp.where(iota((8, BODY), 0) < 3, linear, angular)
    for tile in range(OWN_TILES):
        base[:, tile * 128:(tile + 1) * 128] = base_rows[pl.ds(tile, 6, stride=OWN_TILES), :]
    scatter_near(near_values, high_near, hot_near, pulse, left_near)


def store_blocks(pulse, total):
    for block in range(OWN_WIDE):
        pulse[:, block * WIDE:(block + 1) * WIDE] = total[block * 8:block * 8 + 8]


def scatter_near(values, high_near, hot_near, pulse, left_near):
    spread_rows(left_near, values, high_near, OWN_BLOCKS)
    store_blocks(pulse, product(left_near, hot_near[...], OWN_WIDE))


def masked(flags, number, value):
    return jnp.where(flags[number:number + 1, :] > 0, value, jnp.zeros_like(value))


def gx_tiles(flags, first, second):
    from_above = jnp.broadcast_to(flags[5:6, 127:] > 0, (8, 128))
    tiles = []
    for part in range(2):
        cut = slice(part * 128, (part + 1) * 128)
        one, two = first[:, cut], second[:, cut]
        tiles.append((jnp.where(from_above, one, two), jnp.where(from_above, two, one)))
    up, down = zip(*tiles)
    return [masked(flags, 0, tile) for tile in up] + [masked(flags, 1, tile) for tile in down]


def gy_tiles(flags, first, second):
    tiles = []
    for part in range(2):
        cut = slice(part * 128, (part + 1) * 128)
        one, two = first[:, cut], second[:, cut]
        tiles.append((jnp.where(flag(flags, 6), one, two), jnp.where(flag(flags, 6), two, one)))
    left, right = zip(*tiles)
    corners = jnp.where(flags[7:8, :] > 0, first[:, FACE:], second[:, FACE:])
    return (
        [masked(flags, 2, tile) for tile in left] + [masked(flags, 3, tile) for tile in right]
        + [masked(flags, 4, corners)]
    )


def list_product(left_list, tiles, list_places, hot, first):
    for row, tile in enumerate(tiles):
        high_row = list_places[first + row:first + row + 1, :] >> 8
        spread(left_list, high_row, halves(tile), OWN_BLOCKS, row * 128)
    rows = slice(first * 128, (first + len(tiles)) * 128)
    return product(left_list, hot[rows, :], OWN_WIDE)


def scatter_far(
    flags, values, high_far, hot_far, near_pulse, list_places, hot_list, from_up, from_down,
    pulse, left_far, left_list,
):
    spread_rows(left_far, values, high_far, OWN_BLOCKS)
    total = product(left_far, hot_far[...], OWN_WIDE)
    total = total + list_product(
        left_list, gx_tiles(flags, from_up, from_down), list_places, hot_list, 0
    )
    for block in range(OWN_WIDE):
        cut = slice(block * WIDE, (block + 1) * WIDE)
        pulse[:, cut] = near_pulse[:, cut] + total[block * 8:block * 8 + 8]


def settled(flags, own, inverse, base, list_places, hot_list, from_left, from_right, left_list):
    added = list_product(
        left_list, gy_tiles(flags, from_left, from_right), list_places, hot_list, 4
    )
    blocks = []
    for block in range(OWN_WIDE):
        cut = slice(block * WIDE, (block + 1) * WIDE)
        total = own[:6, cut] + added[block * 8:block * 8 + 6]
        blocks.append(base[:, cut] + inverse[:6, cut] * total)
    return blocks


def listed(velocity, list_places, row):
    entry = jnp.broadcast_to(list_places[row:row + 1, :], (8, 128))
    tile_id, lane = entry >> 7, entry & 127
    total = jnp.zeros((8, 128), F32)
    for tile in range(OWN_TILES):
        table = velocity[:, tile * 128:(tile + 1) * 128]
        total = jnp.where(tile_id == tile, lanes_of(table, lane), total)
    return total


def settle(
    flags, own, inverse, base, list_places, hot_list, from_left, from_right,
    velocity, gx_first, gx_second, left_list,
):
    blocks = settled(
        flags, own, inverse, base, list_places, hot_list, from_left, from_right, left_list
    )
    zero = jnp.zeros((2, WIDE), F32)
    for block, value in enumerate(blocks):
        velocity[:, block * WIDE:(block + 1) * WIDE] = jnp.concatenate([value, zero], axis=0)
    found = [listed(velocity, list_places, row) for row in (0, 1, 2, 3, 9)]
    face = [jnp.concatenate(found[2 * k:2 * k + 2], axis=1) for k in range(2)]
    send_gx(flags, *face, found[4], (gx_first, gx_second))


def settle_last(
    flags, own, inverse, base, list_places, hot_list, from_left, from_right,
    velocity, left_list,
):
    blocks = settled(
        flags, own, inverse, base, list_places, hot_list, from_left, from_right, left_list
    )
    for block, value in enumerate(blocks):
        for part in range(2):
            tile = 2 * block + part
            velocity[pl.ds(tile, 6, stride=OWN_TILES), :] = value[:, part * 128:(part + 1) * 128]


def pick(tables, tile_id, lane, firsts, totals):
    for tile, table in zip(firsts, tables):
        here = tile_id == tile
        for comp in range(6):
            row = jnp.broadcast_to(table[comp:comp + 1, :], (ROWS, 128))
            totals[comp] = jnp.where(here, lanes_of(row, lane), totals[comp])
    return totals


def own_tables(velocity):
    return [velocity[:, tile * 128:(tile + 1) * 128] for tile in range(OWN_TILES)]


def blank():
    return [jnp.zeros((ROWS, 128), F32) for _ in range(6)]


def gather_near(flags, velocity, places, list_places, near, gy_first, gy_second):
    tiles = [listed(velocity, list_places, row) for row in range(4, 8)]
    send_gy(
        flags, jnp.concatenate(tiles[:2], axis=1), jnp.concatenate(tiles[2:], axis=1),
        (gy_first, gy_second),
    )
    found = pick(
        own_tables(velocity), places[:ROWS, :], places[ROWS:2 * ROWS, :], range(OWN_TILES), blank()
    )
    for comp in range(6):
        near[comp * ROWS:(comp + 1) * ROWS, :] = found[comp]


def gather_far(flags, velocity, places, from_up, from_down, far):
    found = pick(
        own_tables(velocity) + gx_tiles(flags, from_up, from_down),
        places[2 * ROWS:3 * ROWS, :], places[3 * ROWS:, :], range(OWN_TILES + 4), blank(),
    )
    for comp in range(6):
        far[comp * ROWS:(comp + 1) * ROWS, :] = found[comp]


def sweep(
    flags, near_ref, far_ref, table, places, high_far, hot_far, impulse, from_left, from_right,
    impulse_out, near_values, far_values, gx_first, gx_second, gy_first, gy_second, left_ghost,
):
    near = [plane(near_ref, comp) for comp in range(6)]
    far = pick(
        gy_tiles(flags, from_left, from_right),
        places[2 * ROWS:3 * ROWS, :], places[3 * ROWS:, :],
        range(OWN_TILES + 4, OWN_TILES + 9), [plane(far_ref, comp) for comp in range(6)],
    )
    get = lambda name: plane(table, PLANE[name])
    n0, n1, n2 = get("n0"), get("n1"), get("n2")
    a0, a1 = get("a0"), get("a1")
    b0, b1, b2 = get("b0"), get("b1"), get("b2")
    arm0, arm1, relax, mu = get("arm0"), get("arm1"), get("relax"), get("mu")
    w0, w1, w2 = [near[c] - far[c] for c in range(3)]
    s0, s1, s2 = [arm0 * near[c] + arm1 * far[c] for c in range(3, 6)]
    rate_n = n0 * w0 + n1 * w1 + n2 * w2
    rate_a = (a0 * w0 + a1 * w1) - (b0 * s0 + b1 * s1 + b2 * s2)
    rate_b = (b0 * w0 + b1 * w1 + b2 * w2) + (a0 * s0 + a1 * s1)
    trial_n = plane(impulse, 0) - relax * (rate_n + get("bias"))
    trial_a = plane(impulse, 1) - relax * rate_a
    trial_b = plane(impulse, 2) - relax * rate_b
    length = jnp.sqrt(trial_a * trial_a + trial_b * trial_b)
    inside = length <= mu * trial_n
    dead = mu * length <= -trial_n
    level = (trial_n + mu * length) / (1.0 + mu * mu)
    factor = mu * level / jnp.maximum(length, SMALLEST)
    choose = lambda kept, cone: jnp.where(inside, kept, jnp.where(dead, 0.0, cone))
    fresh = [
        choose(trial_n, level), choose(trial_a, factor * trial_a), choose(trial_b, factor * trial_b)
    ]
    for comp in range(3):
        impulse_out[comp * ROWS:(comp + 1) * ROWS, :] = fresh[comp]
    end_pulses(fresh, table, near_values, far_values)
    ghost_pulses(
        flags, far_values, high_far, hot_far, (gx_first, gx_second), (gy_first, gy_second), left_ghost
    )


def shape(*dims, kind=F32):
    return jax.ShapeDtypeStruct(dims, kind)


FACES = (shape(8, FACE), shape(8, FACE))
GX_SENDS = (shape(8, MESSAGE), shape(8, MESSAGE))
VALUES = shape(8 * ROWS, 128)
PULSE = shape(8, BODY)
LEFT_OWN = pltpu.VMEM((2 * OWN_WIDE * 8, CONTACTS), BF16)
LEFT_GHOST = pltpu.VMEM((2 * GHOST_WIDE * 8, CONTACTS), BF16)


def left_list(tiles):
    return pltpu.VMEM((2 * OWN_WIDE * 8, tiles * 128), BF16)


def call(body, outs, scratch, *operands, specs=None):
    vmem = pl.BlockSpec(memory_space=pltpu.VMEM)
    return pl.pallas_call(
        body,
        out_shape=outs,
        in_specs=specs or [vmem] * len(operands),
        out_specs=[vmem] * len(outs),
        scratch_shapes=scratch,
        compiler_params=pltpu.CompilerParams(vmem_limit_bytes=10 * 1024 * 1024),
    )(*operands)


def loop(value, back, lines, place):
    count, length = lines
    pairs = []
    for line in range(0, count, 2):
        ring = [place(line, step) for step in range(length)]
        ring += [place(line + 1, step) for step in reversed(range(length))]
        for here, there in zip(ring, ring[1:] + ring[:1]):
            pairs.append((there, here) if back else (here, there))
    return lax.ppermute(value, ("gx", "gy"), pairs)


def along_gx(swap, first, second):
    rows, columns = lax.axis_size("gx"), lax.axis_size("gy")
    if not swap:
        down = [(i, (i + 1) % rows) for i in range(rows)]
        up = [(j, i) for i, j in down]
        return lax.ppermute(first, "gx", down), lax.ppermute(second, "gx", up)
    outer, inner = [], []
    for row in range(rows):
        for column in range(columns):
            here = row * columns + column
            near = row ^ 1
            far = row - 1 if row % 2 == 0 else row + 1
            inner.append((here, near * columns + column))
            if 0 <= far < rows:
                outer.append((here, far * columns + column))
            else:
                outer.append((here, row * columns + (column ^ 1)))
    axes = ("gx", "gy")
    return lax.ppermute(first, axes, outer), lax.ppermute(second, axes, inner)


def along_gy(got_first, got_second, face_first, face_second):
    rows, columns = lax.axis_size("gx"), lax.axis_size("gy")
    corners = got_first[:, FACE:] + got_second[:, FACE:]
    first = jnp.concatenate([face_first, corners], axis=1)
    second = jnp.concatenate([face_second, corners], axis=1)
    place = lambda line, step: line * columns + step
    lines = (rows, columns)
    return loop(first, False, lines, place), loop(second, True, lines, place)


def presence(swap):
    row_at, row_count = lax.axis_index("gx"), lax.axis_size("gx")
    col_at, col_count = lax.axis_index("gy"), lax.axis_size("gy")
    row, slot = iota((8, 128), 0), iota((8, 128), 1) // CORNER
    above = (row == 0) | ((row == 4) & ((slot == 0) | (slot == 2)))
    below = (row == 1) | ((row == 4) & ((slot == 1) | (slot == 3)))
    before = (row == 2) | ((row == 4) & (slot < 2))
    after = (row == 3) | ((row == 4) & (slot >= 2))
    odd_row = lax.rem(row_at, 2)
    off = (
        (above & (row_at == 0)) | (below & (row_at == row_count - 1))
        | (before & (col_at == 0)) | (after & (col_at == col_count - 1))
        | ((row == 6) & (odd_row == 1))
        | ((row == 5) & (swap & ((slot >> 1) == odd_row)))
        | ((row == 7) & ((slot >> 1) != odd_row))
    )
    return jnp.where(off, 0.0, 1.0)


def shards(
    free_velocity, body_radius, face_lists, corner_lists, owner_body, other_body,
    contact_angles, contact_arms, friction, approach, start_impulse,
):
    kinds = [presence(swap) for swap in (False, True)]
    in_rows = lambda value: value[0, 0].reshape(-1, 128)
    dma = pltpu.SemaphoreType.DMA
    raw = [
        pltpu.with_memory_space_constraint(value, pltpu.HBM)
        for value in (
            contact_angles[0, 0], contact_arms[0, 0], in_rows(friction), in_rows(approach),
            in_rows(start_impulse), in_rows(owner_body), in_rows(other_body),
            body_radius[0], face_lists[0, 0], corner_lists[0, 0], in_rows(free_velocity),
        )
    ]
    (
        table, places, high_far, impulse, hot_far, near_values, far_values,
        gx_first, gx_second, gy_first, gy_second, owner, radius, faces, corners, base_rows,
    ) = call(
        prepare,
        (
            shape(len(PLANES) * ROWS, 128),
            shape(4 * ROWS, 128, kind=I32),
            shape(ROWS, 128, kind=I32),
            shape(IMPULSE_ROWS, 128),
            shape(CONTACTS, WIDE, kind=BF16),
            VALUES, VALUES,
        ) + GX_SENDS + FACES + (
            shape(ROWS, 128, kind=I32),
            shape(1, BODY),
            shape(4, FACE, kind=I32),
            shape(4, CORNER, kind=I32),
            shape(6 * OWN_TILES, 128),
        ),
        (
            pltpu.VMEM((2, CONTACTS), F32),
            pltpu.VMEM((2, CONTACTS), F32),
            pltpu.VMEM((ROWS, 128), F32),
            pltpu.VMEM((ROWS, 128), F32),
            pltpu.VMEM((ROWS, 128), I32),
            pltpu.VMEM((4 * ROWS, 128), F32),
            LEFT_GHOST,
            dma((11,)),
        ),
        kinds[SWAPS[0]], *raw,
        specs=[pl.BlockSpec(memory_space=pltpu.VMEM)]
        + [pl.BlockSpec(memory_space=pltpu.HBM)] * len(raw),
    )
    for number in range(SWEEPS + 1):
        back, fetch = SWAPS[2 * number:2 * number + 2]
        follow = SWAPS[2 * number + 2] if number < SWEEPS else False
        got = along_gx(back, gx_first, gx_second)
        if number == 0:
            pulse, high_near, hot_near, hot_list, list_places, inverse, base = call(
                prepare_own,
                (
                    PULSE,
                    shape(ROWS, 128, kind=I32),
                    shape(CONTACTS, WIDE, kind=BF16),
                    shape(LISTED, WIDE, kind=BF16),
                    shape(16, 128, kind=I32),
                    PULSE,
                    shape(6, BODY),
                ),
                (LEFT_OWN,),
                near_values, owner, radius, faces, corners, base_rows,
            )
        else:
            (pulse,) = call(
                scatter_near, (PULSE,), (LEFT_OWN,), near_values, high_near, hot_near
            )
        got_gy = along_gy(*got, gy_first, gy_second)
        (own,) = call(
            scatter_far, (PULSE,), (LEFT_OWN, left_list(4)),
            kinds[back], far_values, high_far, hot_far, pulse, list_places, hot_list, *got,
        )
        fixed = (kinds[fetch], own, inverse, base, list_places, hot_list, *got_gy)
        if number == SWEEPS:
            (velocity,) = call(
                settle_last, (shape(6 * OWN_TILES, 128),), (left_list(5),), *fixed
            )
            break
        velocity, gx_first, gx_second = call(
            settle, (PULSE,) + GX_SENDS, (left_list(5),), *fixed
        )
        got = along_gx(fetch, gx_first, gx_second)
        near, gy_first, gy_second = call(
            gather_near, (shape(6 * ROWS, 128),) + FACES, (), kinds[fetch], velocity, places, list_places
        )
        got_gy = along_gy(*got, gy_first, gy_second)
        (far,) = call(
            gather_far, (shape(6 * ROWS, 128),), (), kinds[fetch], velocity, places, *got
        )
        impulse, near_values, far_values, gx_first, gx_second, gy_first, gy_second = call(
            sweep, (shape(IMPULSE_ROWS, 128), VALUES, VALUES) + GX_SENDS + FACES, (LEFT_GHOST,),
            kinds[follow], near, far, table, places, high_far, hot_far, impulse, *got_gy,
        )
    return velocity.reshape(1, 1, 6, BODY), impulse.reshape(1, 1, 3, CONTACTS)

def solution(mesh):
    in_specs = (
        P("gx", "gy", None, None),
        P("gx", "gy", None),
        P("gx", "gy", None, None),
        P("gx", "gy", None, None),
        P("gx", "gy", None),
        P("gx", "gy", None),
        P("gx", "gy", None, None),
        P("gx", "gy", None, None),
        P("gx", "gy", None),
        P("gx", "gy", None),
        P("gx", "gy", None, None),
    )
    out_specs = (P("gx", "gy", None, None), P("gx", "gy", None, None))
    return jax.shard_map(shards, mesh=mesh, in_specs=in_specs, out_specs=out_specs, check_vma=False)
```
